32 devices in a mesh: site: 4 (over z), patch: 8 (over y, x, core).
Axes of the slice: x: 2, y: 2, z: 4, core: 2. Of those that a mesh axis runs over, the one named last changes fastest.
Arguments:
- slip_rates: bfloat16 [128, 64, 256], P('patch', 'site'), may hold values from -6 to 6
- green_tiles: bfloat16 [4, 256, 2, 1024], P('site', 'patch'), may hold values from -0.03125 to 0.03125
- patch_slot: int32 [128], replicated, may hold values from 0 to 255, as said below
Outputs:
- seismograms: float32 [4, 64, 2, 1280], P('site', 'patch')
The draws below stay inside these ranges and needn't reach their ends.
Inputs may be any that keep to these rules, and one draw needn't show every extreme that they name: The values of patch_slot all differ. Patch p belongs to owner patch_slot[p] // 32 and fills its slot patch_slot[p] % 32; each owner has 1 to 32 patches in its first slots, and some owner has exactly 32. The 16 patches p with the same p // 16 include at most 4 of any one owner, and some such group includes exactly 4 of one owner.
All inputs are finite; a program needn't handle non-finite values.
Results may differ from the reference program's by a relative error of at most 0.0003.
Values may be sent and summed in bfloat16 or wider, within the bound.
No kernel may reach another device: no remote copies, remote signals or barrier semaphores. Data moves between devices by JAX's collectives and lax.ppermute only.
A program may use at most 64 MiB of HBM per device.

```python
import jax
import jax.numpy as jnp
from jax import lax

V = 64
SAMPLES = 256
LAGS = 1024
PATCH_DEV = 16
PATCHES = 128
SLOTS = 256
SITES = 4
OUT = 1280


def draw_patch_slot(key, part):
    sources = PATCHES // PATCH_DEV
    per_source = PATCH_DEV
    half_len = per_source // 2
    slot_width = 2 * per_source
    key_offs, key_heavy, key_perm = jax.random.split(jax.random.fold_in(key, 17), 3)
    offsets = jax.random.randint(key_offs, (sources + 1,), 1 - half_len, half_len)
    heavy_run = jax.random.randint(key_heavy, (), 1, sources - 1)
    mark_index = jnp.arange(sources + 1)
    offsets = jnp.where(mark_index == heavy_run, -half_len, offsets)
    offsets = jnp.where(mark_index == heavy_run + 1, half_len, offsets)
    offsets = jnp.where((mark_index == 0) | (mark_index == sources), 0, offsets)
    cut_points = mark_index * per_source + offsets
    labels = jax.random.permutation(key_perm, sources)
    places = jnp.arange(PATCHES)
    run_of = jnp.sum((places[:, None] >= cut_points[None, 1:sources]).astype(jnp.int32), axis=1)
    slot_at = labels[run_of] * slot_width + places - cut_points[run_of]
    patches = jnp.arange(PATCHES)
    source_of = patches // per_source
    local_of = patches % per_source
    place_of = local_of // 2 * (2 * sources) + 2 * source_of + local_of % 2
    return slot_at[place_of].astype(jnp.int32)


def shard_levels(key, extent, cuts, least, largest):
    def one(position, shards_of):
        draws = jax.random.uniform(jax.random.fold_in(jax.random.fold_in(key, 6), position), (shards_of,), jnp.float32, least / len(cuts), largest / len(cuts))
        return jnp.repeat(jnp.exp(draws), extent[position] // shards_of).reshape((-1,) + (1,) * (len(extent) - position - 1))

    gain = one(*cuts[0])
    for cut in cuts[1:]:
        gain = gain * one(*cut)
    return gain


def noise(rng, shape, spread, reach, cuts=(), held_as=jnp.bfloat16):
    result = spread * jax.random.normal(rng, shape, jnp.float32)
    if cuts:
        result = result * shard_levels(rng, shape, cuts, -0.22, 0.18)
    return jnp.clip(result, -reach, reach).astype(held_as)


def setup_inputs(seed: int = 0) -> dict:
    keys = jax.random.split(jax.random.key(seed), 4)
    return {
        "slip_rates": noise(keys[0], (PATCHES, V, SAMPLES), 1.0, 6.0, ((0, 8), (1, 4))),
        "green_tiles": noise(keys[1], (SITES, SLOTS, 2, LAGS), (PATCHES * SAMPLES) ** -0.5, 0.03125, ((0, 4), (1, 8))),
        "patch_slot": draw_patch_slot(jax.random.fold_in(keys[3], 71), 0),
    }


def reference(slip_rates, green_tiles, patch_slot):
    fft_length = SAMPLES + OUT
    slip_freq = jnp.fft.rfft(slip_rates.astype(jnp.float32), n=fft_length, axis=-1)

    def one_site(site_tiles):
        patch_tiles = jnp.take(site_tiles, patch_slot, axis=0).astype(jnp.float32)
        tile_freq = jnp.fft.rfft(patch_tiles, n=fft_length, axis=-1)
        product = jnp.einsum('pvf,pcf->vcf', slip_freq, tile_freq)
        return jnp.fft.irfft(product, n=fft_length, axis=-1)[..., :OUT]

    return lax.map(one_site, green_tiles)
```

```python
import functools

import jax
import jax.numpy as jnp
from jax import lax
from jax.experimental import pallas as pl
from jax.experimental.pallas import tpu as pltpu
from jax.sharding import PartitionSpec as P

BLOCK = 16
LANES = 128
ROWS = 8
VMEM_LIMIT = 32 * 1024 * 1024


def round_up(value, unit):
    return -(-value // unit) * unit


def params():
    return pltpu.CompilerParams(vmem_limit_bytes=VMEM_LIMIT)


def split_kernel(slip_ref, keep_ref, give_ref):
    patches, both, samples = slip_ref.shape
    rows = both // 2
    per_reg = LANES // BLOCK
    blocks = samples // BLOCK
    core = lax.rem(lax.axis_index("patch"), 2)
    lane_block = lax.broadcasted_iota(jnp.int32, (rows, LANES), 1) // BLOCK
    out_regs = patches * BLOCK // LANES
    for group in range(out_regs):
        done = {}
        for place in range(per_reg):
            full = slip_ref[group * per_reg + place].astype(jnp.float32)
            low, high = full[:rows], full[rows:]
            for which, source in enumerate(
                (jnp.where(core == 0, low, high), jnp.where(core == 0, high, low))
            ):
                for reg in range(samples // LANES):
                    piece = source[:, reg * LANES : (reg + 1) * LANES]
                    for inner in range(per_reg):
                        turn = (place - inner) % per_reg * BLOCK
                        moved = pltpu.roll(piece, turn, 1) if turn else piece
                        key = (which, reg * per_reg + inner)
                        if key in done:
                            done[key] = jnp.where(lane_block == place, moved, done[key])
                        else:
                            done[key] = moved
        for which, ref in enumerate((keep_ref, give_ref)):
            for block in range(0, blocks, 2):
                pair = jnp.concatenate([done[which, block], done[which, block + 1]], axis=0)
                ref[
                    block * rows : (block + 2) * rows, group * LANES : (group + 1) * LANES
                ] = pair.astype(jnp.bfloat16)


def split_slips(slips):
    patches, both, samples = slips.shape
    shape = jax.ShapeDtypeStruct((samples // BLOCK * both // 2, patches * BLOCK), jnp.bfloat16)
    return pl.pallas_call(
        split_kernel, out_shape=(shape, shape), compiler_params=params(), name="split_slips"
    )(slips)


def pick_kernel(slots_ref, *refs):
    pieces, out_ref = refs[:-1], refs[-1]
    own = lax.axis_index("patch")
    width = pieces[0].shape[0]
    count = out_ref.shape[0]
    total = jnp.zeros(out_ref.shape, jnp.float32)
    for step, piece in enumerate(pieces):
        owner = own ^ (2 * step)
        slot = lax.broadcasted_iota(jnp.int32, (count, width), 1) + owner * width
        pick = (slots_ref[...] == slot).astype(jnp.float32).astype(jnp.bfloat16)
        total = total + jnp.dot(pick, piece[...], preferred_element_type=jnp.float32)
    out_ref[...] = total.astype(jnp.bfloat16)


def pick_tiles(slots, pieces):
    shape = jax.ShapeDtypeStruct((slots.shape[0], pieces[0].shape[1]), jnp.bfloat16)
    return pl.pallas_call(
        pick_kernel, out_shape=shape, compiler_params=params(), name="pick_tiles"
    )(slots, *pieces)


def shift_kernel(lags, left_ref, right_ref, out_ref):
    tiles = left_ref[...].astype(jnp.float32) + right_ref[...].astype(jnp.float32)
    count = tiles.shape[0]
    components = tiles.shape[1] // lags
    width = out_ref.shape[1] // components
    tail = jnp.zeros((BLOCK, width - lags), jnp.float32)
    for patch in range(count):
        for comp in range(components):
            row = tiles[patch : patch + 1, comp * lags : (comp + 1) * lags]
            wide = jnp.concatenate([jnp.broadcast_to(row, (BLOCK, lags)), tail], axis=1)
            moved = pltpu.roll(wide, 0, 1, stride=1, stride_axis=0)
            out_ref[
                patch * BLOCK : (patch + 1) * BLOCK, comp * width : (comp + 1) * width
            ] = moved.astype(jnp.bfloat16)


def shift_tiles(left, right, lags):
    components = left.shape[1] // lags
    width = round_up(lags + BLOCK, LANES)
    shape = jax.ShapeDtypeStruct((left.shape[0] * BLOCK, components * width), jnp.bfloat16)
    return pl.pallas_call(
        functools.partial(shift_kernel, lags),
        out_shape=shape,
        compiler_params=params(),
        name="shift_tiles",
    )(left, right)


def convolve_kernel(sites, rows, length, shifted_ref, *refs):
    slip_refs, out_refs = refs[: 2 * sites], refs[2 * sites : 3 * sites]
    stack_ref, product_ref = refs[3 * sites :]
    components = out_refs[0].shape[1]
    height, depth = slip_refs[0].shape
    width = shifted_ref.shape[1] // components
    per_reg = LANES // BLOCK
    blocks = height // rows
    turn = lax.axis_index("site") ^ (lax.axis_index("patch") // 2)
    for step in range(sites):
        place = step ^ turn
        stack_ref[place, :, :depth] = slip_refs[2 * step][...]
        stack_ref[place, :, depth:] = slip_refs[2 * step + 1][...]
    for comp in range(components):
        product_ref[...] = jnp.dot(
            stack_ref[...].reshape(sites * height, 2 * depth),
            shifted_ref[:, comp * width : (comp + 1) * width],
            preferred_element_type=jnp.float32,
        )
        for step in range(sites):
            total = None
            for inner in range(per_reg):
                part = None
                for outer in range(inner, blocks, per_reg):
                    lead = outer // per_reg * LANES
                    start = step * height + outer * rows
                    block = product_ref[start : start + rows, :]
                    pieces = [jnp.zeros((rows, lead), jnp.float32)] if lead else []
                    pieces.append(block[:, : min(width, length - lead)])
                    if length > lead + width:
                        pieces.append(jnp.zeros((rows, length - lead - width), jnp.float32))
                    block = jnp.concatenate(pieces, axis=1) if len(pieces) > 1 else pieces[0]
                    part = block if part is None else part + block
                if inner:
                    part = pltpu.roll(part, inner * BLOCK, 1)
                total = part if total is None else total + part
            out_refs[step][:, comp, :] = total


def convolve(shifted, slips, sites, rows, components, length):
    height, depth = slips[0].shape
    width = shifted.shape[1] // components
    shape = jax.ShapeDtypeStruct((rows, components, length), jnp.float32)
    return pl.pallas_call(
        functools.partial(convolve_kernel, sites, rows, length),
        out_shape=(shape,) * sites,
        scratch_shapes=[
            pltpu.VMEM((sites, height, 2 * depth), jnp.bfloat16),
            pltpu.VMEM((sites * height, width), jnp.float32),
        ],
        compiler_params=params(),
        name="convolve",
    )(shifted, *slips)


def local(slip_rates, green_tiles, patch_slot):
    devices = lax.axis_size("patch")
    sites = lax.axis_size("site")
    chips = devices // 2
    patches, held, samples = slip_rates.shape
    slot_width, components, lags = green_tiles.shape[1:]
    length = samples + lags
    part = held // 2
    rows = round_up(part, ROWS)
    assert chips == sites

    def over_patch(value, offset):
        return lax.ppermute(value, "patch", [(i, i ^ offset) for i in range(devices)])

    def over_site(value, offset):
        return lax.ppermute(value, "site", [(i, i ^ offset) for i in range(sites)])

    slips = slip_rates.reshape(patches, 2, part, samples)
    slips = jnp.pad(slips, ((0, 0), (0, 0), (0, rows - part), (0, 0)))
    keep, give = split_slips(slips.reshape(patches, 2 * rows, samples))
    other = over_patch(give, 1)
    gathered = [keep, other]
    for step in range(1, sites):
        gathered += [over_site(keep, step), over_site(other, step)]

    resident = green_tiles[0].reshape(slot_width, components * lags)
    pieces = [resident] + [over_patch(resident, 2 * step) for step in range(1, chips)]
    own = lax.axis_index("patch")
    by_device = patch_slot.reshape(devices, patches)
    mine = lax.dynamic_index_in_dim(by_device, own, 0, keepdims=False)
    theirs = lax.dynamic_index_in_dim(by_device, own ^ 1, 0, keepdims=False)
    mine, theirs = mine.reshape(-1, 1), theirs.reshape(-1, 1)
    picked = pick_tiles(jnp.concatenate([mine, theirs], axis=0), pieces)
    swapped = jnp.concatenate([picked[patches:], picked[:patches]], axis=0)
    shifted = shift_tiles(picked, over_patch(swapped, 1), lags)

    sums = convolve(shifted, gathered, sites, rows, components, length)
    result = sums[0]
    for step in range(1, chips):
        result = result + over_patch(sums[step], 2 * step)
    return result[None, :part]


def solution(mesh):
    in_specs = (P("patch", "site", None), P("site", "patch", None, None), P())
    out_specs = P("site", "patch", None, None)
    return jax.shard_map(local, mesh=mesh, in_specs=in_specs, out_specs=out_specs, check_vma=False)
```

```python
import functools

import jax
import jax.numpy as jnp
from jax import lax
from jax.experimental import pallas as pl
from jax.experimental.pallas import tpu as pltpu
from jax.sharding import PartitionSpec as P

BLOCK = 16
LANES = 128
ROWS = 8
VMEM_LIMIT = 32 * 1024 * 1024


def round_up(value, unit):
    return -(-value // unit) * unit


def params():
    return pltpu.CompilerParams(vmem_limit_bytes=VMEM_LIMIT)


def arrange_kernel(own_ref, other_ref, out_ref):
    patches, both, samples = own_ref.shape
    rows = both // 2
    per_reg = LANES // BLOCK
    blocks = samples // BLOCK
    depth = patches * BLOCK
    core = lax.rem(lax.axis_index("patch"), 2)
    lane_block = lax.broadcasted_iota(jnp.int32, (rows, LANES), 1) // BLOCK
    for which, ref in enumerate((own_ref, other_ref)):
        base = (core if which == 0 else 1 - core) * depth
        for group in range(depth // LANES):
            done = {}
            for place in range(per_reg):
                full = ref[group * per_reg + place].astype(jnp.float32)
                source = jnp.where(core == 0, full[:rows], full[rows:])
                for reg in range(samples // LANES):
                    piece = source[:, reg * LANES : (reg + 1) * LANES]
                    for inner in range(per_reg):
                        turn = (place - inner) % per_reg * BLOCK
                        moved = pltpu.roll(piece, turn, 1) if turn else piece
                        block = reg * per_reg + inner
                        if block in done:
                            moved = jnp.where(lane_block == place, moved, done[block])
                        done[block] = moved
            lanes = pl.ds(pl.multiple_of(base + group * LANES, LANES), LANES)
            for block in range(0, blocks, 2):
                pair = jnp.concatenate([done[block], done[block + 1]], axis=0)
                out_ref[block * rows : (block + 2) * rows, lanes] = pair.astype(jnp.bfloat16)


def arrange_slips(own, other):
    patches, both, samples = own.shape
    shape = jax.ShapeDtypeStruct(
        (samples // BLOCK * both // 2, 2 * patches * BLOCK), jnp.bfloat16
    )
    return pl.pallas_call(
        arrange_kernel, out_shape=shape, compiler_params=params(), name="arrange_slips"
    )(own, other)


def line_transfers(sites):
    last = sites - 1
    steps = [
        (-1, [(i, i ^ 1) for i in range(sites)]),
        (-1, [(i, i + 1) for i in range(1, last, 2)] + [(i + 1, i) for i in range(1, last, 2)]),
    ]
    feeds = {1: [1]}
    for gap in range(2, last):
        up = [(i, i + gap) for i in range(last - gap)]
        down = [(last - i, last - j) for i, j in up]
        if {i for i, _ in up} & {i for i, _ in down} or {j for _, j in up} & {j for _, j in down}:
            feeds[gap] = [len(steps), len(steps) + 1]
            steps += [(-1, up), (-1, down)]
        else:
            feeds[gap] = [len(steps)]
            steps.append((-1, up + down))
    for gap in range(2, sites):
        ends = [(last - 1, last), (1, 0)]
        sources = feeds[gap - 1]
        for which, source in enumerate(sources):
            steps.append((source, ends if len(sources) == 1 else [ends[which]]))
    holds = []
    for operand, pairs in steps:
        held = [-1] * sites
        for i, j in pairs:
            held[j] = i if operand < 0 else holds[operand][i]
        holds.append(held)
    return steps, holds


def pick_kernel(slots_ref, *refs):
    pieces, out_ref = refs[:-1], refs[-1]
    own = lax.axis_index("patch")
    width = pieces[0].shape[0]
    count = out_ref.shape[0]
    total = jnp.zeros(out_ref.shape, jnp.float32)
    for step, piece in enumerate(pieces):
        owner = own ^ (2 * step)
        slot = lax.broadcasted_iota(jnp.int32, (count, width), 1) + owner * width
        pick = (slots_ref[...] == slot).astype(jnp.float32).astype(jnp.bfloat16)
        total = total + jnp.dot(pick, piece[...], preferred_element_type=jnp.float32)
    out_ref[...] = total.astype(jnp.bfloat16)


def pick_tiles(slots, pieces):
    shape = jax.ShapeDtypeStruct((slots.shape[0], pieces[0].shape[1]), jnp.bfloat16)
    return pl.pallas_call(
        pick_kernel, out_shape=shape, compiler_params=params(), name="pick_tiles"
    )(slots, *pieces)


def shift_kernel(lags, left_ref, right_ref, out_ref):
    tiles = left_ref[...].astype(jnp.float32) + right_ref[...].astype(jnp.float32)
    count = tiles.shape[0]
    components = tiles.shape[1] // lags
    width = out_ref.shape[1] // components
    tail = jnp.zeros((BLOCK, width - lags), jnp.float32)
    for patch in range(count):
        for comp in range(components):
            row = tiles[patch : patch + 1, comp * lags : (comp + 1) * lags]
            wide = jnp.concatenate([jnp.broadcast_to(row, (BLOCK, lags)), tail], axis=1)
            moved = pltpu.roll(wide, 0, 1, stride=1, stride_axis=0)
            out_ref[
                patch * BLOCK : (patch + 1) * BLOCK, comp * width : (comp + 1) * width
            ] = moved.astype(jnp.bfloat16)


def shift_tiles(left, right, lags):
    components = left.shape[1] // lags
    width = round_up(lags + BLOCK, LANES)
    shape = jax.ShapeDtypeStruct((left.shape[0] * BLOCK, components * width), jnp.bfloat16)
    return pl.pallas_call(
        functools.partial(shift_kernel, lags),
        out_shape=shape,
        compiler_params=params(),
        name="shift_tiles",
    )(left, right)


def convolve_kernel(sites, rows, length, holds, shifted_ref, *refs):
    slip_refs, out_refs = refs[: 1 + len(holds)], refs[1 + len(holds) : -2]
    stack_ref, product_ref = refs[-2:]
    components = out_refs[0].shape[1]
    height = slip_refs[0].shape[0]
    width = shifted_ref.shape[1] // components
    per_reg = LANES // BLOCK
    blocks = height // rows
    site = lax.axis_index("site")
    chip = lax.axis_index("patch") // 2
    stack_ref[site ^ chip] = slip_refs[0][...]
    for ref, held in zip(slip_refs[1:], holds):
        source = jnp.int32(-1)
        for index, value in enumerate(held):
            source = jnp.where(site == index, value, source)

        @pl.when(source >= 0)
        def _():
            stack_ref[source ^ chip] = ref[...]

    for comp in range(components):
        product_ref[...] = jnp.dot(
            stack_ref[...].reshape(sites * height, stack_ref.shape[2]),
            shifted_ref[:, comp * width : (comp + 1) * width],
            preferred_element_type=jnp.float32,
        )
        for step in range(sites):
            total = None
            for inner in range(per_reg):
                part = None
                for outer in range(inner, blocks, per_reg):
                    lead = outer // per_reg * LANES
                    start = step * height + outer * rows
                    block = product_ref[start : start + rows, :]
                    pieces = [jnp.zeros((rows, lead), jnp.float32)] if lead else []
                    pieces.append(block[:, : min(width, length - lead)])
                    if length > lead + width:
                        pieces.append(jnp.zeros((rows, length - lead - width), jnp.float32))
                    block = jnp.concatenate(pieces, axis=1) if len(pieces) > 1 else pieces[0]
                    part = block if part is None else part + block
                if inner:
                    part = pltpu.roll(part, inner * BLOCK, 1)
                total = part if total is None else total + part
            out_refs[step][:, comp, :] = total


def convolve(shifted, slips, holds, rows, components, length):
    sites = len(holds[0])
    height, depth = slips[0].shape
    width = shifted.shape[1] // components
    shape = jax.ShapeDtypeStruct((rows, components, length), jnp.float32)
    return pl.pallas_call(
        functools.partial(convolve_kernel, sites, rows, length, holds),
        out_shape=(shape,) * sites,
        scratch_shapes=[
            pltpu.VMEM((sites, height, depth), jnp.bfloat16),
            pltpu.VMEM((sites * height, width), jnp.float32),
        ],
        compiler_params=params(),
        name="convolve",
    )(shifted, *slips)


def local(slip_rates, green_tiles, patch_slot):
    devices = lax.axis_size("patch")
    sites = lax.axis_size("site")
    chips = devices // 2
    patches, held, samples = slip_rates.shape
    slot_width, components, lags = green_tiles.shape[1:]
    length = samples + lags
    part = held // 2
    rows = round_up(part, ROWS)
    assert chips == sites

    def over_patch(value, offset):
        return lax.ppermute(value, "patch", [(i, i ^ offset) for i in range(devices)])

    slips = slip_rates
    if rows > part:
        slips = slips.reshape(patches, 2, part, samples)
        slips = jnp.pad(slips, ((0, 0), (0, 0), (0, rows - part), (0, 0)))
        slips = slips.reshape(patches, 2 * rows, samples)
    blocks = [arrange_slips(slips, over_patch(slips, 1))]
    steps, holds = line_transfers(sites)
    for operand, pairs in steps:
        blocks.append(lax.ppermute(blocks[1 + operand], "site", pairs))

    resident = green_tiles[0].reshape(slot_width, components * lags)
    pieces = [resident] + [over_patch(resident, 2 * step) for step in range(1, chips)]
    slots = lax.dynamic_slice(
        patch_slot, (lax.axis_index("patch") // 2 * (2 * patches),), (2 * patches,)
    )
    picked = pick_tiles(slots.reshape(-1, 1), pieces)
    shifted = shift_tiles(picked, over_patch(picked, 1), lags)

    sums = convolve(shifted, blocks, holds, rows, components, length)
    result = sums[0]
    for step in range(1, chips):
        result = result + over_patch(sums[step], 2 * step)
    return result[None, :part]


def solution(mesh):
    in_specs = (P("patch", "site", None), P("site", "patch", None, None), P())
    out_specs = P("site", "patch", None, None)
    return jax.shard_map(local, mesh=mesh, in_specs=in_specs, out_specs=out_specs, check_vma=False)
```

```python
import functools

import jax
import jax.numpy as jnp
from jax import lax
from jax.experimental import pallas as pl
from jax.experimental.pallas import tpu as pltpu
from jax.sharding import PartitionSpec as P

BLOCK = 16
LANES = 128
ROWS = 8
VMEM_LIMIT = 32 * 1024 * 1024


def round_up(value, unit):
    return -(-value // unit) * unit


def params(limit=VMEM_LIMIT):
    return pltpu.CompilerParams(vmem_limit_bytes=limit)


def arrange_half(slip_ref, out_ref, core, owner):
    patches, both, samples = slip_ref.shape
    rows = both // 2
    per_reg = LANES // BLOCK
    blocks = samples // BLOCK
    depth = patches * BLOCK
    lane_block = lax.broadcasted_iota(jnp.int32, (rows, LANES), 1) // BLOCK
    for group in range(depth // LANES):
        done = {}
        for place in range(per_reg):
            full = slip_ref[group * per_reg + place].astype(jnp.float32)
            source = jnp.where(core == 0, full[:rows], full[rows:])
            for reg in range(samples // LANES):
                piece = source[:, reg * LANES : (reg + 1) * LANES]
                for inner in range(per_reg):
                    turn = (place - inner) % per_reg * BLOCK
                    moved = pltpu.roll(piece, turn, 1) if turn else piece
                    block = reg * per_reg + inner
                    if block in done:
                        moved = jnp.where(lane_block == place, moved, done[block])
                    done[block] = moved
        lanes = pl.ds(pl.multiple_of(owner * depth + group * LANES, LANES), LANES)
        for block in range(0, blocks, 2):
            pair = jnp.concatenate([done[block], done[block + 1]], axis=0)
            out_ref[block * rows : (block + 2) * rows, lanes] = pair.astype(jnp.bfloat16)


def arrange_own_kernel(slip_hbm, green_hbm, out_ref, tiles_ref, slip_ref, green_ref, sems):
    fetch_green = pltpu.make_async_copy(green_hbm, green_ref, sems.at[0])
    fetch_slips = pltpu.make_async_copy(slip_hbm, slip_ref, sems.at[1])
    fetch_green.start()
    fetch_slips.start()
    fetch_green.wait()
    lags = green_ref.shape[2]
    tiles = green_ref[...].astype(jnp.float32)
    for comp in range(green_ref.shape[1]):
        tiles_ref[:, comp * lags : (comp + 1) * lags] = tiles[:, comp, :].astype(jnp.bfloat16)
    fetch_slips.wait()
    core = lax.rem(lax.axis_index("patch"), 2)
    arrange_half(slip_ref, out_ref, core, core)


def arrange_other_kernel(slip_ref, block_ref, out_ref):
    core = lax.rem(lax.axis_index("patch"), 2)
    arrange_half(slip_ref, out_ref, core, 1 - core)


def arrange_own(slips, greens):
    patches, both, samples = slips.shape
    slots, components, lags = greens.shape
    block = jax.ShapeDtypeStruct(
        (samples // BLOCK * both // 2, 2 * patches * BLOCK), jnp.bfloat16
    )
    tiles = jax.ShapeDtypeStruct((slots, components * lags), jnp.bfloat16)
    return pl.pallas_call(
        arrange_own_kernel,
        in_specs=[pl.BlockSpec(memory_space=pltpu.HBM)] * 2,
        out_shape=(block, tiles),
        scratch_shapes=[
            pltpu.VMEM(slips.shape, slips.dtype),
            pltpu.VMEM(greens.shape, greens.dtype),
            pltpu.SemaphoreType.DMA((2,)),
        ],
        compiler_params=params(),
        name="arrange_own",
    )(*(pltpu.with_memory_space_constraint(x, pltpu.HBM) for x in (slips, greens)))


def arrange_other(slips, block):
    return pl.pallas_call(
        arrange_other_kernel,
        out_shape=jax.ShapeDtypeStruct(block.shape, block.dtype),
        input_output_aliases={1: 0},
        compiler_params=params(),
        name="arrange_other",
    )(slips, block)


def pick_kernel(slots_ref, *refs):
    pieces, out_ref = refs[:-1], refs[-1]
    own = lax.axis_index("patch")
    width = pieces[0].shape[0]
    count = out_ref.shape[0]
    total = jnp.zeros(out_ref.shape, jnp.float32)
    for step, piece in enumerate(pieces):
        owner = own ^ (2 * step)
        slot = lax.broadcasted_iota(jnp.int32, (count, width), 1) + owner * width
        pick = (slots_ref[...] == slot).astype(jnp.float32).astype(jnp.bfloat16)
        total = total + jnp.dot(pick, piece[...], preferred_element_type=jnp.float32)
    out_ref[...] = total.astype(jnp.bfloat16)


def pick_tiles(slots, pieces):
    shape = jax.ShapeDtypeStruct((slots.shape[0], pieces[0].shape[1]), jnp.bfloat16)
    return pl.pallas_call(
        pick_kernel, out_shape=shape, compiler_params=params(), name="pick_tiles"
    )(slots, *pieces)


def shift_kernel(lags, left_ref, right_ref, out_ref):
    tiles = left_ref[...].astype(jnp.float32) + right_ref[...].astype(jnp.float32)
    count = tiles.shape[0]
    components = tiles.shape[1] // lags
    width = out_ref.shape[1] // components
    tail = jnp.zeros((BLOCK, width - lags), jnp.float32)
    for patch in range(count):
        for comp in range(components):
            row = tiles[patch : patch + 1, comp * lags : (comp + 1) * lags]
            wide = jnp.concatenate([jnp.broadcast_to(row, (BLOCK, lags)), tail], axis=1)
            moved = pltpu.roll(wide, 0, 1, stride=1, stride_axis=0)
            out_ref[
                patch * BLOCK : (patch + 1) * BLOCK, comp * width : (comp + 1) * width
            ] = moved.astype(jnp.bfloat16)


def shift_tiles(left, right, lags):
    components = left.shape[1] // lags
    width = round_up(lags + BLOCK, LANES)
    shape = jax.ShapeDtypeStruct((left.shape[0] * BLOCK, components * width), jnp.bfloat16)
    return pl.pallas_call(
        functools.partial(shift_kernel, lags),
        out_shape=shape,
        compiler_params=params(),
        name="shift_tiles",
    )(left, right)


def convolve_kernel(rows, length, shifted_ref, *refs):
    sites = len(refs) // 2 - 1
    slip_refs, out_refs = refs[:sites], refs[sites : 2 * sites]
    stack_ref, product_ref = refs[2 * sites :]
    components = out_refs[0].shape[1]
    height = slip_refs[0].shape[0]
    width = shifted_ref.shape[1] // components
    per_reg = LANES // BLOCK
    blocks = height // rows
    turn = lax.axis_index("site") ^ (lax.axis_index("patch") // 2)
    for step, ref in enumerate(slip_refs):
        stack_ref[step ^ turn] = ref[...]
    for comp in range(components):
        product_ref[...] = jnp.dot(
            stack_ref[...].reshape(sites * height, stack_ref.shape[2]),
            shifted_ref[:, comp * width : (comp + 1) * width],
            preferred_element_type=jnp.float32,
        )
        for step in range(sites):
            total = None
            for inner in range(per_reg):
                part = None
                for outer in range(inner, blocks, per_reg):
                    lead = outer // per_reg * LANES
                    start = step * height + outer * rows
                    block = product_ref[start : start + rows, :]
                    pieces = [jnp.zeros((rows, lead), jnp.float32)] if lead else []
                    pieces.append(block[:, : min(width, length - lead)])
                    if length > lead + width:
                        pieces.append(jnp.zeros((rows, length - lead - width), jnp.float32))
                    block = jnp.concatenate(pieces, axis=1) if len(pieces) > 1 else pieces[0]
                    part = block if part is None else part + block
                if inner:
                    part = pltpu.roll(part, inner * BLOCK, 1)
                total = part if total is None else total + part
            out_refs[step][:, comp, :] = total


def convolve(shifted, slips, rows, components, length):
    sites = len(slips)
    height, depth = slips[0].shape
    width = shifted.shape[1] // components
    shape = jax.ShapeDtypeStruct((rows, components, length), jnp.float32)
    return pl.pallas_call(
        functools.partial(convolve_kernel, rows, length),
        out_shape=(shape,) * sites,
        scratch_shapes=[
            pltpu.VMEM((sites, height, depth), jnp.bfloat16),
            pltpu.VMEM((sites * height, width), jnp.float32),
        ],
        compiler_params=params(),
        name="convolve",
    )(shifted, *slips)


def local(slip_rates, green_tiles, patch_slot):
    devices = lax.axis_size("patch")
    sites = lax.axis_size("site")
    chips = devices // 2
    patches, held, samples = slip_rates.shape
    components, lags = green_tiles.shape[2:]
    length = samples + lags
    part = held // 2
    rows = round_up(part, ROWS)
    assert chips == sites and sites & (sites - 1) == 0

    def over_patch(value, offset):
        return lax.ppermute(value, "patch", [(i, i ^ offset) for i in range(devices)])

    slips = slip_rates
    if rows > part:
        slips = slips.reshape(patches, 2, part, samples)
        slips = jnp.pad(slips, ((0, 0), (0, 0), (0, rows - part), (0, 0)))
        slips = slips.reshape(patches, 2 * rows, samples)
    other = over_patch(slips, 1)
    block, resident = arrange_own(slips, green_tiles[0])
    blocks = {0: arrange_other(other, block)}
    for step in [2**i for i in range(sites.bit_length())] + list(range(sites)):
        if 0 < step < sites and step not in blocks:
            low = step & -step
            blocks[step] = lax.ppermute(
                blocks[step - low], "site", [(i, i ^ low) for i in range(sites)]
            )

    pieces = [resident] + [over_patch(resident, 2 * step) for step in range(1, chips)]
    slots = lax.dynamic_slice(
        patch_slot, (lax.axis_index("patch") // 2 * (2 * patches),), (2 * patches,)
    )
    picked = pick_tiles(slots.reshape(-1, 1), pieces)
    shifted = shift_tiles(picked, over_patch(picked, 1), lags)

    sums = convolve(shifted, [blocks[i] for i in range(sites)], rows, components, length)
    result = sums[0]
    for step in range(1, chips):
        result = result + over_patch(sums[step], 2 * step)
    return result[None, :part]


def solution(mesh):
    in_specs = (P("patch", "site", None), P("site", "patch", None, None), P())
    out_specs = P("site", "patch", None, None)
    return jax.shard_map(local, mesh=mesh, in_specs=in_specs, out_specs=out_specs, check_vma=False)
```

```python
import functools

import jax
import jax.numpy as jnp
from jax import lax
from jax.experimental import pallas as pl
from jax.experimental.pallas import tpu as pltpu
from jax.sharding import PartitionSpec as P

BLOCK = 16
LANES = 128
ROWS = 8
VMEM_LIMIT = 32 * 1024 * 1024


def round_up(value, unit):
    return -(-value // unit) * unit


def params(limit=VMEM_LIMIT):
    return pltpu.CompilerParams(vmem_limit_bytes=limit)


def arrange_half(slip_ref, out_ref, core, owner):
    patches, both, samples = slip_ref.shape
    rows = both // 2
    per_reg = LANES // BLOCK
    blocks = samples // BLOCK
    depth = patches * BLOCK
    lane_block = lax.broadcasted_iota(jnp.int32, (rows, LANES), 1) // BLOCK
    for group in range(depth // LANES):
        done = {}
        for place in range(per_reg):
            full = slip_ref[group * per_reg + place].astype(jnp.float32)
            source = jnp.where(core == 0, full[:rows], full[rows:])
            for reg in range(samples // LANES):
                piece = source[:, reg * LANES : (reg + 1) * LANES]
                for inner in range(per_reg):
                    turn = (place - inner) % per_reg * BLOCK
                    moved = pltpu.roll(piece, turn, 1) if turn else piece
                    block = reg * per_reg + inner
                    if block in done:
                        moved = jnp.where(lane_block == place, moved, done[block])
                    done[block] = moved
        lanes = pl.ds(pl.multiple_of(owner * depth + group * LANES, LANES), LANES)
        for block in range(0, blocks, 2):
            pair = jnp.concatenate([done[block], done[block + 1]], axis=0)
            out_ref[block * rows : (block + 2) * rows, lanes] = pair.astype(jnp.bfloat16)


def lay_out(green_ref, tiles_ref):
    lags = green_ref.shape[2]
    tiles = green_ref[...].astype(jnp.float32)
    for comp in range(green_ref.shape[1]):
        tiles_ref[:, comp * lags : (comp + 1) * lags] = tiles[:, comp, :].astype(jnp.bfloat16)


def arrange_own_kernel(slip_hbm, green_hbm, out_ref, tiles_ref, slip_ref, green_ref, sems):
    fetch_green = pltpu.make_async_copy(green_hbm, green_ref, sems.at[0])
    fetch_slips = pltpu.make_async_copy(slip_hbm, slip_ref, sems.at[1])
    fetch_green.start()
    fetch_slips.start()
    fetch_green.wait()
    lay_out(green_ref, tiles_ref)
    fetch_slips.wait()
    core = lax.rem(lax.axis_index("patch"), 2)
    arrange_half(slip_ref, out_ref, core, core)


def arrange_other_kernel(slip_ref, green_ref, block_ref, out_ref, tiles_ref):
    core = lax.rem(lax.axis_index("patch"), 2)
    arrange_half(slip_ref, out_ref, core, 1 - core)
    lay_out(green_ref, tiles_ref)


def arrange_own(slips, greens):
    patches, both, samples = slips.shape
    slots, components, lags = greens.shape
    block = jax.ShapeDtypeStruct(
        (samples // BLOCK * both // 2, 2 * patches * BLOCK), jnp.bfloat16
    )
    tiles = jax.ShapeDtypeStruct((slots, components * lags), jnp.bfloat16)
    return pl.pallas_call(
        arrange_own_kernel,
        in_specs=[pl.BlockSpec(memory_space=pltpu.HBM)] * 2,
        out_shape=(block, tiles),
        scratch_shapes=[
            pltpu.VMEM(slips.shape, slips.dtype),
            pltpu.VMEM(greens.shape, greens.dtype),
            pltpu.SemaphoreType.DMA((2,)),
        ],
        compiler_params=params(),
        name="arrange_own",
    )(*(pltpu.with_memory_space_constraint(x, pltpu.HBM) for x in (slips, greens)))


def arrange_other(slips, greens, block):
    slots, components, lags = greens.shape
    tiles = jax.ShapeDtypeStruct((slots, components * lags), jnp.bfloat16)
    return pl.pallas_call(
        arrange_other_kernel,
        out_shape=(jax.ShapeDtypeStruct(block.shape, block.dtype), tiles),
        input_output_aliases={2: 0},
        compiler_params=params(),
        name="arrange_other",
    )(slips, greens, block)


def earlier_in_chip(count, per_chip):
    q = lax.broadcasted_iota(jnp.int32, (count, count), 0)
    p = lax.broadcasted_iota(jnp.int32, (count, count), 1)
    return ((q < p) & (q // per_chip == p // per_chip)).astype(jnp.float32).astype(jnp.bfloat16)


def one_hot(condition):
    return condition.astype(jnp.float32).astype(jnp.bfloat16)


def route_kernel(chips, per_chip, capacity, slots_ref, own_ref, other_ref, *out_refs):
    width = own_ref.shape[0]
    components = out_refs[0].shape[0] // capacity
    lags = own_ref.shape[1] // components
    count = slots_ref.shape[1]
    own = lax.axis_index("patch")
    chip, core = own // 2, lax.rem(own, 2)
    slots = slots_ref[...]
    owner = slots // width
    mine = owner // 2 == chip
    place = slots % width + jnp.where(owner % 2 == core, 0, width)
    marks = jnp.broadcast_to(one_hot(mine), (16, count))
    rank = jnp.dot(marks, earlier_in_chip(count, per_chip), preferred_element_type=jnp.float32)
    rank = rank[:1].astype(jnp.int32)
    target = (lax.broadcasted_iota(jnp.int32, (1, count), 1) // per_chip) ^ chip
    code = jnp.where(mine, target * capacity + rank, -1)
    code_pick = one_hot(lax.broadcasted_iota(jnp.int32, (chips * capacity, count), 0) == code)
    slot_pick = one_hot(lax.broadcasted_iota(jnp.int32, (2 * width, count), 0) == place)
    pick = lax.dot_general(
        code_pick, slot_pick, (((1,), (1,)), ((), ())), preferred_element_type=jnp.float32
    ).astype(jnp.bfloat16)
    for comp in range(components):
        lanes = slice(comp * lags, (comp + 1) * lags)
        both = jnp.concatenate([own_ref[:, lanes], other_ref[:, lanes]], axis=0)
        chosen = jnp.dot(pick, both, preferred_element_type=jnp.float32).astype(jnp.bfloat16)
        for step, out_ref in enumerate(out_refs):
            out_ref[comp * capacity : (comp + 1) * capacity, :] = chosen[
                step * capacity : (step + 1) * capacity
            ]


def route_tiles(slots, own, other, chips, per_chip, capacity, components):
    lags = own.shape[1] // components
    shape = jax.ShapeDtypeStruct((components * capacity, lags), jnp.bfloat16)
    return pl.pallas_call(
        functools.partial(route_kernel, chips, per_chip, capacity),
        out_shape=(shape,) * chips,
        compiler_params=params(),
        name="route_tiles",
    )(slots, own, other)


def pass_on(value, *others):
    def kernel(*refs):
        pass

    return pl.pallas_call(
        kernel,
        in_specs=[pl.BlockSpec(memory_space=pl.ANY)] * (1 + len(others)),
        out_specs=pl.BlockSpec(memory_space=pl.ANY),
        out_shape=jax.ShapeDtypeStruct(value.shape, value.dtype),
        input_output_aliases={0: 0},
        compiler_params=params(),
        name="pass_on",
    )(value, *others)


def shift_kernel(width, per_chip, slots_ref, *refs):
    pieces, out_ref = refs[:-1], refs[-1]
    chips = len(pieces)
    lags = pieces[0].shape[1]
    span = out_ref.shape[1]
    components = span // round_up(lags + BLOCK, LANES)
    span = span // components
    capacity = pieces[0].shape[0] // components
    count = slots_ref.shape[1]
    chip = lax.axis_index("patch") // 2
    mine = pltpu.roll(slots_ref[...], lax.rem(count - chip * per_chip, count), 1)[:, :per_chip]
    owner = (mine // (2 * width)) ^ chip
    marks = lax.broadcasted_iota(jnp.int32, (round_up(chips, 16), per_chip), 0) == owner
    rank = jnp.dot(
        one_hot(marks), earlier_in_chip(per_chip, per_chip), preferred_element_type=jnp.float32
    )
    rank = jnp.sum(jnp.where(marks, rank, 0.0), axis=0, keepdims=True).astype(jnp.int32)
    code = owner * capacity + rank
    pick = one_hot(lax.broadcasted_iota(jnp.int32, (chips * capacity, per_chip), 0) == code)
    tail = jnp.zeros((BLOCK, span - lags), jnp.float32)
    for comp in range(components):
        arrived = jnp.concatenate(
            [piece[comp * capacity : (comp + 1) * capacity, :] for piece in pieces], axis=0
        )
        tiles = lax.dot_general(
            pick, arrived, (((0,), (0,)), ((), ())), preferred_element_type=jnp.float32
        )
        for patch in range(per_chip):
            row = jnp.broadcast_to(tiles[patch : patch + 1], (BLOCK, lags))
            wide = jnp.concatenate([row, tail], axis=1)
            moved = pltpu.roll(wide, 0, 1, stride=1, stride_axis=0)
            out_ref[
                patch * BLOCK : (patch + 1) * BLOCK, comp * span : (comp + 1) * span
            ] = moved.astype(jnp.bfloat16)


def shift_tiles(slots, pieces, width, per_chip, components):
    lags = pieces[0].shape[1]
    span = round_up(lags + BLOCK, LANES)
    shape = jax.ShapeDtypeStruct((per_chip * BLOCK, components * span), jnp.bfloat16)
    return pl.pallas_call(
        functools.partial(shift_kernel, width, per_chip),
        out_shape=shape,
        compiler_params=params(),
        name="shift_tiles",
    )(slots, *pieces)


def convolve_kernel(rows, length, shifted_ref, *refs):
    sites = len(refs) // 2 - 1
    slip_refs, out_refs = refs[:sites], refs[sites : 2 * sites]
    stack_ref, product_ref = refs[2 * sites :]
    components = out_refs[0].shape[1]
    height = slip_refs[0].shape[0]
    width = shifted_ref.shape[1] // components
    per_reg = LANES // BLOCK
    blocks = height // rows
    turn = lax.axis_index("site") ^ (lax.axis_index("patch") // 2)
    for step, ref in enumerate(slip_refs):
        stack_ref[step ^ turn] = ref[...]
    for comp in range(components):
        product_ref[...] = jnp.dot(
            stack_ref[...].reshape(sites * height, stack_ref.shape[2]),
            shifted_ref[:, comp * width : (comp + 1) * width],
            preferred_element_type=jnp.float32,
        )
        for step in range(sites):
            total = None
            for inner in range(per_reg):
                part = None
                for outer in range(inner, blocks, per_reg):
                    lead = outer // per_reg * LANES
                    start = step * height + outer * rows
                    block = product_ref[start : start + rows, :]
                    pieces = [jnp.zeros((rows, lead), jnp.float32)] if lead else []
                    pieces.append(block[:, : min(width, length - lead)])
                    if length > lead + width:
                        pieces.append(jnp.zeros((rows, length - lead - width), jnp.float32))
                    block = jnp.concatenate(pieces, axis=1) if len(pieces) > 1 else pieces[0]
                    part = block if part is None else part + block
                if inner:
                    part = pltpu.roll(part, inner * BLOCK, 1)
                total = part if total is None else total + part
            out_refs[step][:, comp, :] = total


def convolve(shifted, slips, rows, components, length):
    sites = len(slips)
    height, depth = slips[0].shape
    width = shifted.shape[1] // components
    shape = jax.ShapeDtypeStruct((rows, components, length), jnp.float32)
    return pl.pallas_call(
        functools.partial(convolve_kernel, rows, length),
        out_shape=(shape,) * sites,
        scratch_shapes=[
            pltpu.VMEM((sites, height, depth), jnp.bfloat16),
            pltpu.VMEM((sites * height, width), jnp.float32),
        ],
        compiler_params=params(),
        name="convolve",
    )(shifted, *slips)


def local(slip_rates, green_tiles, patch_slot):
    devices = lax.axis_size("patch")
    sites = lax.axis_size("site")
    chips = devices // 2
    patches, held, samples = slip_rates.shape
    slot_width, components, lags = green_tiles.shape[1:]
    length = samples + lags
    part = held // 2
    rows = round_up(part, ROWS)
    assert chips == sites and sites & (sites - 1) == 0

    def over_patch(value, offset):
        return lax.ppermute(value, "patch", [(i, i ^ offset) for i in range(devices)])

    slips = slip_rates
    if rows > part:
        slips = slips.reshape(patches, 2, part, samples)
        slips = jnp.pad(slips, ((0, 0), (0, 0), (0, rows - part), (0, 0)))
        slips = slips.reshape(patches, 2 * rows, samples)
    other = over_patch(slips, 1)
    other_tiles = over_patch(green_tiles[0], 1)
    block, own_tiles = arrange_own(slips, green_tiles[0])
    block, other_tiles = arrange_other(other, other_tiles, block)

    slots = patch_slot.reshape(1, -1)
    share = 2 * max(1, patches // devices)
    capacity = round_up(4 * share, 16)
    pieces = route_tiles(
        slots, own_tiles, other_tiles, chips, 2 * patches, capacity, components
    )
    pieces = [pieces[0]] + [over_patch(pieces[step], 2 * step) for step in range(1, chips)]

    blocks = {0: block}
    for step in [2**i for i in range(sites.bit_length())] + list(range(sites)):
        if 0 < step < sites and step not in blocks:
            low = step & -step
            blocks[step] = lax.ppermute(
                blocks[step - low], "site", [(i, i ^ low) for i in range(sites)]
            )
            if step == sites // 2:
                blocks[step] = pass_on(blocks[step], *pieces[1:])
    shifted = shift_tiles(slots, pieces, slot_width, 2 * patches, components)

    sums = convolve(shifted, [blocks[i] for i in range(sites)], rows, components, length)
    result = sums[0]
    for step in range(1, chips):
        result = result + over_patch(sums[step], 2 * step)
    return result[None, :part]


def solution(mesh):
    in_specs = (P("patch", "site", None), P("site", "patch", None, None), P())
    out_specs = P("site", "patch", None, None)
    return jax.shard_map(local, mesh=mesh, in_specs=in_specs, out_specs=out_specs, check_vma=False)
```

```python
import functools

import jax
import jax.numpy as jnp
from jax import lax
from jax.experimental import pallas as pl
from jax.experimental.pallas import tpu as pltpu
from jax.sharding import PartitionSpec as P

BLOCK = 16
LANES = 128
ROWS = 8
VMEM_LIMIT = 32 * 1024 * 1024
LARGEST = 32767.0
STEPS = 16
SMALLEST = 1e-30


def round_up(value, unit):
    return -(-value // unit) * unit


def params(limit=VMEM_LIMIT):
    return pltpu.CompilerParams(vmem_limit_bytes=limit)


def arrange_half(slip_ref, out_ref, core, owner):
    patches, both, samples = slip_ref.shape
    rows = both // 2
    per_reg = LANES // BLOCK
    blocks = samples // BLOCK
    depth = patches * BLOCK
    lane_block = lax.broadcasted_iota(jnp.int32, (rows, LANES), 1) // BLOCK
    for group in range(depth // LANES):
        done = {}
        for place in range(per_reg):
            full = slip_ref[group * per_reg + place].astype(jnp.float32)
            source = jnp.where(core == 0, full[:rows], full[rows:])
            for reg in range(samples // LANES):
                piece = source[:, reg * LANES : (reg + 1) * LANES]
                for inner in range(per_reg):
                    turn = (place - inner) % per_reg * BLOCK
                    moved = pltpu.roll(piece, turn, 1) if turn else piece
                    block = reg * per_reg + inner
                    if block in done:
                        moved = jnp.where(lane_block == place, moved, done[block])
                    done[block] = moved
        lanes = pl.ds(pl.multiple_of(owner * depth + group * LANES, LANES), LANES)
        for block in range(0, blocks, 2):
            pair = jnp.concatenate([done[block], done[block + 1]], axis=0)
            out_ref[block * rows : (block + 2) * rows, lanes] = pair.astype(jnp.bfloat16)


def arrange_own_kernel(slip_hbm, slots_hbm, out_ref, slots_ref, slip_ref, sems):
    fetch_slips = pltpu.make_async_copy(slip_hbm, slip_ref, sems.at[0])
    fetch_slots = pltpu.make_async_copy(slots_hbm, slots_ref, sems.at[1])
    fetch_slips.start()
    fetch_slots.start()
    fetch_slots.wait()
    fetch_slips.wait()
    core = lax.rem(lax.axis_index("patch"), 2)
    arrange_half(slip_ref, out_ref, core, core)


def arrange_other_kernel(slip_ref, green_ref, block_ref, out_ref):
    core = lax.rem(lax.axis_index("patch"), 2)
    arrange_half(slip_ref, out_ref, core, 1 - core)


def in_hbm(*values):
    return [pltpu.with_memory_space_constraint(value, pltpu.HBM) for value in values]


def arrange_own(slips, slots):
    patches, both, samples = slips.shape
    block = jax.ShapeDtypeStruct(
        (samples // BLOCK * both // 2, 2 * patches * BLOCK), jnp.bfloat16
    )
    return pl.pallas_call(
        arrange_own_kernel,
        in_specs=[pl.BlockSpec(memory_space=pltpu.HBM)] * 2,
        out_shape=(block, jax.ShapeDtypeStruct(slots.shape, slots.dtype)),
        scratch_shapes=[
            pltpu.VMEM(slips.shape, slips.dtype),
            pltpu.SemaphoreType.DMA((2,)),
        ],
        compiler_params=params(),
        name="arrange_own",
    )(*in_hbm(slips, slots))


def arrange_other(slips, greens, block):
    return pl.pallas_call(
        arrange_other_kernel,
        in_specs=[
            pl.BlockSpec(memory_space=pltpu.VMEM),
            pl.BlockSpec(memory_space=pl.ANY),
            pl.BlockSpec(memory_space=pltpu.VMEM),
        ],
        out_shape=jax.ShapeDtypeStruct(block.shape, block.dtype),
        input_output_aliases={2: 0},
        compiler_params=params(),
        name="arrange_other",
    )(slips, greens, block)


def earlier_in_chip(count, per_chip):
    q = lax.broadcasted_iota(jnp.int32, (count, count), 0)
    p = lax.broadcasted_iota(jnp.int32, (count, count), 1)
    return ((q < p) & (q // per_chip == p // per_chip)).astype(jnp.float32).astype(jnp.bfloat16)


def one_hot(condition):
    return condition.astype(jnp.float32).astype(jnp.bfloat16)


def route_kernel(chips, per_chip, capacity, slots_ref, own_hbm, other_ref, *refs):
    out_refs, (own_ref, sem) = refs[:-2], refs[-2:]
    fetch = pltpu.make_async_copy(own_hbm, own_ref, sem)
    fetch.start()
    width, components, lags = own_ref.shape
    count = slots_ref.shape[1]
    own = lax.axis_index("patch")
    chip, core = own // 2, lax.rem(own, 2)
    slots = slots_ref[...]
    owner = slots // width
    mine = owner // 2 == chip
    place = slots % width + jnp.where(owner % 2 == core, 0, width)
    marks = jnp.broadcast_to(one_hot(mine), (16, count))
    rank = jnp.dot(marks, earlier_in_chip(count, per_chip), preferred_element_type=jnp.float32)
    rank = rank[:1].astype(jnp.int32)
    target = (lax.broadcasted_iota(jnp.int32, (1, count), 1) // per_chip) ^ chip
    code = jnp.where(mine, target * capacity + rank, -1)
    code_pick = one_hot(lax.broadcasted_iota(jnp.int32, (chips * capacity, count), 0) == code)
    slot_pick = one_hot(lax.broadcasted_iota(jnp.int32, (2 * width, count), 0) == place)
    pick = lax.dot_general(
        code_pick, slot_pick, (((1,), (1,)), ((), ())), preferred_element_type=jnp.float32
    ).astype(jnp.bfloat16)
    fetch.wait()
    tiles = jnp.concatenate([own_ref[...], other_ref[...]], axis=0).astype(jnp.float32)
    for comp in range(components):
        both = tiles[:, comp, :].astype(jnp.bfloat16)
        chosen = jnp.dot(pick, both, preferred_element_type=jnp.float32).astype(jnp.bfloat16)
        for step, out_ref in enumerate(out_refs):
            out_ref[comp * capacity : (comp + 1) * capacity, :] = chosen[
                step * capacity : (step + 1) * capacity
            ]


def route_tiles(slots, own, other, chips, per_chip, capacity):
    components, lags = own.shape[1:]
    shape = jax.ShapeDtypeStruct((components * capacity, lags), jnp.bfloat16)
    return pl.pallas_call(
        functools.partial(route_kernel, chips, per_chip, capacity),
        in_specs=[
            pl.BlockSpec(memory_space=pltpu.VMEM),
            pl.BlockSpec(memory_space=pltpu.HBM),
            pl.BlockSpec(memory_space=pltpu.VMEM),
        ],
        out_shape=(shape,) * chips,
        scratch_shapes=[pltpu.VMEM(own.shape, own.dtype), pltpu.SemaphoreType.DMA],
        compiler_params=params(),
        name="route_tiles",
    )(slots, *in_hbm(own), other)


def pass_on(value, *others):
    def kernel(*refs):
        pass

    return pl.pallas_call(
        kernel,
        in_specs=[pl.BlockSpec(memory_space=pl.ANY)] * (1 + len(others)),
        out_specs=pl.BlockSpec(memory_space=pl.ANY),
        out_shape=jax.ShapeDtypeStruct(value.shape, value.dtype),
        input_output_aliases={0: 0},
        compiler_params=params(),
        name="pass_on",
    )(value, *others)


def shift_kernel(width, per_chip, slots_ref, *refs):
    pieces, out_ref = refs[:-1], refs[-1]
    chips = len(pieces)
    lags = pieces[0].shape[1]
    span = out_ref.shape[1]
    components = span // round_up(lags + BLOCK, LANES)
    span = span // components
    capacity = pieces[0].shape[0] // components
    count = slots_ref.shape[1]
    chip = lax.axis_index("patch") // 2
    mine = pltpu.roll(slots_ref[...], lax.rem(count - chip * per_chip, count), 1)[:, :per_chip]
    owner = (mine // (2 * width)) ^ chip
    marks = lax.broadcasted_iota(jnp.int32, (round_up(chips, 16), per_chip), 0) == owner
    rank = jnp.dot(
        one_hot(marks), earlier_in_chip(per_chip, per_chip), preferred_element_type=jnp.float32
    )
    rank = jnp.sum(jnp.where(marks, rank, 0.0), axis=0, keepdims=True).astype(jnp.int32)
    code = owner * capacity + rank
    pick = one_hot(lax.broadcasted_iota(jnp.int32, (chips * capacity, per_chip), 0) == code)
    tail = jnp.zeros((BLOCK, span - lags), jnp.float32)
    for comp in range(components):
        arrived = jnp.concatenate(
            [piece[comp * capacity : (comp + 1) * capacity, :] for piece in pieces], axis=0
        )
        tiles = lax.dot_general(
            pick, arrived, (((0,), (0,)), ((), ())), preferred_element_type=jnp.float32
        )
        for patch in range(per_chip):
            row = jnp.broadcast_to(tiles[patch : patch + 1], (BLOCK, lags))
            wide = jnp.concatenate([row, tail], axis=1)
            moved = pltpu.roll(wide, 0, 1, stride=1, stride_axis=0)
            out_ref[
                patch * BLOCK : (patch + 1) * BLOCK, comp * span : (comp + 1) * span
            ] = moved.astype(jnp.bfloat16)


def shift_tiles(slots, pieces, width, per_chip, components):
    lags = pieces[0].shape[1]
    span = round_up(lags + BLOCK, LANES)
    shape = jax.ShapeDtypeStruct((per_chip * BLOCK, components * span), jnp.bfloat16)
    return pl.pallas_call(
        functools.partial(shift_kernel, width, per_chip),
        out_shape=shape,
        compiler_params=params(),
        name="shift_tiles",
    )(slots, *pieces)


def convolve_blocks(shifted_ref, slip_refs, stack_ref, product_ref, out_ref, rows):
    length = out_ref.shape[2]
    components = out_ref.shape[1] // rows
    height = slip_refs[0].shape[0]
    width = shifted_ref.shape[1] // components
    per_reg = LANES // BLOCK
    blocks = height // rows
    for step, ref in enumerate(slip_refs):
        stack_ref[step * height : (step + 1) * height] = ref[...]
    for comp in range(components):
        product_ref[...] = jnp.dot(
            stack_ref[...],
            shifted_ref[:, comp * width : (comp + 1) * width],
            preferred_element_type=jnp.float32,
        )
        for step in range(len(slip_refs)):
            total = None
            for inner in range(per_reg):
                part = None
                for outer in range(inner, blocks, per_reg):
                    lead = outer // per_reg * LANES
                    start = step * height + outer * rows
                    block = product_ref[start : start + rows, :]
                    pieces = [jnp.zeros((rows, lead), jnp.float32)] if lead else []
                    pieces.append(block[:, : min(width, length - lead)])
                    if length > lead + width:
                        pieces.append(jnp.zeros((rows, length - lead - width), jnp.float32))
                    block = jnp.concatenate(pieces, axis=1) if len(pieces) > 1 else pieces[0]
                    part = block if part is None else part + block
                if inner:
                    part = pltpu.roll(part, inner * BLOCK, 1)
                total = part if total is None else total + part
            out_ref[step, comp * rows : (comp + 1) * rows, :] = total


def convolve_first_kernel(rows, shifted_ref, *refs):
    slip_refs, (out_ref, stack_ref, product_ref) = refs[:-3], refs[-3:]
    convolve_blocks(shifted_ref, slip_refs, stack_ref, product_ref, out_ref, rows)


def convolve_scratch(shifted, count, height, depth, components):
    return [
        pltpu.VMEM((count * height, depth), jnp.bfloat16),
        pltpu.VMEM((count * height, shifted.shape[1] // components), jnp.float32),
    ]


def convolve_first(shifted, slips, rows, components, length):
    shape = jax.ShapeDtypeStruct((len(slips), components * rows, length), jnp.float32)
    return pl.pallas_call(
        functools.partial(convolve_first_kernel, rows),
        out_shape=shape,
        scratch_shapes=convolve_scratch(shifted, len(slips), *slips[0].shape, components),
        compiler_params=params(),
        name="convolve_first",
    )(shifted, *slips)


def unit_of(exponent):
    return jnp.exp2(exponent.astype(jnp.float32) * (1.0 / STEPS)) * (1.0 / LARGEST)


def convolve_last_kernel(rows, shifted_ref, slip_ref, first_ref, *refs):
    out_refs, (stack_ref, product_ref, last_ref) = refs[:-3], refs[-3:]
    convolve_blocks(shifted_ref, [slip_ref], stack_ref, product_ref, last_ref, rows)
    count = first_ref.shape[0]
    length = first_ref.shape[2]
    turn = lax.axis_index("site") ^ (lax.axis_index("patch") // 2)
    last = last_ref[0]
    for step, ref in enumerate(out_refs):
        source = step ^ turn
        total = jnp.where(source == count, last, first_ref[jnp.minimum(source, count - 1)])
        if step == 0:
            ref[...] = total
            continue
        peak = jnp.maximum(jnp.max(jnp.abs(total), axis=1, keepdims=True), SMALLEST)
        exponent = jnp.ceil(jnp.log2(peak) * STEPS).astype(jnp.int32)
        scaled = jnp.round(total * (1.0 / unit_of(exponent)))
        whole = jnp.clip(scaled, -LARGEST, LARGEST).astype(jnp.int32)
        ref[:, :length] = whole.astype(jnp.int16)
        ref[:, length:] = jnp.broadcast_to(
            exponent, (exponent.shape[0], ref.shape[1] - length)
        ).astype(jnp.int16)


def convolve_last(shifted, slip, first, rows, components):
    count, height, length = first.shape
    own = jax.ShapeDtypeStruct((height, length), jnp.float32)
    sent = jax.ShapeDtypeStruct((height, round_up(length, LANES) + LANES), jnp.int16)
    return pl.pallas_call(
        functools.partial(convolve_last_kernel, rows),
        out_shape=(own,) + (sent,) * count,
        scratch_shapes=convolve_scratch(shifted, 1, *slip.shape, components)
        + [pltpu.VMEM((1, height, length), jnp.float32)],
        compiler_params=params(),
        name="convolve_last",
    )(shifted, slip, first)


def add_kernel(own_ref, *refs):
    sent_refs, out_ref = refs[:-1], refs[-1]
    part, components, length = out_ref.shape
    rows = own_ref.shape[0] // components
    total = own_ref[...]
    for ref in sent_refs:
        unit = unit_of(ref[:, length:].astype(jnp.int32)[:, :1])
        total = total + ref[:, :length].astype(jnp.int32).astype(jnp.float32) * unit
    for comp in range(components):
        out_ref[:, comp, :] = total[comp * rows : comp * rows + part]


def add_up(own, sent, part, components):
    return pl.pallas_call(
        add_kernel,
        out_shape=jax.ShapeDtypeStruct((part, components, own.shape[1]), jnp.float32),
        compiler_params=params(),
        name="add_up",
    )(own, *sent)


def local(slip_rates, green_tiles, patch_slot):
    devices = lax.axis_size("patch")
    sites = lax.axis_size("site")
    chips = devices // 2
    patches, held, samples = slip_rates.shape
    slot_width, components, lags = green_tiles.shape[1:]
    length = samples + lags
    part = held // 2
    rows = round_up(part, ROWS)
    assert chips == sites and sites & (sites - 1) == 0

    def over_patch(value, offset):
        return lax.ppermute(value, "patch", [(i, i ^ offset) for i in range(devices)])

    slips = slip_rates
    if rows > part:
        slips = slips.reshape(patches, 2, part, samples)
        slips = jnp.pad(slips, ((0, 0), (0, 0), (0, rows - part), (0, 0)))
        slips = slips.reshape(patches, 2 * rows, samples)
    greens = green_tiles[0]
    other, other_tiles = over_patch(slips, 1), over_patch(greens, 1)
    block, slots = arrange_own(slips, patch_slot.reshape(1, -1))
    block = arrange_other(other, other_tiles, block)

    share = 2 * max(1, patches // devices)
    capacity = round_up(4 * share, 16)
    pieces = route_tiles(slots, greens, other_tiles, chips, 2 * patches, capacity)
    pieces = [pieces[0]] + [over_patch(pieces[step], 2 * step) for step in range(1, chips)]

    blocks = {0: block}
    for step in [2**i for i in range(sites.bit_length())] + list(range(sites)):
        if 0 < step < sites and step not in blocks:
            low = step & -step
            blocks[step] = lax.ppermute(
                blocks[step - low], "site", [(i, i ^ low) for i in range(sites)]
            )
            if step == sites // 2:
                blocks[step] = pass_on(blocks[step], *pieces[1:])
    shifted = shift_tiles(slots, pieces, slot_width, 2 * patches, components)

    slips = [blocks[step] for step in range(sites)]
    first = convolve_first(shifted, slips[:-1], rows, components, length)
    sums = convolve_last(shifted, slips[-1], first, rows, components)
    sent = [over_patch(sums[step], 2 * step) for step in range(1, chips)]
    return add_up(sums[0], sent, part, components)[None]


def solution(mesh):
    in_specs = (P("patch", "site", None), P("site", "patch", None, None), P())
    out_specs = P("site", "patch", None, None)
    return jax.shard_map(local, mesh=mesh, in_specs=in_specs, out_specs=out_specs, check_vma=False)
```

```python
import functools

import jax
import jax.numpy as jnp
from jax import lax
from jax.experimental import pallas as pl
from jax.experimental.pallas import tpu as pltpu
from jax.sharding import PartitionSpec as P

BLOCK = 16
LANES = 128
ROWS = 8
VMEM_LIMIT = 32 * 1024 * 1024
LARGEST = 32767.0
STEPS = 16
SMALLEST = 1e-30


def round_up(value, unit):
    return -(-value // unit) * unit


def params(limit=VMEM_LIMIT):
    return pltpu.CompilerParams(vmem_limit_bytes=limit)


def arrange_half(slip_ref, out_ref, core, owner):
    patches, both, samples = slip_ref.shape
    rows = both // 2
    per_reg = LANES // BLOCK
    blocks = samples // BLOCK
    depth = patches * BLOCK
    lane_block = lax.broadcasted_iota(jnp.int32, (rows, LANES), 1) // BLOCK
    for group in range(depth // LANES):
        done = {}
        for place in range(per_reg):
            full = slip_ref[group * per_reg + place].astype(jnp.float32)
            source = jnp.where(core == 0, full[:rows], full[rows:])
            for reg in range(samples // LANES):
                piece = source[:, reg * LANES : (reg + 1) * LANES]
                for inner in range(per_reg):
                    turn = (place - inner) % per_reg * BLOCK
                    moved = pltpu.roll(piece, turn, 1) if turn else piece
                    block = reg * per_reg + inner
                    if block in done:
                        moved = jnp.where(lane_block == place, moved, done[block])
                    done[block] = moved
        lanes = pl.ds(pl.multiple_of(owner * depth + group * LANES, LANES), LANES)
        for block in range(0, blocks, 2):
            pair = jnp.concatenate([done[block], done[block + 1]], axis=0)
            out_ref[block * rows : (block + 2) * rows, lanes] = pair.astype(jnp.bfloat16)


def arrange_own_kernel(
    slip_hbm, slots_hbm, green_hbm, out_ref, slots_ref, green_ref, slip_ref, sems
):
    fetch_slips = pltpu.make_async_copy(slip_hbm, slip_ref, sems.at[0])
    fetch_slots = pltpu.make_async_copy(slots_hbm, slots_ref, sems.at[1])
    fetch_greens = pltpu.make_async_copy(green_hbm, green_ref, sems.at[2])
    fetch_slips.start()
    fetch_slots.start()
    fetch_greens.start()
    fetch_slips.wait()
    core = lax.rem(lax.axis_index("patch"), 2)
    arrange_half(slip_ref, out_ref, core, core)
    fetch_slots.wait()
    fetch_greens.wait()


def arrange_other_kernel(slip_ref, green_ref, block_ref, out_ref):
    core = lax.rem(lax.axis_index("patch"), 2)
    arrange_half(slip_ref, out_ref, core, 1 - core)


def in_hbm(*values):
    return [pltpu.with_memory_space_constraint(value, pltpu.HBM) for value in values]


def arrange_own(slips, slots, greens):
    patches, both, samples = slips.shape
    block = jax.ShapeDtypeStruct(
        (samples // BLOCK * both // 2, 2 * patches * BLOCK), jnp.bfloat16
    )
    return pl.pallas_call(
        arrange_own_kernel,
        in_specs=[pl.BlockSpec(memory_space=pltpu.HBM)] * 3,
        out_shape=(
            block,
            jax.ShapeDtypeStruct(slots.shape, slots.dtype),
            jax.ShapeDtypeStruct(greens.shape, greens.dtype),
        ),
        scratch_shapes=[
            pltpu.VMEM(slips.shape, slips.dtype),
            pltpu.SemaphoreType.DMA((3,)),
        ],
        compiler_params=params(),
        name="arrange_own",
    )(*in_hbm(slips, slots, greens))


def arrange_other(slips, greens, block):
    return pl.pallas_call(
        arrange_other_kernel,
        in_specs=[
            pl.BlockSpec(memory_space=pltpu.VMEM),
            pl.BlockSpec(memory_space=pl.ANY),
            pl.BlockSpec(memory_space=pltpu.VMEM),
        ],
        out_shape=jax.ShapeDtypeStruct(block.shape, block.dtype),
        input_output_aliases={2: 0},
        compiler_params=params(),
        name="arrange_other",
    )(slips, greens, block)


def earlier_in_chip(count, per_chip):
    q = lax.broadcasted_iota(jnp.int32, (count, count), 0)
    p = lax.broadcasted_iota(jnp.int32, (count, count), 1)
    return ((q < p) & (q // per_chip == p // per_chip)).astype(jnp.float32).astype(jnp.bfloat16)


def one_hot(condition):
    return condition.astype(jnp.float32).astype(jnp.bfloat16)


def route_kernel(chips, per_chip, capacity, slots_ref, own_ref, other_ref, pick_ref, *out_refs):
    width, components, lags = own_ref.shape
    count = slots_ref.shape[1]
    own = lax.axis_index("patch")
    chip, core = own // 2, lax.rem(own, 2)
    slots = slots_ref[...]
    owner = slots // width
    mine = owner // 2 == chip
    place = slots % width + jnp.where(owner % 2 == core, 0, width)
    marks = jnp.broadcast_to(one_hot(mine), (16, count))
    rank = jnp.dot(marks, earlier_in_chip(count, per_chip), preferred_element_type=jnp.float32)
    rank = rank[:1].astype(jnp.int32)
    target = (lax.broadcasted_iota(jnp.int32, (1, count), 1) // per_chip) ^ chip
    code = jnp.where(mine, target * capacity + rank, -1)
    code_pick = one_hot(lax.broadcasted_iota(jnp.int32, (chips * capacity, count), 0) == code)
    slot_pick = one_hot(lax.broadcasted_iota(jnp.int32, (2 * width, count), 0) == place)
    pick = lax.dot_general(
        code_pick, slot_pick, (((1,), (1,)), ((), ())), preferred_element_type=jnp.float32
    ).astype(jnp.bfloat16)
    tiles = jnp.concatenate([own_ref[...], other_ref[...]], axis=0).astype(jnp.float32)
    for comp in range(components):
        both = tiles[:, comp, :].astype(jnp.bfloat16)
        chosen = jnp.dot(pick, both, preferred_element_type=jnp.float32).astype(jnp.bfloat16)
        for step, out_ref in enumerate(out_refs):
            out_ref[comp * capacity : (comp + 1) * capacity, :] = chosen[
                step * capacity : (step + 1) * capacity
            ]
    here = pltpu.roll(slots, lax.rem(count - chip * per_chip, count), 1)[:, :per_chip]
    owner = (here // (2 * width)) ^ chip
    marks = lax.broadcasted_iota(jnp.int32, (round_up(chips, 16), per_chip), 0) == owner
    rank = jnp.dot(
        one_hot(marks), earlier_in_chip(per_chip, per_chip), preferred_element_type=jnp.float32
    )
    rank = jnp.sum(jnp.where(marks, rank, 0.0), axis=0, keepdims=True).astype(jnp.int32)
    code = owner * capacity + rank
    pick_ref[...] = one_hot(lax.broadcasted_iota(jnp.int32, pick_ref.shape, 0) == code)


def route_tiles(slots, own, other, chips, per_chip, capacity):
    components, lags = own.shape[1:]
    pick = jax.ShapeDtypeStruct((chips * capacity, per_chip), jnp.bfloat16)
    shape = jax.ShapeDtypeStruct((components * capacity, lags), jnp.bfloat16)
    return pl.pallas_call(
        functools.partial(route_kernel, chips, per_chip, capacity),
        out_shape=(pick,) + (shape,) * chips,
        compiler_params=params(),
        name="route_tiles",
    )(slots, own, other)


def pass_on(value, *others):
    def kernel(*refs):
        pass

    return pl.pallas_call(
        kernel,
        in_specs=[pl.BlockSpec(memory_space=pl.ANY)] * (1 + len(others)),
        out_specs=pl.BlockSpec(memory_space=pl.ANY),
        out_shape=jax.ShapeDtypeStruct(value.shape, value.dtype),
        input_output_aliases={0: 0},
        compiler_params=params(),
        name="pass_on",
    )(value, *others)


def shift_kernel(pick_ref, *refs):
    pieces, out_ref = refs[:-1], refs[-1]
    capacity, count = pick_ref.shape[0] // len(pieces), pick_ref.shape[1]
    components = pieces[0].shape[0] // capacity
    lags = pieces[0].shape[1]
    span = out_ref.shape[1] // components
    tail = jnp.zeros((BLOCK, span - lags), jnp.float32)
    for comp in range(components):
        arrived = jnp.concatenate(
            [piece[comp * capacity : (comp + 1) * capacity, :] for piece in pieces], axis=0
        )
        tiles = lax.dot_general(
            pick_ref[...], arrived, (((0,), (0,)), ((), ())), preferred_element_type=jnp.float32
        )
        for patch in range(count):
            row = jnp.broadcast_to(tiles[patch : patch + 1], (BLOCK, lags))
            wide = jnp.concatenate([row, tail], axis=1)
            moved = pltpu.roll(wide, 0, 1, stride=1, stride_axis=0)
            out_ref[
                patch * BLOCK : (patch + 1) * BLOCK, comp * span : (comp + 1) * span
            ] = moved.astype(jnp.bfloat16)


def shift_tiles(pick, pieces, components):
    lags = pieces[0].shape[1]
    span = round_up(lags + BLOCK, LANES)
    shape = jax.ShapeDtypeStruct((pick.shape[1] * BLOCK, components * span), jnp.bfloat16)
    return pl.pallas_call(
        shift_kernel, out_shape=shape, compiler_params=params(), name="shift_tiles"
    )(pick, *pieces)


def convolve_blocks(shifted_ref, slip_refs, stack_ref, product_ref, out_ref, rows):
    length = out_ref.shape[2]
    components = out_ref.shape[1] // rows
    height = slip_refs[0].shape[0]
    width = shifted_ref.shape[1] // components
    per_reg = LANES // BLOCK
    blocks = height // rows
    for step, ref in enumerate(slip_refs):
        stack_ref[step * height : (step + 1) * height] = ref[...]
    for comp in range(components):
        product_ref[...] = jnp.dot(
            stack_ref[...],
            shifted_ref[:, comp * width : (comp + 1) * width],
            preferred_element_type=jnp.float32,
        )
        for step in range(len(slip_refs)):
            total = None
            for inner in range(per_reg):
                part = None
                for outer in range(inner, blocks, per_reg):
                    lead = outer // per_reg * LANES
                    start = step * height + outer * rows
                    block = product_ref[start : start + rows, :]
                    pieces = [jnp.zeros((rows, lead), jnp.float32)] if lead else []
                    pieces.append(block[:, : min(width, length - lead)])
                    if length > lead + width:
                        pieces.append(jnp.zeros((rows, length - lead - width), jnp.float32))
                    block = jnp.concatenate(pieces, axis=1) if len(pieces) > 1 else pieces[0]
                    part = block if part is None else part + block
                if inner:
                    part = pltpu.roll(part, inner * BLOCK, 1)
                total = part if total is None else total + part
            out_ref[step, comp * rows : (comp + 1) * rows, :] = total


def convolve_first_kernel(rows, shifted_ref, *refs):
    slip_refs, (out_ref, stack_ref, product_ref) = refs[:-3], refs[-3:]
    convolve_blocks(shifted_ref, slip_refs, stack_ref, product_ref, out_ref, rows)


def convolve_scratch(shifted, count, height, depth, components):
    return [
        pltpu.VMEM((count * height, depth), jnp.bfloat16),
        pltpu.VMEM((count * height, shifted.shape[1] // components), jnp.float32),
    ]


def convolve_first(shifted, slips, rows, components, length):
    shape = jax.ShapeDtypeStruct((len(slips), components * rows, length), jnp.float32)
    return pl.pallas_call(
        functools.partial(convolve_first_kernel, rows),
        out_shape=shape,
        scratch_shapes=convolve_scratch(shifted, len(slips), *slips[0].shape, components),
        compiler_params=params(),
        name="convolve_first",
    )(shifted, *slips)


def unit_of(exponent):
    return jnp.exp2(exponent.astype(jnp.float32) * (1.0 / STEPS)) * (1.0 / LARGEST)


def convolve_last_kernel(rows, shifted_ref, slip_ref, first_ref, *refs):
    own_ref, sent_ref, stack_ref, product_ref, last_ref = refs
    convolve_blocks(shifted_ref, [slip_ref], stack_ref, product_ref, last_ref, rows)
    count = first_ref.shape[0]
    length = first_ref.shape[2]
    site, chip = lax.axis_index("site"), lax.axis_index("patch") // 2
    last = last_ref[0]
    for step in range(sent_ref.shape[0]):
        target = step ^ chip
        source = target ^ site
        total = jnp.where(source == count, last, first_ref[jnp.minimum(source, count - 1)])
        if step == 0:
            own_ref[...] = total
            continue
        peak = jnp.maximum(jnp.max(jnp.abs(total), axis=1, keepdims=True), SMALLEST)
        exponent = jnp.ceil(jnp.log2(peak) * STEPS).astype(jnp.int32)
        scaled = jnp.round(total * (1.0 / unit_of(exponent)))
        whole = jnp.clip(scaled, -LARGEST, LARGEST).astype(jnp.int32)
        sent_ref[target, :, :length] = whole.astype(jnp.int16)
        sent_ref[target, :, length:] = jnp.broadcast_to(
            exponent, (exponent.shape[0], sent_ref.shape[2] - length)
        ).astype(jnp.int16)


def convolve_last(shifted, slip, first, rows, components):
    count, height, length = first.shape
    own = jax.ShapeDtypeStruct((height, length), jnp.float32)
    sent = jax.ShapeDtypeStruct((count + 1, height, round_up(length, LANES) + LANES), jnp.int16)
    return pl.pallas_call(
        functools.partial(convolve_last_kernel, rows),
        out_shape=(own, sent),
        scratch_shapes=convolve_scratch(shifted, 1, *slip.shape, components)
        + [pltpu.VMEM((1, height, length), jnp.float32)],
        compiler_params=params(),
        name="convolve_last",
    )(shifted, slip, first)


def add_kernel(own_ref, sent_ref, out_ref):
    part, components, length = out_ref.shape
    rows = own_ref.shape[0] // components
    chip = lax.axis_index("patch") // 2
    total = own_ref[...]
    for step in range(1, sent_ref.shape[0]):
        sent = sent_ref[step ^ chip].astype(jnp.int32)
        total = total + sent[:, :length].astype(jnp.float32) * unit_of(sent[:, length:][:, :1])
    for comp in range(components):
        out_ref[:, comp, :] = total[comp * rows : comp * rows + part]


def add_up(own, sent, part, components):
    return pl.pallas_call(
        add_kernel,
        out_shape=jax.ShapeDtypeStruct((part, components, own.shape[1]), jnp.float32),
        compiler_params=params(),
        name="add_up",
    )(own, sent)


def local(slip_rates, green_tiles, patch_slot):
    devices = lax.axis_size("patch")
    sites = lax.axis_size("site")
    chips = devices // 2
    patches, held, samples = slip_rates.shape
    components, lags = green_tiles.shape[2:]
    length = samples + lags
    part = held // 2
    rows = round_up(part, ROWS)
    assert chips == sites and sites & (sites - 1) == 0

    def over_patch(value, offset):
        return lax.ppermute(value, "patch", [(i, i ^ offset) for i in range(devices)])

    slips = slip_rates
    if rows > part:
        slips = slips.reshape(patches, 2, part, samples)
        slips = jnp.pad(slips, ((0, 0), (0, 0), (0, rows - part), (0, 0)))
        slips = slips.reshape(patches, 2 * rows, samples)
    greens = green_tiles[0]
    other, other_tiles = over_patch(slips, 1), over_patch(greens, 1)
    block, slots, greens = arrange_own(slips, patch_slot.reshape(1, -1), greens)
    block = arrange_other(other, other_tiles, block)

    share = 2 * max(1, patches // devices)
    capacity = round_up(4 * share, 16)
    pick, *pieces = route_tiles(slots, greens, other_tiles, chips, 2 * patches, capacity)
    pieces = [pieces[0]] + [over_patch(pieces[step], 2 * step) for step in range(1, chips)]

    blocks = {0: block}
    for step in [2**i for i in range(sites.bit_length())] + list(range(sites)):
        if 0 < step < sites and step not in blocks:
            low = step & -step
            blocks[step] = lax.ppermute(
                blocks[step - low], "site", [(i, i ^ low) for i in range(sites)]
            )
            if step == sites // 2:
                blocks[step] = pass_on(blocks[step], *pieces[1:])
    shifted = shift_tiles(pick, pieces, components)

    slips = [blocks[step] for step in range(sites)]
    first = convolve_first(shifted, slips[:-1], rows, components, length)
    own, sent = convolve_last(shifted, slips[-1], first, rows, components)
    groups = [[2 * chip + core for chip in range(chips)] for core in range(2)]
    sent = lax.all_to_all(sent, "patch", 0, 0, axis_index_groups=groups, tiled=True)
    return add_up(own, sent, part, components)[None]


def solution(mesh):
    in_specs = (P("patch", "site", None), P("site", "patch", None, None), P())
    out_specs = P("site", "patch", None, None)
    return jax.shard_map(local, mesh=mesh, in_specs=in_specs, out_specs=out_specs, check_vma=False)
```

```python
import functools

import jax
import jax.numpy as jnp
from jax import lax
from jax.experimental import pallas as pl
from jax.experimental.pallas import tpu as pltpu
from jax.sharding import PartitionSpec as P

BLOCK = 16
LANES = 128
ROWS = 8
VMEM_LIMIT = 32 * 1024 * 1024
LARGEST = 32767.0
STEPS = 16
SMALLEST = 1e-30


def round_up(value, unit):
    return -(-value // unit) * unit


def params(limit=VMEM_LIMIT):
    return pltpu.CompilerParams(vmem_limit_bytes=limit)


def arrange_half(slip_ref, out_ref, core, owner):
    patches, both, samples = slip_ref.shape
    rows = both // 2
    per_reg = LANES // BLOCK
    blocks = samples // BLOCK
    depth = patches * BLOCK
    lane_block = lax.broadcasted_iota(jnp.int32, (rows, LANES), 1) // BLOCK
    for group in range(depth // LANES):
        done = {}
        for place in range(per_reg):
            full = slip_ref[group * per_reg + place].astype(jnp.float32)
            source = jnp.where(core == 0, full[:rows], full[rows:])
            for reg in range(samples // LANES):
                piece = source[:, reg * LANES : (reg + 1) * LANES]
                for inner in range(per_reg):
                    turn = (place - inner) % per_reg * BLOCK
                    moved = pltpu.roll(piece, turn, 1) if turn else piece
                    block = reg * per_reg + inner
                    if block in done:
                        moved = jnp.where(lane_block == place, moved, done[block])
                    done[block] = moved
        lanes = pl.ds(pl.multiple_of(owner * depth + group * LANES, LANES), LANES)
        for block in range(0, blocks, 2):
            pair = jnp.concatenate([done[block], done[block + 1]], axis=0)
            out_ref[block * rows : (block + 2) * rows, lanes] = pair.astype(jnp.bfloat16)


def arrange_own_kernel(
    slip_hbm, slots_hbm, green_hbm, out_ref, slots_ref, green_ref, slip_ref, sems
):
    fetch_slips = pltpu.make_async_copy(slip_hbm, slip_ref, sems.at[0])
    fetch_slots = pltpu.make_async_copy(slots_hbm, slots_ref, sems.at[1])
    fetch_greens = pltpu.make_async_copy(green_hbm, green_ref, sems.at[2])
    fetch_slips.start()
    fetch_slots.start()
    fetch_greens.start()
    fetch_slips.wait()
    core = lax.rem(lax.axis_index("patch"), 2)
    arrange_half(slip_ref, out_ref, core, core)
    fetch_slots.wait()
    fetch_greens.wait()


def arrange_other_kernel(slip_ref, green_ref, block_ref, out_ref):
    core = lax.rem(lax.axis_index("patch"), 2)
    arrange_half(slip_ref, out_ref, core, 1 - core)


def in_hbm(*values):
    return [pltpu.with_memory_space_constraint(value, pltpu.HBM) for value in values]


def arrange_own(slips, slots, greens):
    patches, both, samples = slips.shape
    block = jax.ShapeDtypeStruct(
        (samples // BLOCK * both // 2, 2 * patches * BLOCK), jnp.bfloat16
    )
    return pl.pallas_call(
        arrange_own_kernel,
        in_specs=[pl.BlockSpec(memory_space=pltpu.HBM)] * 3,
        out_shape=(
            block,
            jax.ShapeDtypeStruct(slots.shape, slots.dtype),
            jax.ShapeDtypeStruct(greens.shape, greens.dtype),
        ),
        scratch_shapes=[
            pltpu.VMEM(slips.shape, slips.dtype),
            pltpu.SemaphoreType.DMA((3,)),
        ],
        compiler_params=params(),
        name="arrange_own",
    )(*in_hbm(slips, slots, greens))


def arrange_other(slips, greens, block):
    return pl.pallas_call(
        arrange_other_kernel,
        in_specs=[
            pl.BlockSpec(memory_space=pltpu.VMEM),
            pl.BlockSpec(memory_space=pl.ANY),
            pl.BlockSpec(memory_space=pltpu.VMEM),
        ],
        out_shape=jax.ShapeDtypeStruct(block.shape, block.dtype),
        input_output_aliases={2: 0},
        compiler_params=params(),
        name="arrange_other",
    )(slips, greens, block)


def earlier_in_chip(count, per_chip):
    q = lax.broadcasted_iota(jnp.int32, (count, count), 0)
    p = lax.broadcasted_iota(jnp.int32, (count, count), 1)
    return ((q < p) & (q // per_chip == p // per_chip)).astype(jnp.float32).astype(jnp.bfloat16)


def one_hot(condition):
    return condition.astype(jnp.float32).astype(jnp.bfloat16)


def route_kernel(chips, per_chip, capacity, slots_ref, own_ref, other_ref, pick_ref, *out_refs):
    width, components, lags = own_ref.shape
    half = capacity // 2
    count = slots_ref.shape[1]
    own = lax.axis_index("patch")
    chip, core = own // 2, lax.rem(own, 2)
    slots = slots_ref[...]
    owner = slots // width
    mine = owner // 2 == chip
    place = slots % width + jnp.where(owner % 2 == core, 0, width)
    marks = jnp.broadcast_to(one_hot(mine), (16, count))
    rank = jnp.dot(marks, earlier_in_chip(count, per_chip), preferred_element_type=jnp.float32)
    rank = rank[:1].astype(jnp.int32)
    target = (lax.broadcasted_iota(jnp.int32, (1, count), 1) // per_chip) ^ chip
    code = jnp.where(mine, target * capacity + rank, -1)
    code_pick = one_hot(lax.broadcasted_iota(jnp.int32, (chips * capacity, count), 0) == code)
    slot_pick = one_hot(lax.broadcasted_iota(jnp.int32, (2 * width, count), 0) == place)
    pick = lax.dot_general(
        code_pick, slot_pick, (((1,), (1,)), ((), ())), preferred_element_type=jnp.float32
    ).astype(jnp.bfloat16)
    tiles = jnp.concatenate([own_ref[...], other_ref[...]], axis=0).astype(jnp.float32)
    by_comp = []
    for comp in range(components):
        both = tiles[:, comp, :].astype(jnp.bfloat16)
        chosen = jnp.dot(pick, both, preferred_element_type=jnp.float32)
        chosen = [chosen[step * capacity : (step + 1) * capacity] for step in range(chips)]
        last = chosen[-1]
        sent = [chosen[0]]
        for step in range(1, chips - 1, 2):
            sent.append(jnp.where(core == 0, chosen[step], chosen[step + 1]))
        sent.append(jnp.where(core == 0, last[:half], last[half:]))
        by_comp.append(sent)
    for values, out_ref in zip(zip(*by_comp), out_refs):
        out_ref[...] = jnp.concatenate(values, axis=0).astype(jnp.bfloat16)
    here = pltpu.roll(slots, lax.rem(count - chip * per_chip, count), 1)[:, :per_chip]
    owner = (here // (2 * width)) ^ chip
    marks = lax.broadcasted_iota(jnp.int32, (round_up(chips, 16), per_chip), 0) == owner
    rank = jnp.dot(
        one_hot(marks), earlier_in_chip(per_chip, per_chip), preferred_element_type=jnp.float32
    )
    rank = jnp.sum(jnp.where(marks, rank, 0.0), axis=0, keepdims=True).astype(jnp.int32)
    from_other = jnp.where(owner == chips - 1, rank // half, 1 - owner % 2) != core
    base = (owner - jnp.where(owner == chips - 1, 0, 1 - owner % 2)) * capacity
    code = base + jnp.where(
        owner == chips - 1,
        jnp.where(from_other, half, 0) + rank % half,
        jnp.where(from_other, capacity, 0) + rank,
    )
    code = jnp.where(owner == 0, rank, code)
    pick_ref[...] = one_hot(lax.broadcasted_iota(jnp.int32, pick_ref.shape, 0) == code)


def route_tiles(slots, own, other, chips, per_chip, capacity):
    components, lags = own.shape[1:]
    pick = jax.ShapeDtypeStruct((chips * capacity, per_chip), jnp.bfloat16)
    shape = jax.ShapeDtypeStruct((components * capacity, lags), jnp.bfloat16)
    part = jax.ShapeDtypeStruct((components * capacity // 2, lags), jnp.bfloat16)
    return pl.pallas_call(
        functools.partial(route_kernel, chips, per_chip, capacity),
        out_shape=(pick,) + (shape,) * (chips // 2) + (part,),
        compiler_params=params(),
        name="route_tiles",
    )(slots, own, other)


def pass_on(value, *others):
    def kernel(*refs):
        pass

    return pl.pallas_call(
        kernel,
        in_specs=[pl.BlockSpec(memory_space=pl.ANY)] * (1 + len(others)),
        out_specs=pl.BlockSpec(memory_space=pl.ANY),
        out_shape=jax.ShapeDtypeStruct(value.shape, value.dtype),
        input_output_aliases={0: 0},
        compiler_params=params(),
        name="pass_on",
    )(value, *others)


def shift_kernel(pick_ref, *refs):
    pieces, out_ref = refs[:-1], refs[-1]
    count = pick_ref.shape[1]
    components = sum(piece.shape[0] for piece in pieces) // pick_ref.shape[0]
    lags = pieces[0].shape[1]
    span = out_ref.shape[1] // components
    tail = jnp.zeros((BLOCK, span - lags), jnp.float32)
    for comp in range(components):
        arrived = []
        for piece in pieces:
            size = piece.shape[0] // components
            arrived.append(piece[...].astype(jnp.float32)[comp * size : (comp + 1) * size])
        arrived = jnp.concatenate(arrived, axis=0).astype(jnp.bfloat16)
        tiles = lax.dot_general(
            pick_ref[...], arrived, (((0,), (0,)), ((), ())), preferred_element_type=jnp.float32
        )
        for patch in range(count):
            row = jnp.broadcast_to(tiles[patch : patch + 1], (BLOCK, lags))
            wide = jnp.concatenate([row, tail], axis=1)
            moved = pltpu.roll(wide, 0, 1, stride=1, stride_axis=0)
            out_ref[
                patch * BLOCK : (patch + 1) * BLOCK, comp * span : (comp + 1) * span
            ] = moved.astype(jnp.bfloat16)


def shift_tiles(pick, pieces, components):
    lags = pieces[0].shape[1]
    span = round_up(lags + BLOCK, LANES)
    shape = jax.ShapeDtypeStruct((pick.shape[1] * BLOCK, components * span), jnp.bfloat16)
    return pl.pallas_call(
        shift_kernel, out_shape=shape, compiler_params=params(), name="shift_tiles"
    )(pick, *pieces)


def convolve_blocks(shifted_ref, slip_refs, stack_ref, product_ref, out_ref, rows):
    length = out_ref.shape[2]
    components = out_ref.shape[1] // rows
    height = slip_refs[0].shape[0]
    width = shifted_ref.shape[1] // components
    per_reg = LANES // BLOCK
    blocks = height // rows
    for step, ref in enumerate(slip_refs):
        stack_ref[step * height : (step + 1) * height] = ref[...]
    for comp in range(components):
        product_ref[...] = jnp.dot(
            stack_ref[...],
            shifted_ref[:, comp * width : (comp + 1) * width],
            preferred_element_type=jnp.float32,
        )
        for step in range(len(slip_refs)):
            total = None
            for inner in range(per_reg):
                part = None
                for outer in range(inner, blocks, per_reg):
                    lead = outer // per_reg * LANES
                    start = step * height + outer * rows
                    block = product_ref[start : start + rows, :]
                    pieces = [jnp.zeros((rows, lead), jnp.float32)] if lead else []
                    pieces.append(block[:, : min(width, length - lead)])
                    if length > lead + width:
                        pieces.append(jnp.zeros((rows, length - lead - width), jnp.float32))
                    block = jnp.concatenate(pieces, axis=1) if len(pieces) > 1 else pieces[0]
                    part = block if part is None else part + block
                if inner:
                    part = pltpu.roll(part, inner * BLOCK, 1)
                total = part if total is None else total + part
            out_ref[step, comp * rows : (comp + 1) * rows, :] = total


def convolve_first_kernel(rows, shifted_ref, *refs):
    slip_refs, (out_ref, stack_ref, product_ref) = refs[:-3], refs[-3:]
    convolve_blocks(shifted_ref, slip_refs, stack_ref, product_ref, out_ref, rows)


def convolve_scratch(shifted, count, height, depth, components):
    return [
        pltpu.VMEM((count * height, depth), jnp.bfloat16),
        pltpu.VMEM((count * height, shifted.shape[1] // components), jnp.float32),
    ]


def convolve_first(shifted, slips, rows, components, length):
    shape = jax.ShapeDtypeStruct((len(slips), components * rows, length), jnp.float32)
    return pl.pallas_call(
        functools.partial(convolve_first_kernel, rows),
        out_shape=shape,
        scratch_shapes=convolve_scratch(shifted, len(slips), *slips[0].shape, components),
        compiler_params=params(),
        name="convolve_first",
    )(shifted, *slips)


def unit_of(exponent):
    return jnp.exp2(exponent.astype(jnp.float32) * (1.0 / STEPS)) * (1.0 / LARGEST)


def convolve_last_kernel(rows, shifted_ref, slip_ref, first_ref, *refs):
    out_refs, (stack_ref, product_ref, last_ref) = refs[:-3], refs[-3:]
    convolve_blocks(shifted_ref, [slip_ref], stack_ref, product_ref, last_ref, rows)
    count = first_ref.shape[0]
    length = first_ref.shape[2]
    turn = lax.axis_index("site") ^ (lax.axis_index("patch") // 2)
    last = last_ref[0]
    for step, ref in enumerate(out_refs):
        source = step ^ turn
        total = jnp.where(source == count, last, first_ref[jnp.minimum(source, count - 1)])
        if step == 0:
            ref[...] = total
            continue
        peak = jnp.maximum(jnp.max(jnp.abs(total), axis=1, keepdims=True), SMALLEST)
        exponent = jnp.ceil(jnp.log2(peak) * STEPS).astype(jnp.int32)
        scaled = jnp.round(total * (1.0 / unit_of(exponent)))
        whole = jnp.clip(scaled, -LARGEST, LARGEST).astype(jnp.int32)
        ref[:, :length] = whole.astype(jnp.int16)
        ref[:, length:] = jnp.broadcast_to(
            exponent, (exponent.shape[0], ref.shape[1] - length)
        ).astype(jnp.int16)


def convolve_last(shifted, slip, first, rows, components):
    count, height, length = first.shape
    own = jax.ShapeDtypeStruct((height, length), jnp.float32)
    sent = jax.ShapeDtypeStruct((height, round_up(length, LANES) + LANES), jnp.int16)
    return pl.pallas_call(
        functools.partial(convolve_last_kernel, rows),
        out_shape=(own,) + (sent,) * count,
        scratch_shapes=convolve_scratch(shifted, 1, *slip.shape, components)
        + [pltpu.VMEM((1, height, length), jnp.float32)],
        compiler_params=params(),
        name="convolve_last",
    )(shifted, slip, first)


def add_kernel(own_ref, *refs):
    sent_refs, out_ref = refs[:-1], refs[-1]
    part, components, length = out_ref.shape
    rows = own_ref.shape[0] // components
    total = own_ref[...]
    for ref in sent_refs:
        unit = unit_of(ref[:, length:].astype(jnp.int32)[:, :1])
        total = total + ref[:, :length].astype(jnp.int32).astype(jnp.float32) * unit
    for comp in range(components):
        out_ref[:, comp, :] = total[comp * rows : comp * rows + part]


def add_up(own, sent, part, components):
    return pl.pallas_call(
        add_kernel,
        out_shape=jax.ShapeDtypeStruct((part, components, own.shape[1]), jnp.float32),
        compiler_params=params(),
        name="add_up",
    )(own, *sent)


def local(slip_rates, green_tiles, patch_slot):
    devices = lax.axis_size("patch")
    sites = lax.axis_size("site")
    chips = devices // 2
    patches, held, samples = slip_rates.shape
    components, lags = green_tiles.shape[2:]
    length = samples + lags
    part = held // 2
    rows = round_up(part, ROWS)
    assert chips == sites and sites & (sites - 1) == 0

    def over_patch(value, offset):
        return lax.ppermute(value, "patch", [(i, i ^ offset) for i in range(devices)])

    slips = slip_rates
    if rows > part:
        slips = slips.reshape(patches, 2, part, samples)
        slips = jnp.pad(slips, ((0, 0), (0, 0), (0, rows - part), (0, 0)))
        slips = slips.reshape(patches, 2 * rows, samples)
    greens = green_tiles[0]
    other, other_tiles = over_patch(slips, 1), over_patch(greens, 1)
    block, slots, greens = arrange_own(slips, patch_slot.reshape(1, -1), greens)
    block = arrange_other(other, other_tiles, block)

    share = 2 * max(1, patches // devices)
    capacity = round_up(4 * share, 16)
    pick, *pieces = route_tiles(slots, greens, other_tiles, chips, 2 * patches, capacity)
    arrived = []
    for index, piece in enumerate(pieces[1:]):
        hops = [(2 * index + 1, 2 * index + 2), (chips - 1, chips - 1)][index == len(pieces) - 2]
        arrived.append(
            lax.ppermute(piece, "patch", [(i, i ^ (2 * hops[i % 2])) for i in range(devices)])
        )

    blocks = {0: block}
    for step in [2**i for i in range(sites.bit_length())] + list(range(sites)):
        if 0 < step < sites and step not in blocks:
            low = step & -step
            blocks[step] = lax.ppermute(
                blocks[step - low], "site", [(i, i ^ low) for i in range(sites)]
            )
            if step == sites // 2:
                blocks[step] = pass_on(blocks[step], *arrived)
    pieces = pieces[:1]
    for piece in arrived:
        pieces += [piece, over_patch(piece, 1)]
    shifted = shift_tiles(pick, pieces, components)

    slips = [blocks[step] for step in range(sites)]
    first = convolve_first(shifted, slips[:-1], rows, components, length)
    sums = convolve_last(shifted, slips[-1], first, rows, components)
    sent = [over_patch(sums[step], 2 * step) for step in range(1, chips)]
    return add_up(sums[0], sent, part, components)[None]


def solution(mesh):
    in_specs = (P("patch", "site", None), P("site", "patch", None, None), P())
    out_specs = P("site", "patch", None, None)
    return jax.shard_map(local, mesh=mesh, in_specs=in_specs, out_specs=out_specs, check_vma=False)
```

```python
import functools

import jax
import jax.numpy as jnp
from jax import lax
from jax.experimental import pallas as pl
from jax.experimental.pallas import tpu as pltpu
from jax.sharding import PartitionSpec as P

BLOCK = 16
LANES = 128
ROWS = 8
VMEM_LIMIT = 32 * 1024 * 1024
LARGEST = 32767.0
STEPS = 16
SMALLEST = 1e-30


def round_up(value, unit):
    return -(-value // unit) * unit


def params(limit=VMEM_LIMIT):
    return pltpu.CompilerParams(vmem_limit_bytes=limit)


def arrange(slip_ref, keep_ref, give_ref):
    patches, both, samples = slip_ref.shape
    rows = both // 2
    per_reg = LANES // BLOCK
    blocks = samples // BLOCK
    core = lax.rem(lax.axis_index("patch"), 2)
    lane_block = lax.broadcasted_iota(jnp.int32, (rows, LANES), 1) // BLOCK
    for group in range(patches * BLOCK // LANES):
        done = {}
        for place in range(per_reg):
            full = slip_ref[group * per_reg + place].astype(jnp.float32)
            low, high = full[:rows], full[rows:]
            halves = (jnp.where(core == 0, low, high), jnp.where(core == 0, high, low))
            for half, source in enumerate(halves):
                for reg in range(samples // LANES):
                    piece = source[:, reg * LANES : (reg + 1) * LANES]
                    for inner in range(per_reg):
                        turn = (place - inner) % per_reg * BLOCK
                        moved = pltpu.roll(piece, turn, 1) if turn else piece
                        key = half, reg * per_reg + inner
                        if key in done:
                            moved = jnp.where(lane_block == place, moved, done[key])
                        done[key] = moved
        lanes = slice(group * LANES, (group + 1) * LANES)
        for half, ref in enumerate((keep_ref, give_ref)):
            for block in range(0, blocks, 2):
                pair = jnp.concatenate([done[half, block], done[half, block + 1]], axis=0)
                ref[block * rows : (block + 2) * rows, lanes] = pair.astype(jnp.bfloat16)


def arrange_own_kernel(
    slip_hbm, slots_hbm, green_hbm, keep_ref, give_ref, slots_ref, green_ref, slip_ref, sems
):
    fetch_slips = pltpu.make_async_copy(slip_hbm, slip_ref, sems.at[0])
    fetch_slots = pltpu.make_async_copy(slots_hbm, slots_ref, sems.at[1])
    fetch_greens = pltpu.make_async_copy(green_hbm, green_ref, sems.at[2])
    fetch_slips.start()
    fetch_slots.start()
    fetch_greens.start()
    fetch_slips.wait()
    arrange(slip_ref, keep_ref, give_ref)
    fetch_slots.wait()
    fetch_greens.wait()


def in_hbm(*values):
    return [pltpu.with_memory_space_constraint(value, pltpu.HBM) for value in values]


def half_shape(slips):
    patches, both, samples = slips.shape
    return jax.ShapeDtypeStruct((samples // BLOCK * both // 2, patches * BLOCK), jnp.bfloat16)


def arrange_own(slips, slots, greens):
    half = half_shape(slips)
    return pl.pallas_call(
        arrange_own_kernel,
        in_specs=[pl.BlockSpec(memory_space=pltpu.HBM)] * 3,
        out_shape=(
            half,
            half,
            jax.ShapeDtypeStruct(slots.shape, slots.dtype),
            jax.ShapeDtypeStruct(greens.shape, greens.dtype),
        ),
        scratch_shapes=[
            pltpu.VMEM(slips.shape, slips.dtype),
            pltpu.SemaphoreType.DMA((3,)),
        ],
        compiler_params=params(),
        name="arrange_own",
    )(*in_hbm(slips, slots, greens))


def arrange_far(slips, *others):
    def kernel(slip_ref, *refs):
        arrange(slip_ref, *refs[-2:])

    half = half_shape(slips)
    return pl.pallas_call(
        kernel,
        in_specs=[pl.BlockSpec(memory_space=pltpu.VMEM)]
        + [pl.BlockSpec(memory_space=pl.ANY)] * len(others),
        out_shape=(half, half),
        compiler_params=params(),
        name="arrange_far",
    )(slips, *others)


def earlier_in_chip(count, per_chip):
    q = lax.broadcasted_iota(jnp.int32, (count, count), 0)
    p = lax.broadcasted_iota(jnp.int32, (count, count), 1)
    return ((q < p) & (q // per_chip == p // per_chip)).astype(jnp.float32).astype(jnp.bfloat16)


def one_hot(condition):
    return condition.astype(jnp.float32).astype(jnp.bfloat16)


def route_kernel(chips, per_chip, capacity, slots_ref, own_ref, other_ref, pick_ref, *out_refs):
    width, components, lags = own_ref.shape
    half = capacity // 2
    count = slots_ref.shape[1]
    own = lax.axis_index("patch")
    chip, core = own // 2, lax.rem(own, 2)
    slots = slots_ref[...]
    owner = slots // width
    mine = owner // 2 == chip
    place = slots % width + jnp.where(owner % 2 == core, 0, width)
    marks = jnp.broadcast_to(one_hot(mine), (16, count))
    rank = jnp.dot(marks, earlier_in_chip(count, per_chip), preferred_element_type=jnp.float32)
    rank = rank[:1].astype(jnp.int32)
    target = (lax.broadcasted_iota(jnp.int32, (1, count), 1) // per_chip) ^ chip
    code = jnp.where(mine, target * capacity + rank, -1)
    code_pick = one_hot(lax.broadcasted_iota(jnp.int32, (chips * capacity, count), 0) == code)
    slot_pick = one_hot(lax.broadcasted_iota(jnp.int32, (2 * width, count), 0) == place)
    pick = lax.dot_general(
        code_pick, slot_pick, (((1,), (1,)), ((), ())), preferred_element_type=jnp.float32
    ).astype(jnp.bfloat16)
    tiles = jnp.concatenate([own_ref[...], other_ref[...]], axis=0).astype(jnp.float32)
    by_comp = []
    for comp in range(components):
        both = tiles[:, comp, :].astype(jnp.bfloat16)
        chosen = jnp.dot(pick, both, preferred_element_type=jnp.float32)
        chosen = [chosen[step * capacity : (step + 1) * capacity] for step in range(chips)]
        last = chosen[-1]
        sent = [chosen[0]]
        for step in range(1, chips - 1, 2):
            sent.append(jnp.where(core == 0, chosen[step], chosen[step + 1]))
        sent.append(jnp.where(core == 0, last[:half], last[half:]))
        by_comp.append(sent)
    for values, out_ref in zip(zip(*by_comp), out_refs):
        out_ref[...] = jnp.concatenate(values, axis=0).astype(jnp.bfloat16)
    here = pltpu.roll(slots, lax.rem(count - chip * per_chip, count), 1)[:, :per_chip]
    owner = (here // (2 * width)) ^ chip
    marks = lax.broadcasted_iota(jnp.int32, (round_up(chips, 16), per_chip), 0) == owner
    rank = jnp.dot(
        one_hot(marks), earlier_in_chip(per_chip, per_chip), preferred_element_type=jnp.float32
    )
    rank = jnp.sum(jnp.where(marks, rank, 0.0), axis=0, keepdims=True).astype(jnp.int32)
    from_other = jnp.where(owner == chips - 1, rank // half, 1 - owner % 2) != core
    base = (owner - jnp.where(owner == chips - 1, 0, 1 - owner % 2)) * capacity
    code = base + jnp.where(
        owner == chips - 1,
        jnp.where(from_other, half, 0) + rank % half,
        jnp.where(from_other, capacity, 0) + rank,
    )
    code = jnp.where(owner == 0, rank, code)
    pick_ref[...] = one_hot(lax.broadcasted_iota(jnp.int32, pick_ref.shape, 0) == code)


def route_tiles(slots, own, other, chips, per_chip, capacity):
    components, lags = own.shape[1:]
    pick = jax.ShapeDtypeStruct((chips * capacity, per_chip), jnp.bfloat16)
    shape = jax.ShapeDtypeStruct((components * capacity, lags), jnp.bfloat16)
    part = jax.ShapeDtypeStruct((components * capacity // 2, lags), jnp.bfloat16)
    return pl.pallas_call(
        functools.partial(route_kernel, chips, per_chip, capacity),
        out_shape=(pick,) + (shape,) * (chips // 2) + (part,),
        compiler_params=params(),
        name="route_tiles",
    )(slots, own, other)


def shift_kernel(pick_ref, *refs):
    pieces, out_ref = refs[:-1], refs[-1]
    count = pick_ref.shape[1]
    components = sum(piece.shape[0] for piece in pieces) // pick_ref.shape[0]
    lags = pieces[0].shape[1]
    span = out_ref.shape[1] // components
    tail = jnp.zeros((BLOCK, span - lags), jnp.float32)
    for comp in range(components):
        arrived = []
        for piece in pieces:
            size = piece.shape[0] // components
            arrived.append(piece[...].astype(jnp.float32)[comp * size : (comp + 1) * size])
        arrived = jnp.concatenate(arrived, axis=0).astype(jnp.bfloat16)
        tiles = lax.dot_general(
            pick_ref[...], arrived, (((0,), (0,)), ((), ())), preferred_element_type=jnp.float32
        )
        for patch in range(count):
            row = jnp.broadcast_to(tiles[patch : patch + 1], (BLOCK, lags))
            wide = jnp.concatenate([row, tail], axis=1)
            moved = pltpu.roll(wide, 0, 1, stride=1, stride_axis=0)
            out_ref[
                patch * BLOCK : (patch + 1) * BLOCK, comp * span : (comp + 1) * span
            ] = moved.astype(jnp.bfloat16)


def shift_tiles(pick, pieces, components):
    lags = pieces[0].shape[1]
    span = round_up(lags + BLOCK, LANES)
    shape = jax.ShapeDtypeStruct((pick.shape[1] * BLOCK, components * span), jnp.bfloat16)
    return pl.pallas_call(
        shift_kernel, out_shape=shape, compiler_params=params(), name="shift_tiles"
    )(pick, *pieces)


def convolve_blocks(shifted_ref, slip_refs, stack_ref, product_ref, out_ref, rows):
    length = out_ref.shape[2]
    components = out_ref.shape[1] // rows
    height, depth = slip_refs[0].shape
    width = shifted_ref.shape[1] // components
    per_reg = LANES // BLOCK
    blocks = height // rows
    core = lax.rem(lax.axis_index("patch"), 2)
    for index, ref in enumerate(slip_refs):
        step, other = index // 2, index % 2
        lanes = pl.ds(pl.multiple_of((core ^ other) * depth, LANES), depth)
        stack_ref[step * height : (step + 1) * height, lanes] = ref[...]
    for comp in range(components):
        product_ref[...] = jnp.dot(
            stack_ref[...],
            shifted_ref[:, comp * width : (comp + 1) * width],
            preferred_element_type=jnp.float32,
        )
        for step in range(len(slip_refs) // 2):
            total = None
            for inner in range(per_reg):
                part = None
                for outer in range(inner, blocks, per_reg):
                    lead = outer // per_reg * LANES
                    start = step * height + outer * rows
                    block = product_ref[start : start + rows, :]
                    pieces = [jnp.zeros((rows, lead), jnp.float32)] if lead else []
                    pieces.append(block[:, : min(width, length - lead)])
                    if length > lead + width:
                        pieces.append(jnp.zeros((rows, length - lead - width), jnp.float32))
                    block = jnp.concatenate(pieces, axis=1) if len(pieces) > 1 else pieces[0]
                    part = block if part is None else part + block
                if inner:
                    part = pltpu.roll(part, inner * BLOCK, 1)
                total = part if total is None else total + part
            out_ref[step, comp * rows : (comp + 1) * rows, :] = total


def convolve_first_kernel(rows, shifted_ref, *refs):
    slip_refs, (out_ref, stack_ref, product_ref) = refs[:-3], refs[-3:]
    convolve_blocks(shifted_ref, slip_refs, stack_ref, product_ref, out_ref, rows)


def convolve_scratch(shifted, count, height, depth, components):
    return [
        pltpu.VMEM((count * height, 2 * depth), jnp.bfloat16),
        pltpu.VMEM((count * height, shifted.shape[1] // components), jnp.float32),
    ]


def convolve_first(shifted, slips, rows, components, length):
    count = len(slips) // 2
    shape = jax.ShapeDtypeStruct((count, components * rows, length), jnp.float32)
    return pl.pallas_call(
        functools.partial(convolve_first_kernel, rows),
        out_shape=shape,
        scratch_shapes=convolve_scratch(shifted, count, *slips[0].shape, components),
        compiler_params=params(),
        name="convolve_first",
    )(shifted, *slips)


def unit_of(exponent):
    return jnp.exp2(exponent.astype(jnp.float32) * (1.0 / STEPS)) * (1.0 / LARGEST)


def convolve_last_kernel(rows, shifted_ref, slip_ref, other_ref, first_ref, *refs):
    out_refs, (stack_ref, product_ref, last_ref) = refs[:-3], refs[-3:]
    convolve_blocks(shifted_ref, [slip_ref, other_ref], stack_ref, product_ref, last_ref, rows)
    count = first_ref.shape[0]
    length = first_ref.shape[2]
    turn = lax.axis_index("site") ^ (lax.axis_index("patch") // 2)
    last = last_ref[0]
    for step, ref in enumerate(out_refs):
        source = step ^ turn
        total = jnp.where(source == count, last, first_ref[jnp.minimum(source, count - 1)])
        if step == 0:
            ref[...] = total
            continue
        peak = jnp.maximum(jnp.max(jnp.abs(total), axis=1, keepdims=True), SMALLEST)
        exponent = jnp.ceil(jnp.log2(peak) * STEPS).astype(jnp.int32)
        scaled = jnp.round(total * (1.0 / unit_of(exponent)))
        whole = jnp.clip(scaled, -LARGEST, LARGEST).astype(jnp.int32)
        ref[:, :length] = whole.astype(jnp.int16)
        ref[:, length:] = jnp.broadcast_to(
            exponent, (exponent.shape[0], ref.shape[1] - length)
        ).astype(jnp.int16)


def convolve_last(shifted, slips, first, rows, components):
    count, height, length = first.shape
    own = jax.ShapeDtypeStruct((height, length), jnp.float32)
    sent = jax.ShapeDtypeStruct((height, round_up(length, LANES) + LANES), jnp.int16)
    return pl.pallas_call(
        functools.partial(convolve_last_kernel, rows),
        out_shape=(own,) + (sent,) * count,
        scratch_shapes=convolve_scratch(shifted, 1, *slips[0].shape, components)
        + [pltpu.VMEM((1, height, length), jnp.float32)],
        compiler_params=params(),
        name="convolve_last",
    )(shifted, *slips, first)


def add_kernel(own_ref, *refs):
    sent_refs, out_ref = refs[:-1], refs[-1]
    part, components, length = out_ref.shape
    rows = own_ref.shape[0] // components
    total = own_ref[...]
    for ref in sent_refs:
        unit = unit_of(ref[:, length:].astype(jnp.int32)[:, :1])
        total = total + ref[:, :length].astype(jnp.int32).astype(jnp.float32) * unit
    for comp in range(components):
        out_ref[:, comp, :] = total[comp * rows : comp * rows + part]


def add_up(own, sent, part, components):
    return pl.pallas_call(
        add_kernel,
        out_shape=jax.ShapeDtypeStruct((part, components, own.shape[1]), jnp.float32),
        compiler_params=params(),
        name="add_up",
    )(own, *sent)


def local(slip_rates, green_tiles, patch_slot):
    devices = lax.axis_size("patch")
    sites = lax.axis_size("site")
    chips = devices // 2
    patches, held, samples = slip_rates.shape
    components, lags = green_tiles.shape[2:]
    length = samples + lags
    part = held // 2
    rows = round_up(part, ROWS)
    assert chips == sites and sites & (sites - 1) == 0

    def over_patch(value, offset):
        return lax.ppermute(value, "patch", [(i, i ^ offset) for i in range(devices)])

    slips = slip_rates
    if rows > part:
        slips = slips.reshape(patches, 2, part, samples)
        slips = jnp.pad(slips, ((0, 0), (0, 0), (0, rows - part), (0, 0)))
        slips = slips.reshape(patches, 2 * rows, samples)
    greens = green_tiles[0]
    other_tiles = over_patch(greens, 1)
    far = {}
    for step in [2**i for i in reversed(range(1, sites.bit_length()))] + list(range(2, sites, 2)):
        if step < sites and step not in far:
            low = step & -step
            before = slips if step == low else far[step - low]
            far[step] = lax.ppermute(before, "site", [(i, i ^ low) for i in range(sites)])
    keep, give, slots, greens = arrange_own(slips, patch_slot.reshape(1, -1), greens)

    share = 2 * max(1, patches // devices)
    capacity = round_up(4 * share, 16)
    pick, *pieces = route_tiles(slots, greens, other_tiles, chips, 2 * patches, capacity)
    arrived = []
    for index, piece in enumerate(pieces[1:]):
        hops = [(2 * index + 1, 2 * index + 2), (chips - 1, chips - 1)][index == len(pieces) - 2]
        arrived.append(
            lax.ppermute(piece, "patch", [(i, i ^ (2 * hops[i % 2])) for i in range(devices)])
        )

    blocks = {}
    next_site = [(i, i ^ 1) for i in range(sites)]
    next_both = [
        (i * devices + j, (i ^ 1) * devices + (j ^ 1)) for i in range(sites) for j in range(devices)
    ]
    for step in range(0, sites, 2):
        if step:
            keep, give = arrange_far(far[step], *arrived)
        blocks[step] = keep, over_patch(give, 1)
        blocks[step + 1] = (
            lax.ppermute(keep, "site", next_site),
            lax.ppermute(give, ("site", "patch"), next_both),
        )
    pieces = pieces[:1]
    for piece in arrived:
        pieces += [piece, over_patch(piece, 1)]
    shifted = shift_tiles(pick, pieces, components)

    slips = [part for step in range(sites) for part in blocks[step]]
    first = convolve_first(shifted, slips[:-2], rows, components, length)
    sums = convolve_last(shifted, slips[-2:], first, rows, components)
    sent = [over_patch(sums[step], 2 * step) for step in range(1, chips)]
    return add_up(sums[0], sent, part, components)[None]


def solution(mesh):
    in_specs = (P("patch", "site", None), P("site", "patch", None, None), P())
    out_specs = P("site", "patch", None, None)
    return jax.shard_map(local, mesh=mesh, in_specs=in_specs, out_specs=out_specs, check_vma=False)
```

```python
import functools

import jax
import jax.numpy as jnp
from jax import lax
from jax.experimental import pallas as pl
from jax.experimental.pallas import tpu as pltpu
from jax.sharding import PartitionSpec as P

BLOCK = 16
LANES = 128
ROWS = 8
VMEM_LIMIT = 32 * 1024 * 1024
LARGEST = 32767.0
STEPS = 16
SMALLEST = 1e-30


def round_up(value, unit):
    return -(-value // unit) * unit


def params(limit=VMEM_LIMIT):
    return pltpu.CompilerParams(vmem_limit_bytes=limit)


def arrange_half(slip_ref, out_ref, core, owner):
    patches, both, samples = slip_ref.shape
    rows = both // 2
    per_reg = LANES // BLOCK
    blocks = samples // BLOCK
    depth = patches * BLOCK
    lane_block = lax.broadcasted_iota(jnp.int32, (rows, LANES), 1) // BLOCK
    for group in range(depth // LANES):
        done = {}
        for place in range(per_reg):
            full = slip_ref[group * per_reg + place].astype(jnp.float32)
            source = jnp.where(core == 0, full[:rows], full[rows:])
            for reg in range(samples // LANES):
                piece = source[:, reg * LANES : (reg + 1) * LANES]
                for inner in range(per_reg):
                    turn = (place - inner) % per_reg * BLOCK
                    moved = pltpu.roll(piece, turn, 1) if turn else piece
                    block = reg * per_reg + inner
                    if block in done:
                        moved = jnp.where(lane_block == place, moved, done[block])
                    done[block] = moved
        lanes = pl.ds(pl.multiple_of(owner * depth + group * LANES, LANES), LANES)
        for block in range(0, blocks, 2):
            pair = jnp.concatenate([done[block], done[block + 1]], axis=0)
            out_ref[block * rows : (block + 2) * rows, lanes] = pair.astype(jnp.bfloat16)


def arrange_own_kernel(
    chips,
    per_chip,
    capacity,
    slip_hbm,
    slots_hbm,
    green_hbm,
    out_ref,
    send_ref,
    pick_ref,
    green_ref,
    slip_ref,
    slots_ref,
    sems,
):
    fetch_slips = pltpu.make_async_copy(slip_hbm, slip_ref, sems.at[0])
    fetch_slots = pltpu.make_async_copy(slots_hbm, slots_ref, sems.at[1])
    fetch_greens = pltpu.make_async_copy(green_hbm, green_ref, sems.at[2])
    fetch_slips.start()
    fetch_slots.start()
    fetch_greens.start()
    fetch_slots.wait()
    mark_tiles(chips, per_chip, capacity, green_hbm.shape[0], slots_ref, send_ref, pick_ref)
    fetch_slips.wait()
    core = lax.rem(lax.axis_index("patch"), 2)
    arrange_half(slip_ref, out_ref, core, core)
    fetch_greens.wait()


def arrange_other_kernel(slip_ref, green_ref, block_ref, out_ref):
    core = lax.rem(lax.axis_index("patch"), 2)
    arrange_half(slip_ref, out_ref, core, 1 - core)


def in_hbm(*values):
    return [pltpu.with_memory_space_constraint(value, pltpu.HBM) for value in values]


def arrange_own(slips, slots, greens, chips, per_chip, capacity):
    patches, both, samples = slips.shape
    width = greens.shape[0]
    block = jax.ShapeDtypeStruct(
        (samples // BLOCK * both // 2, 2 * patches * BLOCK), jnp.bfloat16
    )
    return pl.pallas_call(
        functools.partial(arrange_own_kernel, chips, per_chip, capacity),
        in_specs=[pl.BlockSpec(memory_space=pltpu.HBM)] * 3,
        out_shape=(
            block,
            jax.ShapeDtypeStruct((chips * capacity, 2 * width), jnp.bfloat16),
            jax.ShapeDtypeStruct((chips * capacity, per_chip), jnp.bfloat16),
            jax.ShapeDtypeStruct(greens.shape, greens.dtype),
        ),
        scratch_shapes=[
            pltpu.VMEM(slips.shape, slips.dtype),
            pltpu.VMEM(slots.shape, slots.dtype),
            pltpu.SemaphoreType.DMA((3,)),
        ],
        compiler_params=params(),
        name="arrange_own",
    )(*in_hbm(slips, slots, greens))


def arrange_other(slips, greens, block):
    return pl.pallas_call(
        arrange_other_kernel,
        in_specs=[
            pl.BlockSpec(memory_space=pltpu.VMEM),
            pl.BlockSpec(memory_space=pl.ANY),
            pl.BlockSpec(memory_space=pltpu.VMEM),
        ],
        out_shape=jax.ShapeDtypeStruct(block.shape, block.dtype),
        input_output_aliases={2: 0},
        compiler_params=params(),
        name="arrange_other",
    )(slips, greens, block)


def earlier_in_chip(count, per_chip):
    q = lax.broadcasted_iota(jnp.int32, (count, count), 0)
    p = lax.broadcasted_iota(jnp.int32, (count, count), 1)
    return ((q < p) & (q // per_chip == p // per_chip)).astype(jnp.float32).astype(jnp.bfloat16)


def one_hot(condition):
    return condition.astype(jnp.float32).astype(jnp.bfloat16)


def mark_tiles(chips, per_chip, capacity, width, slots_ref, send_ref, pick_ref):
    half = capacity // 2
    count = slots_ref.shape[1]
    own = lax.axis_index("patch")
    chip, core = own // 2, lax.rem(own, 2)
    slots = slots_ref[...]
    owner = slots // width
    mine = owner // 2 == chip
    place = slots % width + jnp.where(owner % 2 == core, 0, width)
    marks = jnp.broadcast_to(one_hot(mine), (16, count))
    rank = jnp.dot(marks, earlier_in_chip(count, per_chip), preferred_element_type=jnp.float32)
    rank = rank[:1].astype(jnp.int32)
    target = (lax.broadcasted_iota(jnp.int32, (1, count), 1) // per_chip) ^ chip
    code = jnp.where(mine, target * capacity + rank, -1)
    code_pick = one_hot(lax.broadcasted_iota(jnp.int32, (chips * capacity, count), 0) == code)
    slot_pick = one_hot(lax.broadcasted_iota(jnp.int32, (2 * width, count), 0) == place)
    send_ref[...] = lax.dot_general(
        code_pick, slot_pick, (((1,), (1,)), ((), ())), preferred_element_type=jnp.float32
    ).astype(jnp.bfloat16)
    here = pltpu.roll(slots, lax.rem(count - chip * per_chip, count), 1)[:, :per_chip]
    owner = (here // (2 * width)) ^ chip
    marks = lax.broadcasted_iota(jnp.int32, (round_up(chips, 16), per_chip), 0) == owner
    rank = jnp.dot(
        one_hot(marks), earlier_in_chip(per_chip, per_chip), preferred_element_type=jnp.float32
    )
    rank = jnp.sum(jnp.where(marks, rank, 0.0), axis=0, keepdims=True).astype(jnp.int32)
    from_other = jnp.where(owner == chips - 1, rank // half, 1 - owner % 2) != core
    base = (owner - jnp.where(owner == chips - 1, 0, 1 - owner % 2)) * capacity
    code = base + jnp.where(
        owner == chips - 1,
        jnp.where(from_other, half, 0) + rank % half,
        jnp.where(from_other, capacity, 0) + rank,
    )
    code = jnp.where(owner == 0, rank, code)
    pick_ref[...] = one_hot(lax.broadcasted_iota(jnp.int32, pick_ref.shape, 0) == code)


def route_kernel(chips, send_ref, own_ref, other_ref, *out_refs):
    capacity = send_ref.shape[0] // chips
    half = capacity // 2
    core = lax.rem(lax.axis_index("patch"), 2)
    tiles = jnp.concatenate([own_ref[...], other_ref[...]], axis=0).astype(jnp.float32)
    by_comp = []
    for comp in range(own_ref.shape[1]):
        both = tiles[:, comp, :].astype(jnp.bfloat16)
        chosen = jnp.dot(send_ref[...], both, preferred_element_type=jnp.float32)
        chosen = [chosen[step * capacity : (step + 1) * capacity] for step in range(chips)]
        last = chosen[-1]
        sent = [chosen[0]]
        for step in range(1, chips - 1, 2):
            sent.append(jnp.where(core == 0, chosen[step], chosen[step + 1]))
        sent.append(jnp.where(core == 0, last[:half], last[half:]))
        by_comp.append(sent)
    for values, out_ref in zip(zip(*by_comp), out_refs):
        out_ref[...] = jnp.concatenate(values, axis=0).astype(jnp.bfloat16)


def route_tiles(send, own, other, chips):
    components, lags = own.shape[1:]
    rows = components * send.shape[0] // chips
    shape = jax.ShapeDtypeStruct((rows, lags), jnp.bfloat16)
    part = jax.ShapeDtypeStruct((rows // 2, lags), jnp.bfloat16)
    return pl.pallas_call(
        functools.partial(route_kernel, chips),
        out_shape=(shape,) * (chips // 2) + (part,),
        compiler_params=params(),
        name="route_tiles",
    )(send, own, other)


def pass_on(value, *others):
    def kernel(*refs):
        pass

    return pl.pallas_call(
        kernel,
        in_specs=[pl.BlockSpec(memory_space=pl.ANY)] * (1 + len(others)),
        out_specs=pl.BlockSpec(memory_space=pl.ANY),
        out_shape=jax.ShapeDtypeStruct(value.shape, value.dtype),
        input_output_aliases={0: 0},
        compiler_params=params(),
        name="pass_on",
    )(value, *others)


def shift_kernel(pick_ref, *refs):
    pieces, out_ref = refs[:-1], refs[-1]
    count = pick_ref.shape[1]
    components = sum(piece.shape[0] for piece in pieces) // pick_ref.shape[0]
    lags = pieces[0].shape[1]
    span = out_ref.shape[1] // components
    tail = jnp.zeros((BLOCK, span - lags), jnp.float32)
    for comp in range(components):
        arrived = []
        for piece in pieces:
            size = piece.shape[0] // components
            arrived.append(piece[...].astype(jnp.float32)[comp * size : (comp + 1) * size])
        arrived = jnp.concatenate(arrived, axis=0).astype(jnp.bfloat16)
        tiles = lax.dot_general(
            pick_ref[...], arrived, (((0,), (0,)), ((), ())), preferred_element_type=jnp.float32
        )
        for patch in range(count):
            row = jnp.broadcast_to(tiles[patch : patch + 1], (BLOCK, lags))
            wide = jnp.concatenate([row, tail], axis=1)
            moved = pltpu.roll(wide, 0, 1, stride=1, stride_axis=0)
            out_ref[
                patch * BLOCK : (patch + 1) * BLOCK, comp * span : (comp + 1) * span
            ] = moved.astype(jnp.bfloat16)


def shift_tiles(pick, pieces, components):
    lags = pieces[0].shape[1]
    span = round_up(lags + BLOCK, LANES)
    shape = jax.ShapeDtypeStruct((pick.shape[1] * BLOCK, components * span), jnp.bfloat16)
    return pl.pallas_call(
        shift_kernel, out_shape=shape, compiler_params=params(), name="shift_tiles"
    )(pick, *pieces)


def convolve_blocks(shifted_ref, slip_refs, stack_ref, product_ref, out_ref, rows):
    length = out_ref.shape[2]
    components = out_ref.shape[1] // rows
    height = slip_refs[0].shape[0]
    width = shifted_ref.shape[1] // components
    per_reg = LANES // BLOCK
    blocks = height // rows
    for step, ref in enumerate(slip_refs):
        stack_ref[step * height : (step + 1) * height] = ref[...]
    for comp in range(components):
        product_ref[...] = jnp.dot(
            stack_ref[...],
            shifted_ref[:, comp * width : (comp + 1) * width],
            preferred_element_type=jnp.float32,
        )
        for step in range(len(slip_refs)):
            total = None
            for inner in range(per_reg):
                part = None
                for outer in range(inner, blocks, per_reg):
                    lead = outer // per_reg * LANES
                    start = step * height + outer * rows
                    block = product_ref[start : start + rows, :]
                    pieces = [jnp.zeros((rows, lead), jnp.float32)] if lead else []
                    pieces.append(block[:, : min(width, length - lead)])
                    if length > lead + width:
                        pieces.append(jnp.zeros((rows, length - lead - width), jnp.float32))
                    block = jnp.concatenate(pieces, axis=1) if len(pieces) > 1 else pieces[0]
                    part = block if part is None else part + block
                if inner:
                    part = pltpu.roll(part, inner * BLOCK, 1)
                total = part if total is None else total + part
            out_ref[step, comp * rows : (comp + 1) * rows, :] = total


def convolve_first_kernel(rows, shifted_ref, *refs):
    slip_refs, (out_ref, stack_ref, product_ref) = refs[:-3], refs[-3:]
    convolve_blocks(shifted_ref, slip_refs, stack_ref, product_ref, out_ref, rows)


def convolve_scratch(shifted, count, height, depth, components):
    return [
        pltpu.VMEM((count * height, depth), jnp.bfloat16),
        pltpu.VMEM((count * height, shifted.shape[1] // components), jnp.float32),
    ]


def convolve_first(shifted, slips, rows, components, length):
    shape = jax.ShapeDtypeStruct((len(slips), components * rows, length), jnp.float32)
    return pl.pallas_call(
        functools.partial(convolve_first_kernel, rows),
        out_shape=shape,
        scratch_shapes=convolve_scratch(shifted, len(slips), *slips[0].shape, components),
        compiler_params=params(),
        name="convolve_first",
    )(shifted, *slips)


def unit_of(exponent):
    return jnp.exp2(exponent.astype(jnp.float32) * (1.0 / STEPS)) * (1.0 / LARGEST)


def convolve_last_kernel(rows, shifted_ref, slip_ref, first_ref, *refs):
    out_refs, (stack_ref, product_ref, last_ref) = refs[:-3], refs[-3:]
    convolve_blocks(shifted_ref, [slip_ref], stack_ref, product_ref, last_ref, rows)
    count = first_ref.shape[0]
    length = first_ref.shape[2]
    turn = lax.axis_index("site") ^ (lax.axis_index("patch") // 2)
    last = last_ref[0]
    for step, ref in enumerate(out_refs):
        source = step ^ turn
        total = jnp.where(source == count, last, first_ref[jnp.minimum(source, count - 1)])
        if step == 0:
            ref[...] = total
            continue
        peak = jnp.maximum(jnp.max(jnp.abs(total), axis=1, keepdims=True), SMALLEST)
        exponent = jnp.ceil(jnp.log2(peak) * STEPS).astype(jnp.int32)
        scaled = jnp.round(total * (1.0 / unit_of(exponent)))
        whole = jnp.clip(scaled, -LARGEST, LARGEST).astype(jnp.int32)
        ref[:, :length] = whole.astype(jnp.int16)
        ref[:, length:] = jnp.broadcast_to(
            exponent, (exponent.shape[0], ref.shape[1] - length)
        ).astype(jnp.int16)


def convolve_last(shifted, slip, first, rows, components):
    count, height, length = first.shape
    own = jax.ShapeDtypeStruct((height, length), jnp.float32)
    sent = jax.ShapeDtypeStruct((height, round_up(length, LANES) + LANES), jnp.int16)
    return pl.pallas_call(
        functools.partial(convolve_last_kernel, rows),
        out_shape=(own,) + (sent,) * count,
        scratch_shapes=convolve_scratch(shifted, 1, *slip.shape, components)
        + [pltpu.VMEM((1, height, length), jnp.float32)],
        compiler_params=params(),
        name="convolve_last",
    )(shifted, slip, first)


def add_kernel(own_ref, *refs):
    sent_refs, out_ref = refs[:-1], refs[-1]
    part, components, length = out_ref.shape
    rows = own_ref.shape[0] // components
    total = own_ref[...]
    for ref in sent_refs:
        unit = unit_of(ref[:, length:].astype(jnp.int32)[:, :1])
        total = total + ref[:, :length].astype(jnp.int32).astype(jnp.float32) * unit
    for comp in range(components):
        out_ref[:, comp, :] = total[comp * rows : comp * rows + part]


def add_up(own, sent, part, components):
    return pl.pallas_call(
        add_kernel,
        out_shape=jax.ShapeDtypeStruct((part, components, own.shape[1]), jnp.float32),
        compiler_params=params(),
        name="add_up",
    )(own, *sent)


def local(slip_rates, green_tiles, patch_slot):
    devices = lax.axis_size("patch")
    sites = lax.axis_size("site")
    chips = devices // 2
    patches, held, samples = slip_rates.shape
    components, lags = green_tiles.shape[2:]
    length = samples + lags
    part = held // 2
    rows = round_up(part, ROWS)
    assert chips == sites and sites & (sites - 1) == 0

    def over_patch(value, offset):
        return lax.ppermute(value, "patch", [(i, i ^ offset) for i in range(devices)])

    slips = slip_rates
    if rows > part:
        slips = slips.reshape(patches, 2, part, samples)
        slips = jnp.pad(slips, ((0, 0), (0, 0), (0, rows - part), (0, 0)))
        slips = slips.reshape(patches, 2 * rows, samples)
    greens = green_tiles[0]
    other, other_tiles = over_patch(slips, 1), over_patch(greens, 1)
    share = 2 * max(1, patches // devices)
    capacity = round_up(4 * share, 16)
    block, send, pick, greens = arrange_own(
        slips, patch_slot.reshape(1, -1), greens, chips, 2 * patches, capacity
    )
    block = arrange_other(other, other_tiles, block)

    pieces = list(route_tiles(send, greens, other_tiles, chips))
    arrived = []
    for index, piece in enumerate(pieces[1:]):
        hops = [(2 * index + 1, 2 * index + 2), (chips - 1, chips - 1)][index == len(pieces) - 2]
        arrived.append(
            lax.ppermute(piece, "patch", [(i, i ^ (2 * hops[i % 2])) for i in range(devices)])
        )

    pieces = pieces[:1]
    for piece in arrived:
        pieces += [piece, over_patch(piece, 1)]

    blocks = {0: block}
    for step in [2**i for i in range(sites.bit_length())] + list(range(sites)):
        if 0 < step < sites and step not in blocks:
            low = step & -step
            blocks[step] = lax.ppermute(
                blocks[step - low], "site", [(i, i ^ low) for i in range(sites)]
            )
            if step == sites // 2:
                blocks[step] = pass_on(blocks[step], *pieces[1:])
    shifted = shift_tiles(pick, pieces, components)

    slips = [blocks[step] for step in range(sites)]
    first = convolve_first(shifted, slips[:-1], rows, components, length)
    sums = convolve_last(shifted, slips[-1], first, rows, components)
    order = [1, chips - 1] + list(range(2, chips - 1))
    sent = [over_patch(sums[step], 2 * step) for step in order]
    return add_up(sums[0], sent, part, components)[None]


def solution(mesh):
    in_specs = (P("patch", "site", None), P("site", "patch", None, None), P())
    out_specs = P("site", "patch", None, None)
    return jax.shard_map(local, mesh=mesh, in_specs=in_specs, out_specs=out_specs, check_vma=False)
```

```python
import functools

import jax
import jax.numpy as jnp
from jax import lax
from jax.experimental import pallas as pl
from jax.experimental.pallas import tpu as pltpu
from jax.sharding import PartitionSpec as P

BLOCK = 16
LANES = 128
ROWS = 8
VMEM_LIMIT = 32 * 1024 * 1024
LARGEST = 32767.0
STEPS = 16
SMALLEST = 1e-30


def round_up(value, unit):
    return -(-value // unit) * unit


def params(limit=VMEM_LIMIT):
    return pltpu.CompilerParams(vmem_limit_bytes=limit)


def arrange_half(slip_ref, out_ref, core, owner):
    patches, both, samples = slip_ref.shape
    rows = both // 2
    per_reg = LANES // BLOCK
    blocks = samples // BLOCK
    depth = patches * BLOCK
    lane_block = lax.broadcasted_iota(jnp.int32, (rows, LANES), 1) // BLOCK
    for group in range(depth // LANES):
        done = {}
        for place in range(per_reg):
            full = slip_ref[group * per_reg + place].astype(jnp.float32)
            source = jnp.where(core == 0, full[:rows], full[rows:])
            for reg in range(samples // LANES):
                piece = source[:, reg * LANES : (reg + 1) * LANES]
                for inner in range(per_reg):
                    turn = (place - inner) % per_reg * BLOCK
                    moved = pltpu.roll(piece, turn, 1) if turn else piece
                    block = reg * per_reg + inner
                    if block in done:
                        moved = jnp.where(lane_block == place, moved, done[block])
                    done[block] = moved
        lanes = pl.ds(pl.multiple_of(owner * depth + group * LANES, LANES), LANES)
        for block in range(0, blocks, 2):
            pair = jnp.concatenate([done[block], done[block + 1]], axis=0)
            out_ref[block * rows : (block + 2) * rows, lanes] = pair.astype(jnp.bfloat16)


def arrange_own_kernel(
    chips,
    per_chip,
    capacity,
    slip_hbm,
    slots_hbm,
    green_hbm,
    out_ref,
    send_ref,
    pick_ref,
    green_ref,
    slip_ref,
    slots_ref,
    sems,
):
    fetch_slips = pltpu.make_async_copy(slip_hbm, slip_ref, sems.at[0])
    fetch_slots = pltpu.make_async_copy(slots_hbm, slots_ref, sems.at[1])
    fetch_greens = pltpu.make_async_copy(green_hbm, green_ref, sems.at[2])
    fetch_slips.start()
    fetch_slots.start()
    fetch_greens.start()
    fetch_slots.wait()
    mark_tiles(chips, per_chip, capacity, green_hbm.shape[0], slots_ref, send_ref, pick_ref)
    fetch_slips.wait()
    core = lax.rem(lax.axis_index("patch"), 2)
    arrange_half(slip_ref, out_ref, core, core)
    fetch_greens.wait()


def arrange_other_kernel(slip_ref, green_ref, block_ref, out_ref):
    core = lax.rem(lax.axis_index("patch"), 2)
    arrange_half(slip_ref, out_ref, core, 1 - core)


def in_hbm(*values):
    return [pltpu.with_memory_space_constraint(value, pltpu.HBM) for value in values]


def arrange_own(slips, slots, greens, chips, per_chip, capacity):
    patches, both, samples = slips.shape
    width = greens.shape[0]
    block = jax.ShapeDtypeStruct(
        (samples // BLOCK * both // 2, 2 * patches * BLOCK), jnp.bfloat16
    )
    return pl.pallas_call(
        functools.partial(arrange_own_kernel, chips, per_chip, capacity),
        in_specs=[pl.BlockSpec(memory_space=pltpu.HBM)] * 3,
        out_shape=(
            block,
            jax.ShapeDtypeStruct((chips * capacity, 2 * width), jnp.bfloat16),
            jax.ShapeDtypeStruct((chips * capacity, per_chip), jnp.bfloat16),
            jax.ShapeDtypeStruct(greens.shape, greens.dtype),
        ),
        scratch_shapes=[
            pltpu.VMEM(slips.shape, slips.dtype),
            pltpu.VMEM(slots.shape, slots.dtype),
            pltpu.SemaphoreType.DMA((3,)),
        ],
        compiler_params=params(),
        name="arrange_own",
    )(*in_hbm(slips, slots, greens))


def arrange_other(slips, greens, block):
    return pl.pallas_call(
        arrange_other_kernel,
        in_specs=[
            pl.BlockSpec(memory_space=pltpu.VMEM),
            pl.BlockSpec(memory_space=pl.ANY),
            pl.BlockSpec(memory_space=pltpu.VMEM),
        ],
        out_shape=jax.ShapeDtypeStruct(block.shape, block.dtype),
        input_output_aliases={2: 0},
        compiler_params=params(),
        name="arrange_other",
    )(slips, greens, block)


def earlier_in_chip(count, per_chip):
    q = lax.broadcasted_iota(jnp.int32, (count, count), 0)
    p = lax.broadcasted_iota(jnp.int32, (count, count), 1)
    return ((q < p) & (q // per_chip == p // per_chip)).astype(jnp.float32).astype(jnp.bfloat16)


def one_hot(condition):
    return condition.astype(jnp.float32).astype(jnp.bfloat16)


def mark_tiles(chips, per_chip, capacity, width, slots_ref, send_ref, pick_ref):
    half = capacity // 2
    count = slots_ref.shape[1]
    own = lax.axis_index("patch")
    chip, core = own // 2, lax.rem(own, 2)
    slots = slots_ref[...]
    owner = slots // width
    mine = owner // 2 == chip
    place = slots % width + jnp.where(owner % 2 == core, 0, width)
    marks = jnp.broadcast_to(one_hot(mine), (16, count))
    rank = jnp.dot(marks, earlier_in_chip(count, per_chip), preferred_element_type=jnp.float32)
    rank = rank[:1].astype(jnp.int32)
    target = (lax.broadcasted_iota(jnp.int32, (1, count), 1) // per_chip) ^ chip
    code = jnp.where(mine, target * capacity + rank, -1)
    code_pick = one_hot(lax.broadcasted_iota(jnp.int32, (chips * capacity, count), 0) == code)
    slot_pick = one_hot(lax.broadcasted_iota(jnp.int32, (2 * width, count), 0) == place)
    send_ref[...] = lax.dot_general(
        code_pick, slot_pick, (((1,), (1,)), ((), ())), preferred_element_type=jnp.float32
    ).astype(jnp.bfloat16)
    here = pltpu.roll(slots, lax.rem(count - chip * per_chip, count), 1)[:, :per_chip]
    owner = (here // (2 * width)) ^ chip
    marks = lax.broadcasted_iota(jnp.int32, (round_up(chips, 16), per_chip), 0) == owner
    rank = jnp.dot(
        one_hot(marks), earlier_in_chip(per_chip, per_chip), preferred_element_type=jnp.float32
    )
    rank = jnp.sum(jnp.where(marks, rank, 0.0), axis=0, keepdims=True).astype(jnp.int32)
    from_other = jnp.where(owner == chips - 1, rank // half, 1 - owner % 2) != core
    base = (owner - jnp.where(owner == chips - 1, 0, 1 - owner % 2)) * capacity
    code = base + jnp.where(
        owner == chips - 1,
        jnp.where(from_other, half, 0) + rank % half,
        jnp.where(from_other, capacity, 0) + rank,
    )
    code = jnp.where(owner == 0, rank, code)
    pick_ref[...] = one_hot(lax.broadcasted_iota(jnp.int32, pick_ref.shape, 0) == code)


def route_kernel(chips, send_ref, own_ref, other_ref, after_ref, *out_refs):
    capacity = send_ref.shape[0] // chips
    half = capacity // 2
    core = lax.rem(lax.axis_index("patch"), 2)
    tiles = jnp.concatenate([own_ref[...], other_ref[...]], axis=0).astype(jnp.float32)
    by_comp = []
    for comp in range(own_ref.shape[1]):
        both = tiles[:, comp, :].astype(jnp.bfloat16)
        chosen = jnp.dot(send_ref[...], both, preferred_element_type=jnp.float32)
        chosen = [chosen[step * capacity : (step + 1) * capacity] for step in range(chips)]
        last = chosen[-1]
        sent = [chosen[0]]
        for step in range(1, chips - 1, 2):
            sent.append(jnp.where(core == 0, chosen[step], chosen[step + 1]))
        sent.append(jnp.where(core == 0, last[:half], last[half:]))
        by_comp.append(sent)
    for values, out_ref in zip(zip(*by_comp), out_refs):
        out_ref[...] = jnp.concatenate(values, axis=0).astype(jnp.bfloat16)


def route_tiles(send, own, other, after, chips):
    components, lags = own.shape[1:]
    rows = components * send.shape[0] // chips
    shape = jax.ShapeDtypeStruct((rows, lags), jnp.bfloat16)
    part = jax.ShapeDtypeStruct((rows // 2, lags), jnp.bfloat16)
    return pl.pallas_call(
        functools.partial(route_kernel, chips),
        in_specs=[pl.BlockSpec(memory_space=pltpu.VMEM)] * 3
        + [pl.BlockSpec(memory_space=pl.ANY)],
        out_shape=(shape,) * (chips // 2) + (part,),
        compiler_params=params(),
        name="route_tiles",
    )(send, own, other, after)


def pass_on(value, *others):
    def kernel(*refs):
        pass

    return pl.pallas_call(
        kernel,
        in_specs=[pl.BlockSpec(memory_space=pl.ANY)] * (1 + len(others)),
        out_specs=pl.BlockSpec(memory_space=pl.ANY),
        out_shape=jax.ShapeDtypeStruct(value.shape, value.dtype),
        input_output_aliases={0: 0},
        compiler_params=params(),
        name="pass_on",
    )(value, *others)


def shift_kernel(pick_ref, *refs):
    pieces, out_ref = refs[:-1], refs[-1]
    count = pick_ref.shape[1]
    components = sum(piece.shape[0] for piece in pieces) // pick_ref.shape[0]
    lags = pieces[0].shape[1]
    span = out_ref.shape[1] // components
    tail = jnp.zeros((BLOCK, span - lags), jnp.float32)
    for comp in range(components):
        arrived = []
        for piece in pieces:
            size = piece.shape[0] // components
            arrived.append(piece[...].astype(jnp.float32)[comp * size : (comp + 1) * size])
        arrived = jnp.concatenate(arrived, axis=0).astype(jnp.bfloat16)
        tiles = lax.dot_general(
            pick_ref[...], arrived, (((0,), (0,)), ((), ())), preferred_element_type=jnp.float32
        )
        for patch in range(count):
            row = jnp.broadcast_to(tiles[patch : patch + 1], (BLOCK, lags))
            wide = jnp.concatenate([row, tail], axis=1)
            moved = pltpu.roll(wide, 0, 1, stride=1, stride_axis=0)
            out_ref[
                patch * BLOCK : (patch + 1) * BLOCK, comp * span : (comp + 1) * span
            ] = moved.astype(jnp.bfloat16)


def shift_tiles(pick, pieces, components):
    lags = pieces[0].shape[1]
    span = round_up(lags + BLOCK, LANES)
    shape = jax.ShapeDtypeStruct((pick.shape[1] * BLOCK, components * span), jnp.bfloat16)
    return pl.pallas_call(
        shift_kernel, out_shape=shape, compiler_params=params(), name="shift_tiles"
    )(pick, *pieces)


def convolve_blocks(shifted_ref, slip_refs, stack_ref, product_ref, out_ref, rows):
    length = out_ref.shape[2]
    components = out_ref.shape[1] // rows
    height = slip_refs[0].shape[0]
    width = shifted_ref.shape[1] // components
    per_reg = LANES // BLOCK
    blocks = height // rows
    for step, ref in enumerate(slip_refs):
        stack_ref[step * height : (step + 1) * height] = ref[...]
    for comp in range(components):
        product_ref[...] = jnp.dot(
            stack_ref[...],
            shifted_ref[:, comp * width : (comp + 1) * width],
            preferred_element_type=jnp.float32,
        )
        for step in range(len(slip_refs)):
            total = None
            for inner in range(per_reg):
                part = None
                for outer in range(inner, blocks, per_reg):
                    lead = outer // per_reg * LANES
                    start = step * height + outer * rows
                    block = product_ref[start : start + rows, :]
                    pieces = [jnp.zeros((rows, lead), jnp.float32)] if lead else []
                    pieces.append(block[:, : min(width, length - lead)])
                    if length > lead + width:
                        pieces.append(jnp.zeros((rows, length - lead - width), jnp.float32))
                    block = jnp.concatenate(pieces, axis=1) if len(pieces) > 1 else pieces[0]
                    part = block if part is None else part + block
                if inner:
                    part = pltpu.roll(part, inner * BLOCK, 1)
                total = part if total is None else total + part
            out_ref[step, comp * rows : (comp + 1) * rows, :] = total


def convolve_first_kernel(rows, shifted_ref, *refs):
    slip_refs, (out_ref, stack_ref, product_ref) = refs[:-3], refs[-3:]
    convolve_blocks(shifted_ref, slip_refs, stack_ref, product_ref, out_ref, rows)


def convolve_scratch(shifted, count, height, depth, components):
    return [
        pltpu.VMEM((count * height, depth), jnp.bfloat16),
        pltpu.VMEM((count * height, shifted.shape[1] // components), jnp.float32),
    ]


def convolve_first(shifted, slips, rows, components, length):
    shape = jax.ShapeDtypeStruct((len(slips), components * rows, length), jnp.float32)
    return pl.pallas_call(
        functools.partial(convolve_first_kernel, rows),
        out_shape=shape,
        scratch_shapes=convolve_scratch(shifted, len(slips), *slips[0].shape, components),
        compiler_params=params(),
        name="convolve_first",
    )(shifted, *slips)


def unit_of(exponent):
    return jnp.exp2(exponent.astype(jnp.float32) * (1.0 / STEPS)) * (1.0 / LARGEST)


def convolve_last_kernel(rows, shifted_ref, slip_ref, first_ref, *refs):
    out_refs, (stack_ref, product_ref, last_ref) = refs[:-3], refs[-3:]
    convolve_blocks(shifted_ref, [slip_ref], stack_ref, product_ref, last_ref, rows)
    count = first_ref.shape[0]
    length = first_ref.shape[2]
    turn = lax.axis_index("site") ^ (lax.axis_index("patch") // 2)
    last = last_ref[0]
    for step, ref in enumerate(out_refs):
        source = step ^ turn
        total = jnp.where(source == count, last, first_ref[jnp.minimum(source, count - 1)])
        if step == 0:
            ref[...] = total
            continue
        peak = jnp.maximum(jnp.max(jnp.abs(total), axis=1, keepdims=True), SMALLEST)
        exponent = jnp.ceil(jnp.log2(peak) * STEPS).astype(jnp.int32)
        scaled = jnp.round(total * (1.0 / unit_of(exponent)))
        whole = jnp.clip(scaled, -LARGEST, LARGEST).astype(jnp.int32)
        ref[:, :length] = whole.astype(jnp.int16)
        ref[:, length:] = jnp.broadcast_to(
            exponent, (exponent.shape[0], ref.shape[1] - length)
        ).astype(jnp.int16)


def convolve_last(shifted, slip, first, rows, components):
    count, height, length = first.shape
    own = jax.ShapeDtypeStruct((height, length), jnp.float32)
    sent = jax.ShapeDtypeStruct((height, round_up(length, LANES) + LANES), jnp.int16)
    return pl.pallas_call(
        functools.partial(convolve_last_kernel, rows),
        out_shape=(own,) + (sent,) * count,
        scratch_shapes=convolve_scratch(shifted, 1, *slip.shape, components)
        + [pltpu.VMEM((1, height, length), jnp.float32)],
        compiler_params=params(),
        name="convolve_last",
    )(shifted, slip, first)


def add_kernel(own_ref, *refs):
    sent_refs, out_ref = refs[:-1], refs[-1]
    part, components, length = out_ref.shape
    rows = own_ref.shape[0] // components
    total = own_ref[...]
    for ref in sent_refs:
        unit = unit_of(ref[:, length:].astype(jnp.int32)[:, :1])
        total = total + ref[:, :length].astype(jnp.int32).astype(jnp.float32) * unit
    for comp in range(components):
        out_ref[:, comp, :] = total[comp * rows : comp * rows + part]


def add_up(own, sent, part, components):
    return pl.pallas_call(
        add_kernel,
        out_shape=jax.ShapeDtypeStruct((part, components, own.shape[1]), jnp.float32),
        compiler_params=params(),
        name="add_up",
    )(own, *sent)


def local(slip_rates, green_tiles, patch_slot):
    devices = lax.axis_size("patch")
    sites = lax.axis_size("site")
    chips = devices // 2
    patches, held, samples = slip_rates.shape
    components, lags = green_tiles.shape[2:]
    length = samples + lags
    part = held // 2
    rows = round_up(part, ROWS)
    assert chips == sites and sites & (sites - 1) == 0

    def over_patch(value, offset):
        return lax.ppermute(value, "patch", [(i, i ^ offset) for i in range(devices)])

    slips = slip_rates
    if rows > part:
        slips = slips.reshape(patches, 2, part, samples)
        slips = jnp.pad(slips, ((0, 0), (0, 0), (0, rows - part), (0, 0)))
        slips = slips.reshape(patches, 2 * rows, samples)
    greens = green_tiles[0]
    other, other_tiles = over_patch(slips, 1), over_patch(greens, 1)
    share = 2 * max(1, patches // devices)
    capacity = round_up(4 * share, 16)
    block, send, pick, greens = arrange_own(
        slips, patch_slot.reshape(1, -1), greens, chips, 2 * patches, capacity
    )
    block = arrange_other(other, other_tiles, block)

    pieces = list(route_tiles(send, greens, other_tiles, block, chips))
    arrived = []
    for index, piece in enumerate(pieces[1:]):
        hops = [(2 * index + 1, 2 * index + 2), (chips - 1, chips - 1)][index == len(pieces) - 2]
        arrived.append(
            lax.ppermute(piece, "patch", [(i, i ^ (2 * hops[i % 2])) for i in range(devices)])
        )

    pieces = pieces[:1]
    for piece in arrived:
        pieces += [piece, over_patch(piece, 1)]

    blocks = {0: block}
    for step in [2**i for i in range(sites.bit_length())] + list(range(sites)):
        if 0 < step < sites and step not in blocks:
            low = step & -step
            blocks[step] = lax.ppermute(
                blocks[step - low], "site", [(i, i ^ low) for i in range(sites)]
            )
            if step == sites // 2:
                blocks[step] = pass_on(blocks[step], *arrived)
    shifted = shift_tiles(pick, pieces, components)

    slips = [blocks[step] for step in range(sites)]
    first = convolve_first(shifted, slips[:-1], rows, components, length)
    sums = convolve_last(shifted, slips[-1], first, rows, components)
    order = [1, chips - 1] + list(range(2, chips - 1))
    sent = [over_patch(sums[step], 2 * step) for step in order]
    return add_up(sums[0], sent, part, components)[None]


def solution(mesh):
    in_specs = (P("patch", "site", None), P("site", "patch", None, None), P())
    out_specs = P("site", "patch", None, None)
    return jax.shard_map(local, mesh=mesh, in_specs=in_specs, out_specs=out_specs, check_vma=False)
```

```python
import functools

import jax
import jax.numpy as jnp
from jax import lax
from jax.experimental import pallas as pl
from jax.experimental.pallas import tpu as pltpu
from jax.sharding import PartitionSpec as P

BLOCK = 16
LANES = 128
ROWS = 8
VMEM_LIMIT = 32 * 1024 * 1024
LARGEST = 32767.0
STEPS = 16
SMALLEST = 1e-30


def round_up(value, unit):
    return -(-value // unit) * unit


def params(limit=VMEM_LIMIT):
    return pltpu.CompilerParams(vmem_limit_bytes=limit)


def arrange_half(slip_ref, out_ref, core, owner):
    patches, both, samples = slip_ref.shape
    rows = both // 2
    per_reg = LANES // BLOCK
    blocks = samples // BLOCK
    depth = patches * BLOCK
    lane_block = lax.broadcasted_iota(jnp.int32, (rows, LANES), 1) // BLOCK
    for group in range(depth // LANES):
        done = {}
        for place in range(per_reg):
            full = slip_ref[group * per_reg + place].astype(jnp.float32)
            source = jnp.where(core == 0, full[:rows], full[rows:])
            for reg in range(samples // LANES):
                piece = source[:, reg * LANES : (reg + 1) * LANES]
                for inner in range(per_reg):
                    turn = (place - inner) % per_reg * BLOCK
                    moved = pltpu.roll(piece, turn, 1) if turn else piece
                    block = reg * per_reg + inner
                    if block in done:
                        moved = jnp.where(lane_block == place, moved, done[block])
                    done[block] = moved
        lanes = pl.ds(pl.multiple_of(owner * depth + group * LANES, LANES), LANES)
        for block in range(0, blocks, 2):
            pair = jnp.concatenate([done[block], done[block + 1]], axis=0)
            out_ref[block * rows : (block + 2) * rows, lanes] = pair.astype(jnp.bfloat16)


def arrange_own_kernel(
    chips,
    per_chip,
    capacity,
    slip_hbm,
    slots_hbm,
    green_hbm,
    out_ref,
    send_ref,
    pick_ref,
    green_ref,
    slip_ref,
    slots_ref,
    sems,
):
    fetch_slips = pltpu.make_async_copy(slip_hbm, slip_ref, sems.at[0])
    fetch_slots = pltpu.make_async_copy(slots_hbm, slots_ref, sems.at[1])
    fetch_greens = pltpu.make_async_copy(green_hbm, green_ref, sems.at[2])
    fetch_slips.start()
    fetch_slots.start()
    fetch_greens.start()
    fetch_slots.wait()
    mark_tiles(chips, per_chip, capacity, green_hbm.shape[0], slots_ref, send_ref, pick_ref)
    fetch_slips.wait()
    core = lax.rem(lax.axis_index("patch"), 2)
    arrange_half(slip_ref, out_ref, core, core)
    fetch_greens.wait()


def arrange_other_kernel(slip_ref, green_ref, block_ref, out_ref):
    core = lax.rem(lax.axis_index("patch"), 2)
    arrange_half(slip_ref, out_ref, core, 1 - core)


def in_hbm(*values):
    return [pltpu.with_memory_space_constraint(value, pltpu.HBM) for value in values]


def arrange_own(slips, slots, greens, chips, per_chip, capacity):
    patches, both, samples = slips.shape
    width = greens.shape[0]
    block = jax.ShapeDtypeStruct(
        (samples // BLOCK * both // 2, 2 * patches * BLOCK), jnp.bfloat16
    )
    return pl.pallas_call(
        functools.partial(arrange_own_kernel, chips, per_chip, capacity),
        in_specs=[pl.BlockSpec(memory_space=pltpu.HBM)] * 3,
        out_shape=(
            block,
            jax.ShapeDtypeStruct((chips * capacity, 2 * width), jnp.bfloat16),
            jax.ShapeDtypeStruct(((chips + 1) * capacity, per_chip), jnp.bfloat16),
            jax.ShapeDtypeStruct(greens.shape, greens.dtype),
        ),
        scratch_shapes=[
            pltpu.VMEM(slips.shape, slips.dtype),
            pltpu.VMEM(slots.shape, slots.dtype),
            pltpu.SemaphoreType.DMA((3,)),
        ],
        compiler_params=params(),
        name="arrange_own",
    )(*in_hbm(slips, slots, greens))


def arrange_other(slips, greens, block):
    return pl.pallas_call(
        arrange_other_kernel,
        in_specs=[
            pl.BlockSpec(memory_space=pltpu.VMEM),
            pl.BlockSpec(memory_space=pl.ANY),
            pl.BlockSpec(memory_space=pltpu.VMEM),
        ],
        out_shape=jax.ShapeDtypeStruct(block.shape, block.dtype),
        input_output_aliases={2: 0},
        compiler_params=params(),
        name="arrange_other",
    )(slips, greens, block)


def earlier_in_chip(count, per_chip):
    q = lax.broadcasted_iota(jnp.int32, (count, count), 0)
    p = lax.broadcasted_iota(jnp.int32, (count, count), 1)
    return ((q < p) & (q // per_chip == p // per_chip)).astype(jnp.float32).astype(jnp.bfloat16)


def one_hot(condition):
    return condition.astype(jnp.float32).astype(jnp.bfloat16)


def mark_tiles(chips, per_chip, capacity, width, slots_ref, send_ref, pick_ref):
    count = slots_ref.shape[1]
    own = lax.axis_index("patch")
    chip, core = own // 2, lax.rem(own, 2)
    slots = slots_ref[...]
    owner = slots // width
    mine = owner // 2 == chip
    place = slots % width + jnp.where(owner % 2 == core, 0, width)
    marks = jnp.broadcast_to(one_hot(mine), (16, count))
    rank = jnp.dot(marks, earlier_in_chip(count, per_chip), preferred_element_type=jnp.float32)
    rank = rank[:1].astype(jnp.int32)
    target = (lax.broadcasted_iota(jnp.int32, (1, count), 1) // per_chip) ^ chip
    code = jnp.where(mine, target * capacity + rank, -1)
    code_pick = one_hot(lax.broadcasted_iota(jnp.int32, (chips * capacity, count), 0) == code)
    slot_pick = one_hot(lax.broadcasted_iota(jnp.int32, (2 * width, count), 0) == place)
    send_ref[...] = lax.dot_general(
        code_pick, slot_pick, (((1,), (1,)), ((), ())), preferred_element_type=jnp.float32
    ).astype(jnp.bfloat16)
    here = pltpu.roll(slots, lax.rem(count - chip * per_chip, count), 1)[:, :per_chip]
    owner = (here // (2 * width)) ^ chip
    marks = lax.broadcasted_iota(jnp.int32, (round_up(chips, 16), per_chip), 0) == owner
    rank = jnp.dot(
        one_hot(marks), earlier_in_chip(per_chip, per_chip), preferred_element_type=jnp.float32
    )
    rank = jnp.sum(jnp.where(marks, rank, 0.0), axis=0, keepdims=True).astype(jnp.int32)
    by_first = (owner % 2 == 1) & (owner < chips - 1)
    index = jnp.where(owner == chips - 1, 0, owner // 2)
    place = 1 + 2 * index + jnp.where(by_first == (core == 0), 0, 1)
    code = jnp.where(owner == 0, 0, place) * capacity + rank
    pick_ref[...] = one_hot(lax.broadcasted_iota(jnp.int32, pick_ref.shape, 0) == code)


def send_rounds(chips):
    firsts = list(range(1, chips - 1, 2)) + [0]
    seconds = [chips - 1] + list(range(2, chips - 1, 2))
    return list(zip(firsts, seconds))


def route_kernel(chips, send_ref, own_ref, other_ref, after_ref, *out_refs):
    capacity = send_ref.shape[0] // chips
    core = lax.rem(lax.axis_index("patch"), 2)
    tiles = jnp.concatenate([own_ref[...], other_ref[...]], axis=0).astype(jnp.float32)
    by_comp = []
    for comp in range(own_ref.shape[1]):
        both = tiles[:, comp, :].astype(jnp.bfloat16)
        chosen = jnp.dot(send_ref[...], both, preferred_element_type=jnp.float32)
        chosen = [chosen[step * capacity : (step + 1) * capacity] for step in range(chips)]
        sent = [chosen[0]]
        for first, second in send_rounds(chips):
            sent.append(jnp.where(core == 0, chosen[first], chosen[second]))
        by_comp.append(sent)
    for values, out_ref in zip(zip(*by_comp), out_refs):
        out_ref[...] = jnp.concatenate(values, axis=0).astype(jnp.bfloat16)


def route_tiles(send, own, other, after, chips):
    components, lags = own.shape[1:]
    rows = components * send.shape[0] // chips
    shape = jax.ShapeDtypeStruct((rows, lags), jnp.bfloat16)
    return pl.pallas_call(
        functools.partial(route_kernel, chips),
        in_specs=[pl.BlockSpec(memory_space=pltpu.VMEM)] * 3
        + [pl.BlockSpec(memory_space=pl.ANY)],
        out_shape=(shape,) * (1 + chips // 2),
        compiler_params=params(),
        name="route_tiles",
    )(send, own, other, after)


def pass_on(value, *others):
    def kernel(*refs):
        pass

    return pl.pallas_call(
        kernel,
        in_specs=[pl.BlockSpec(memory_space=pl.ANY)] * (1 + len(others)),
        out_specs=pl.BlockSpec(memory_space=pl.ANY),
        out_shape=jax.ShapeDtypeStruct(value.shape, value.dtype),
        input_output_aliases={0: 0},
        compiler_params=params(),
        name="pass_on",
    )(value, *others)


def shift_kernel(pick_ref, *refs):
    pieces, out_ref = refs[:-1], refs[-1]
    count = pick_ref.shape[1]
    capacity = pick_ref.shape[0] // len(pieces)
    components = pieces[0].shape[0] // capacity
    lags = pieces[0].shape[1]
    span = out_ref.shape[1] // components
    tail = jnp.zeros((BLOCK, span - lags), jnp.float32)
    for comp in range(components):
        arrived = jnp.concatenate(
            [piece[comp * capacity : (comp + 1) * capacity, :] for piece in pieces], axis=0
        )
        tiles = lax.dot_general(
            pick_ref[...], arrived, (((0,), (0,)), ((), ())), preferred_element_type=jnp.float32
        )
        for patch in range(count):
            row = jnp.broadcast_to(tiles[patch : patch + 1], (BLOCK, lags))
            wide = jnp.concatenate([row, tail], axis=1)
            moved = pltpu.roll(wide, 0, 1, stride=1, stride_axis=0)
            out_ref[
                patch * BLOCK : (patch + 1) * BLOCK, comp * span : (comp + 1) * span
            ] = moved.astype(jnp.bfloat16)


def shift_tiles(pick, pieces, components):
    lags = pieces[0].shape[1]
    span = round_up(lags + BLOCK, LANES)
    shape = jax.ShapeDtypeStruct((pick.shape[1] * BLOCK, components * span), jnp.bfloat16)
    return pl.pallas_call(
        shift_kernel, out_shape=shape, compiler_params=params(), name="shift_tiles"
    )(pick, *pieces)


def convolve_blocks(shifted_ref, slip_refs, stack_ref, product_ref, out_ref, rows):
    length = out_ref.shape[2]
    components = out_ref.shape[1] // rows
    height = slip_refs[0].shape[0]
    width = shifted_ref.shape[1] // components
    per_reg = LANES // BLOCK
    blocks = height // rows
    for step, ref in enumerate(slip_refs):
        stack_ref[step * height : (step + 1) * height] = ref[...]
    for comp in range(components):
        product_ref[...] = jnp.dot(
            stack_ref[...],
            shifted_ref[:, comp * width : (comp + 1) * width],
            preferred_element_type=jnp.float32,
        )
        for step in range(len(slip_refs)):
            total = None
            for inner in range(per_reg):
                part = None
                for outer in range(inner, blocks, per_reg):
                    lead = outer // per_reg * LANES
                    start = step * height + outer * rows
                    block = product_ref[start : start + rows, :]
                    pieces = [jnp.zeros((rows, lead), jnp.float32)] if lead else []
                    pieces.append(block[:, : min(width, length - lead)])
                    if length > lead + width:
                        pieces.append(jnp.zeros((rows, length - lead - width), jnp.float32))
                    block = jnp.concatenate(pieces, axis=1) if len(pieces) > 1 else pieces[0]
                    part = block if part is None else part + block
                if inner:
                    part = pltpu.roll(part, inner * BLOCK, 1)
                total = part if total is None else total + part
            out_ref[step, comp * rows : (comp + 1) * rows, :] = total


def convolve_first_kernel(rows, shifted_ref, *refs):
    slip_refs, (out_ref, stack_ref, product_ref) = refs[:-3], refs[-3:]
    convolve_blocks(shifted_ref, slip_refs, stack_ref, product_ref, out_ref, rows)


def convolve_scratch(shifted, count, height, depth, components):
    return [
        pltpu.VMEM((count * height, depth), jnp.bfloat16),
        pltpu.VMEM((count * height, shifted.shape[1] // components), jnp.float32),
    ]


def convolve_first(shifted, slips, rows, components, length):
    shape = jax.ShapeDtypeStruct((len(slips), components * rows, length), jnp.float32)
    return pl.pallas_call(
        functools.partial(convolve_first_kernel, rows),
        out_shape=shape,
        scratch_shapes=convolve_scratch(shifted, len(slips), *slips[0].shape, components),
        compiler_params=params(),
        name="convolve_first",
    )(shifted, *slips)


def unit_of(exponent):
    return jnp.exp2(exponent.astype(jnp.float32) * (1.0 / STEPS)) * (1.0 / LARGEST)


def convolve_last_kernel(rows, shifted_ref, slip_ref, first_ref, *refs):
    out_refs, (stack_ref, product_ref, last_ref) = refs[:-3], refs[-3:]
    convolve_blocks(shifted_ref, [slip_ref], stack_ref, product_ref, last_ref, rows)
    count = first_ref.shape[0]
    length = first_ref.shape[2]
    turn = lax.axis_index("site") ^ (lax.axis_index("patch") // 2)
    last = last_ref[0]
    for step, ref in enumerate(out_refs):
        source = step ^ turn
        total = jnp.where(source == count, last, first_ref[jnp.minimum(source, count - 1)])
        if step == 0:
            ref[...] = total
            continue
        peak = jnp.maximum(jnp.max(jnp.abs(total), axis=1, keepdims=True), SMALLEST)
        exponent = jnp.ceil(jnp.log2(peak) * STEPS).astype(jnp.int32)
        scaled = jnp.round(total * (1.0 / unit_of(exponent)))
        whole = jnp.clip(scaled, -LARGEST, LARGEST).astype(jnp.int32)
        ref[:, :length] = whole.astype(jnp.int16)
        ref[:, length:] = jnp.broadcast_to(
            exponent, (exponent.shape[0], ref.shape[1] - length)
        ).astype(jnp.int16)


def convolve_last(shifted, slip, first, rows, components):
    count, height, length = first.shape
    own = jax.ShapeDtypeStruct((height, length), jnp.float32)
    sent = jax.ShapeDtypeStruct((height, round_up(length, LANES) + LANES), jnp.int16)
    return pl.pallas_call(
        functools.partial(convolve_last_kernel, rows),
        out_shape=(own,) + (sent,) * count,
        scratch_shapes=convolve_scratch(shifted, 1, *slip.shape, components)
        + [pltpu.VMEM((1, height, length), jnp.float32)],
        compiler_params=params(),
        name="convolve_last",
    )(shifted, slip, first)


def add_kernel(own_ref, *refs):
    sent_refs, out_ref = refs[:-1], refs[-1]
    part, components, length = out_ref.shape
    rows = own_ref.shape[0] // components
    total = own_ref[...]
    for ref in sent_refs:
        unit = unit_of(ref[:, length:].astype(jnp.int32)[:, :1])
        total = total + ref[:, :length].astype(jnp.int32).astype(jnp.float32) * unit
    for comp in range(components):
        out_ref[:, comp, :] = total[comp * rows : comp * rows + part]


def add_up(own, sent, part, components):
    return pl.pallas_call(
        add_kernel,
        out_shape=jax.ShapeDtypeStruct((part, components, own.shape[1]), jnp.float32),
        compiler_params=params(),
        name="add_up",
    )(own, *sent)


def local(slip_rates, green_tiles, patch_slot):
    devices = lax.axis_size("patch")
    sites = lax.axis_size("site")
    chips = devices // 2
    patches, held, samples = slip_rates.shape
    components, lags = green_tiles.shape[2:]
    length = samples + lags
    part = held // 2
    rows = round_up(part, ROWS)
    assert chips == sites and sites & (sites - 1) == 0

    def over_patch(value, offset):
        return lax.ppermute(value, "patch", [(i, i ^ offset) for i in range(devices)])

    slips = slip_rates
    if rows > part:
        slips = slips.reshape(patches, 2, part, samples)
        slips = jnp.pad(slips, ((0, 0), (0, 0), (0, rows - part), (0, 0)))
        slips = slips.reshape(patches, 2 * rows, samples)
    greens = green_tiles[0]
    other, other_tiles = over_patch(slips, 1), over_patch(greens, 1)
    share = 2 * max(1, patches // devices)
    capacity = round_up(4 * share, 16)
    block, send, pick, greens = arrange_own(
        slips, patch_slot.reshape(1, -1), greens, chips, 2 * patches, capacity
    )
    block = arrange_other(other, other_tiles, block)

    pieces = list(route_tiles(send, greens, other_tiles, block, chips))
    arrived = []
    for piece, hops in zip(pieces[1:], send_rounds(chips)):
        arrived.append(
            lax.ppermute(piece, "patch", [(i, i ^ (2 * hops[i % 2])) for i in range(devices)])
        )
    pieces = pieces[:1]
    for piece in arrived:
        pieces += [piece, over_patch(piece, 1)]

    blocks = {0: block}
    for step in [2**i for i in range(sites.bit_length())] + list(range(sites)):
        if 0 < step < sites and step not in blocks:
            low = step & -step
            blocks[step] = lax.ppermute(
                blocks[step - low], "site", [(i, i ^ low) for i in range(sites)]
            )
            if step == sites // 2:
                blocks[step] = pass_on(blocks[step], *arrived)
    shifted = shift_tiles(pick, pieces, components)

    slips = [blocks[step] for step in range(sites)]
    first = convolve_first(shifted, slips[:-1], rows, components, length)
    sums = convolve_last(shifted, slips[-1], first, rows, components)
    order = [1, chips - 1] + list(range(2, chips - 1))
    sent = [over_patch(sums[step], 2 * step) for step in order]
    return add_up(sums[0], sent, part, components)[None]


def solution(mesh):
    in_specs = (P("patch", "site", None), P("site", "patch", None, None), P())
    out_specs = P("site", "patch", None, None)
    return jax.shard_map(local, mesh=mesh, in_specs=in_specs, out_specs=out_specs, check_vma=False)
```

```python
import functools

import jax
import jax.numpy as jnp
from jax import lax
from jax.experimental import pallas as pl
from jax.experimental.pallas import tpu as pltpu
from jax.sharding import PartitionSpec as P

BLOCK = 16
LANES = 128
ROWS = 8
VMEM_LIMIT = 32 * 1024 * 1024
LARGEST = 32767.0
STEPS = 16
SMALLEST = 1e-30


def round_up(value, unit):
    return -(-value // unit) * unit


def params(limit=VMEM_LIMIT):
    return pltpu.CompilerParams(vmem_limit_bytes=limit)


def arrange_half(slip_ref, out_ref, core, owner):
    patches, both, samples = slip_ref.shape
    rows = both // 2
    per_reg = LANES // BLOCK
    blocks = samples // BLOCK
    depth = patches * BLOCK
    lane_block = lax.broadcasted_iota(jnp.int32, (rows, LANES), 1) // BLOCK
    for group in range(depth // LANES):
        done = {}
        for place in range(per_reg):
            full = slip_ref[group * per_reg + place].astype(jnp.float32)
            source = jnp.where(core == 0, full[:rows], full[rows:])
            for reg in range(samples // LANES):
                piece = source[:, reg * LANES : (reg + 1) * LANES]
                for inner in range(per_reg):
                    turn = (place - inner) % per_reg * BLOCK
                    moved = pltpu.roll(piece, turn, 1) if turn else piece
                    block = reg * per_reg + inner
                    if block in done:
                        moved = jnp.where(lane_block == place, moved, done[block])
                    done[block] = moved
        lanes = pl.ds(pl.multiple_of(owner * depth + group * LANES, LANES), LANES)
        for block in range(0, blocks, 2):
            pair = jnp.concatenate([done[block], done[block + 1]], axis=0)
            out_ref[block * rows : (block + 2) * rows, lanes] = pair.astype(jnp.bfloat16)


def arrange_own_kernel(
    chips,
    per_chip,
    capacity,
    slip_ref,
    slots_ref,
    green_ref,
    out_ref,
    send_ref,
    pick_ref,
    tiles_ref,
):
    width = green_ref.shape[0]
    mark_tiles(chips, per_chip, capacity, width, slots_ref, send_ref, pick_ref)
    core = lax.rem(lax.axis_index("patch"), 2)
    arrange_half(slip_ref, out_ref, core, core)
    tiles = green_ref[...].astype(jnp.float32)
    for comp in range(green_ref.shape[1]):
        tiles_ref[comp * width : (comp + 1) * width, :] = tiles[:, comp, :].astype(jnp.bfloat16)


def arrange_other_kernel(slip_ref, green_ref, block_ref, out_ref):
    core = lax.rem(lax.axis_index("patch"), 2)
    arrange_half(slip_ref, out_ref, core, 1 - core)


def arrange_own(slips, slots, greens, chips, per_chip, capacity):
    patches, both, samples = slips.shape
    width, components, lags = greens.shape
    block = jax.ShapeDtypeStruct(
        (samples // BLOCK * both // 2, 2 * patches * BLOCK), jnp.bfloat16
    )
    return pl.pallas_call(
        functools.partial(arrange_own_kernel, chips, per_chip, capacity),
        out_shape=(
            block,
            jax.ShapeDtypeStruct((chips * capacity, 2 * width), jnp.bfloat16),
            jax.ShapeDtypeStruct((chips * capacity, per_chip), jnp.bfloat16),
            jax.ShapeDtypeStruct((components * width, lags), jnp.bfloat16),
        ),
        compiler_params=params(),
        name="arrange_own",
    )(slips, slots, greens)


def arrange_other(slips, greens, block):
    return pl.pallas_call(
        arrange_other_kernel,
        in_specs=[
            pl.BlockSpec(memory_space=pltpu.VMEM),
            pl.BlockSpec(memory_space=pl.ANY),
            pl.BlockSpec(memory_space=pltpu.VMEM),
        ],
        out_shape=jax.ShapeDtypeStruct(block.shape, block.dtype),
        input_output_aliases={2: 0},
        compiler_params=params(),
        name="arrange_other",
    )(slips, greens, block)


def earlier_in_chip(count, per_chip):
    q = lax.broadcasted_iota(jnp.int32, (count, count), 0)
    p = lax.broadcasted_iota(jnp.int32, (count, count), 1)
    return ((q < p) & (q // per_chip == p // per_chip)).astype(jnp.float32).astype(jnp.bfloat16)


def one_hot(condition):
    return condition.astype(jnp.float32).astype(jnp.bfloat16)


def mark_tiles(chips, per_chip, capacity, width, slots_ref, send_ref, pick_ref):
    half = capacity // 2
    count = slots_ref.shape[1]
    own = lax.axis_index("patch")
    chip, core = own // 2, lax.rem(own, 2)
    slots = slots_ref[...]
    owner = slots // width
    mine = owner // 2 == chip
    place = slots % width + jnp.where(owner % 2 == core, 0, width)
    marks = jnp.broadcast_to(one_hot(mine), (16, count))
    rank = jnp.dot(marks, earlier_in_chip(count, per_chip), preferred_element_type=jnp.float32)
    rank = rank[:1].astype(jnp.int32)
    target = (lax.broadcasted_iota(jnp.int32, (1, count), 1) // per_chip) ^ chip
    code = jnp.where(mine, target * capacity + rank, -1)
    code_pick = one_hot(lax.broadcasted_iota(jnp.int32, (chips * capacity, count), 0) == code)
    slot_pick = one_hot(lax.broadcasted_iota(jnp.int32, (2 * width, count), 0) == place)
    send_ref[...] = lax.dot_general(
        code_pick, slot_pick, (((1,), (1,)), ((), ())), preferred_element_type=jnp.float32
    ).astype(jnp.bfloat16)
    here = pltpu.roll(slots, lax.rem(count - chip * per_chip, count), 1)[:, :per_chip]
    owner = (here // (2 * width)) ^ chip
    marks = lax.broadcasted_iota(jnp.int32, (round_up(chips, 16), per_chip), 0) == owner
    rank = jnp.dot(
        one_hot(marks), earlier_in_chip(per_chip, per_chip), preferred_element_type=jnp.float32
    )
    rank = jnp.sum(jnp.where(marks, rank, 0.0), axis=0, keepdims=True).astype(jnp.int32)
    from_other = jnp.where(owner == chips - 1, rank // half, 1 - owner % 2) != core
    base = (owner - jnp.where(owner == chips - 1, 0, 1 - owner % 2)) * capacity
    code = base + jnp.where(
        owner == chips - 1,
        jnp.where(from_other, half, 0) + rank % half,
        jnp.where(from_other, capacity, 0) + rank,
    )
    code = jnp.where(owner == 0, rank, code)
    pick_ref[...] = one_hot(lax.broadcasted_iota(jnp.int32, pick_ref.shape, 0) == code)


def route_kernel(chips, send_ref, own_ref, other_ref, after_ref, *out_refs):
    capacity = send_ref.shape[0] // chips
    half = capacity // 2
    core = lax.rem(lax.axis_index("patch"), 2)
    width, components, _ = other_ref.shape
    tiles = other_ref[...].astype(jnp.float32)
    by_comp = []
    for comp in range(components):
        both = jnp.concatenate(
            [own_ref[comp * width : (comp + 1) * width, :], tiles[:, comp, :].astype(jnp.bfloat16)],
            axis=0,
        )
        chosen = jnp.dot(send_ref[...], both, preferred_element_type=jnp.float32)
        chosen = [chosen[step * capacity : (step + 1) * capacity] for step in range(chips)]
        last = chosen[-1]
        sent = [chosen[0]]
        for step in range(1, chips - 1, 2):
            sent.append(jnp.where(core == 0, chosen[step], chosen[step + 1]))
        sent.append(jnp.where(core == 0, last[:half], last[half:]))
        by_comp.append(sent)
    for values, out_ref in zip(zip(*by_comp), out_refs):
        out_ref[...] = jnp.concatenate(values, axis=0).astype(jnp.bfloat16)


def route_tiles(send, own, other, after, chips):
    components, lags = other.shape[1:]
    rows = components * send.shape[0] // chips
    shape = jax.ShapeDtypeStruct((rows, lags), jnp.bfloat16)
    part = jax.ShapeDtypeStruct((rows // 2, lags), jnp.bfloat16)
    return pl.pallas_call(
        functools.partial(route_kernel, chips),
        in_specs=[pl.BlockSpec(memory_space=pltpu.VMEM)] * 3
        + [pl.BlockSpec(memory_space=pl.ANY)],
        out_shape=(shape,) * (chips // 2) + (part,),
        compiler_params=params(),
        name="route_tiles",
    )(send, own, other, after)


def pass_on(value, *others):
    def kernel(*refs):
        pass

    return pl.pallas_call(
        kernel,
        in_specs=[pl.BlockSpec(memory_space=pl.ANY)] * (1 + len(others)),
        out_specs=pl.BlockSpec(memory_space=pl.ANY),
        out_shape=jax.ShapeDtypeStruct(value.shape, value.dtype),
        input_output_aliases={0: 0},
        compiler_params=params(),
        name="pass_on",
    )(value, *others)


def shift_kernel(pick_ref, *refs):
    pieces, out_ref = refs[:-1], refs[-1]
    count = pick_ref.shape[1]
    components = sum(piece.shape[0] for piece in pieces) // pick_ref.shape[0]
    lags = pieces[0].shape[1]
    span = out_ref.shape[1] // components
    tail = jnp.zeros((BLOCK, span - lags), jnp.float32)
    for comp in range(components):
        arrived = []
        for piece in pieces:
            size = piece.shape[0] // components
            arrived.append(piece[...].astype(jnp.float32)[comp * size : (comp + 1) * size])
        arrived = jnp.concatenate(arrived, axis=0).astype(jnp.bfloat16)
        tiles = lax.dot_general(
            pick_ref[...], arrived, (((0,), (0,)), ((), ())), preferred_element_type=jnp.float32
        )
        for patch in range(count):
            row = jnp.broadcast_to(tiles[patch : patch + 1], (BLOCK, lags))
            wide = jnp.concatenate([row, tail], axis=1)
            moved = pltpu.roll(wide, 0, 1, stride=1, stride_axis=0)
            out_ref[
                patch * BLOCK : (patch + 1) * BLOCK, comp * span : (comp + 1) * span
            ] = moved.astype(jnp.bfloat16)


def shift_tiles(pick, pieces, components):
    lags = pieces[0].shape[1]
    span = round_up(lags + BLOCK, LANES)
    shape = jax.ShapeDtypeStruct((pick.shape[1] * BLOCK, components * span), jnp.bfloat16)
    return pl.pallas_call(
        shift_kernel, out_shape=shape, compiler_params=params(), name="shift_tiles"
    )(pick, *pieces)


def convolve_blocks(shifted_ref, slip_refs, stack_ref, product_ref, out_ref, rows):
    length = out_ref.shape[2]
    components = out_ref.shape[1] // rows
    height = slip_refs[0].shape[0]
    width = shifted_ref.shape[1] // components
    per_reg = LANES // BLOCK
    blocks = height // rows
    for step, ref in enumerate(slip_refs):
        stack_ref[step * height : (step + 1) * height] = ref[...]
    for comp in range(components):
        product_ref[...] = jnp.dot(
            stack_ref[...],
            shifted_ref[:, comp * width : (comp + 1) * width],
            preferred_element_type=jnp.float32,
        )
        for step in range(len(slip_refs)):
            total = None
            for inner in range(per_reg):
                part = None
                for outer in range(inner, blocks, per_reg):
                    lead = outer // per_reg * LANES
                    start = step * height + outer * rows
                    block = product_ref[start : start + rows, :]
                    pieces = [jnp.zeros((rows, lead), jnp.float32)] if lead else []
                    pieces.append(block[:, : min(width, length - lead)])
                    if length > lead + width:
                        pieces.append(jnp.zeros((rows, length - lead - width), jnp.float32))
                    block = jnp.concatenate(pieces, axis=1) if len(pieces) > 1 else pieces[0]
                    part = block if part is None else part + block
                if inner:
                    part = pltpu.roll(part, inner * BLOCK, 1)
                total = part if total is None else total + part
            out_ref[step, comp * rows : (comp + 1) * rows, :] = total


def unit_of(exponent):
    return jnp.exp2(exponent.astype(jnp.float32) * (1.0 / STEPS)) * (1.0 / LARGEST)


def as_sent(total, lanes):
    peak = jnp.maximum(jnp.max(jnp.abs(total), axis=1, keepdims=True), SMALLEST)
    exponent = jnp.ceil(jnp.log2(peak) * STEPS).astype(jnp.int32)
    whole = jnp.clip(jnp.round(total * (1.0 / unit_of(exponent))), -LARGEST, LARGEST)
    rest = jnp.broadcast_to(exponent, (total.shape[0], lanes - total.shape[1]))
    return jnp.concatenate([whole.astype(jnp.int32), rest], axis=1).astype(jnp.int16)


def convolve_first_kernel(rows, shifted_ref, *refs):
    slip_refs, (out_ref, sent_ref, stack_ref, product_ref) = refs[:-4], refs[-4:]
    convolve_blocks(shifted_ref, slip_refs, stack_ref, product_ref, out_ref, rows)
    for step in range(out_ref.shape[0]):
        sent_ref[step] = as_sent(out_ref[step], sent_ref.shape[2])


def convolve_scratch(shifted, count, height, depth, components):
    return [
        pltpu.VMEM((count * height, depth), jnp.bfloat16),
        pltpu.VMEM((count * height, shifted.shape[1] // components), jnp.float32),
    ]


def convolve_first(shifted, slips, rows, components, length):
    size = (len(slips), components * rows)
    lanes = round_up(length, LANES) + LANES
    return pl.pallas_call(
        functools.partial(convolve_first_kernel, rows),
        out_shape=(
            jax.ShapeDtypeStruct(size + (length,), jnp.float32),
            jax.ShapeDtypeStruct(size + (lanes,), jnp.int16),
        ),
        scratch_shapes=convolve_scratch(shifted, len(slips), *slips[0].shape, components),
        compiler_params=params(),
        name="convolve_first",
    )(shifted, *slips)


def convolve_last_kernel(rows, shifted_ref, slip_ref, first_ref, early_ref, *refs):
    out_refs, (stack_ref, product_ref, last_ref) = refs[:-3], refs[-3:]
    convolve_blocks(shifted_ref, [slip_ref], stack_ref, product_ref, last_ref, rows)
    count = first_ref.shape[0]
    turn = lax.axis_index("site") ^ (lax.axis_index("patch") // 2)
    last = last_ref[0]
    late = as_sent(last, early_ref.shape[2])
    for step, ref in enumerate(out_refs):
        source = step ^ turn
        before = jnp.minimum(source, count - 1)

        @pl.when(source == count)
        def _():
            ref[...] = late if step else last

        @pl.when(source < count)
        def _():
            ref[...] = early_ref[before] if step else first_ref[before]


def convolve_last(shifted, slip, first, early, rows, components):
    count, height, length = first.shape
    own = jax.ShapeDtypeStruct((height, length), jnp.float32)
    sent = jax.ShapeDtypeStruct(early.shape[1:], jnp.int16)
    return pl.pallas_call(
        functools.partial(convolve_last_kernel, rows),
        out_shape=(own,) + (sent,) * count,
        scratch_shapes=convolve_scratch(shifted, 1, *slip.shape, components)
        + [pltpu.VMEM((1, height, length), jnp.float32)],
        compiler_params=params(),
        name="convolve_last",
    )(shifted, slip, first, early)


def add_kernel(own_ref, *refs):
    sent_refs, out_ref = refs[:-1], refs[-1]
    part, components, length = out_ref.shape
    rows = own_ref.shape[0] // components
    total = own_ref[...]
    for ref in sent_refs:
        unit = unit_of(ref[:, length:].astype(jnp.int32)[:, :1])
        total = total + ref[:, :length].astype(jnp.int32).astype(jnp.float32) * unit
    for comp in range(components):
        out_ref[:, comp, :] = total[comp * rows : comp * rows + part]


def add_up(own, sent, part, components):
    return pl.pallas_call(
        add_kernel,
        out_shape=jax.ShapeDtypeStruct((part, components, own.shape[1]), jnp.float32),
        compiler_params=params(),
        name="add_up",
    )(own, *sent)


def local(slip_rates, green_tiles, patch_slot):
    devices = lax.axis_size("patch")
    sites = lax.axis_size("site")
    chips = devices // 2
    patches, held, samples = slip_rates.shape
    components, lags = green_tiles.shape[2:]
    length = samples + lags
    part = held // 2
    rows = round_up(part, ROWS)
    assert chips == sites and sites & (sites - 1) == 0

    def over_patch(value, offset):
        return lax.ppermute(value, "patch", [(i, i ^ offset) for i in range(devices)])

    slips = slip_rates
    if rows > part:
        slips = slips.reshape(patches, 2, part, samples)
        slips = jnp.pad(slips, ((0, 0), (0, 0), (0, rows - part), (0, 0)))
        slips = slips.reshape(patches, 2 * rows, samples)
    greens = green_tiles[0]
    other_tiles, other = over_patch(greens, 1), over_patch(slips, 1)
    share = 2 * max(1, patches // devices)
    capacity = round_up(4 * share, 16)
    own_slips, own_tiles = over_patch(slips, 0), over_patch(greens, 0)
    block, send, pick, own_tiles = arrange_own(
        own_slips, patch_slot.reshape(1, -1), own_tiles, chips, 2 * patches, capacity
    )
    block = arrange_other(other, other_tiles, block)

    pieces = list(route_tiles(send, own_tiles, other_tiles, block, chips))
    arrived = [None] * (len(pieces) - 1)
    for index in reversed(range(len(arrived))):
        hops = [(2 * index + 1, 2 * index + 2), (chips - 1, chips - 1)][index == len(arrived) - 1]
        arrived[index] = lax.ppermute(
            pieces[1 + index], "patch", [(i, i ^ (2 * hops[i % 2])) for i in range(devices)]
        )
    pieces = pieces[:1]
    for piece in arrived:
        pieces += [piece, over_patch(piece, 1)]

    blocks = {0: block}
    for step in [2**i for i in range(sites.bit_length())] + list(range(sites)):
        if 0 < step < sites and step not in blocks:
            low = step & -step
            blocks[step] = lax.ppermute(
                blocks[step - low], "site", [(i, i ^ low) for i in range(sites)]
            )
            if step == sites // 2:
                blocks[step] = pass_on(blocks[step], *arrived)
    shifted = shift_tiles(pick, pieces, components)

    slips = [blocks[step] for step in range(sites)]
    first, early = convolve_first(shifted, slips[:-1], rows, components, length)
    sums = convolve_last(shifted, slips[-1], first, early, rows, components)
    order = [1, chips - 1] + list(range(2, chips - 1))
    sent = [over_patch(sums[step], 2 * step) for step in order]
    return add_up(sums[0], sent, part, components)[None]


def solution(mesh):
    in_specs = (P("patch", "site", None), P("site", "patch", None, None), P())
    out_specs = P("site", "patch", None, None)
    return jax.shard_map(local, mesh=mesh, in_specs=in_specs, out_specs=out_specs, check_vma=False)
```

```python
import functools

import jax
import jax.numpy as jnp
from jax import lax
from jax.experimental import pallas as pl
from jax.experimental.pallas import tpu as pltpu
from jax.sharding import PartitionSpec as P

BLOCK = 16
LANES = 128
ROWS = 8
VMEM_LIMIT = 32 * 1024 * 1024
LARGEST = 32767.0
STEPS = 16
SMALLEST = 1e-30


def round_up(value, unit):
    return -(-value // unit) * unit


def params(limit=VMEM_LIMIT):
    return pltpu.CompilerParams(vmem_limit_bytes=limit)


def arrange_half(slip_ref, out_ref, core, owner):
    patches, both, samples = slip_ref.shape
    rows = both // 2
    per_reg = LANES // BLOCK
    blocks = samples // BLOCK
    depth = patches * BLOCK
    lane_block = lax.broadcasted_iota(jnp.int32, (rows, LANES), 1) // BLOCK
    for group in range(depth // LANES):
        done = {}
        for place in range(per_reg):
            full = slip_ref[group * per_reg + place].astype(jnp.float32)
            source = jnp.where(core == 0, full[:rows], full[rows:])
            for reg in range(samples // LANES):
                piece = source[:, reg * LANES : (reg + 1) * LANES]
                for inner in range(per_reg):
                    turn = (place - inner) % per_reg * BLOCK
                    moved = pltpu.roll(piece, turn, 1) if turn else piece
                    block = reg * per_reg + inner
                    if block in done:
                        moved = jnp.where(lane_block == place, moved, done[block])
                    done[block] = moved
        lanes = pl.ds(pl.multiple_of(owner * depth + group * LANES, LANES), LANES)
        for block in range(0, blocks, 2):
            pair = jnp.concatenate([done[block], done[block + 1]], axis=0)
            out_ref[block * rows : (block + 2) * rows, lanes] = pair.astype(jnp.bfloat16)


def arrange_own_kernel(
    chips,
    per_chip,
    capacity,
    slip_hbm,
    slots_hbm,
    green_hbm,
    out_ref,
    send_ref,
    pick_ref,
    tiles_ref,
    slip_ref,
    slots_ref,
    green_ref,
    sems,
):
    width = green_ref.shape[0]
    fetch_slips = pltpu.make_async_copy(slip_hbm, slip_ref, sems.at[0])
    fetch_slots = pltpu.make_async_copy(slots_hbm, slots_ref, sems.at[1])
    fetch_greens = pltpu.make_async_copy(green_hbm, green_ref, sems.at[2])
    fetch_slots.start()
    fetch_slips.start()
    fetch_greens.start()
    fetch_slots.wait()
    mark_tiles(chips, per_chip, capacity, width, slots_ref, send_ref, pick_ref)
    fetch_slips.wait()
    core = lax.rem(lax.axis_index("patch"), 2)
    arrange_half(slip_ref, out_ref, core, core)
    fetch_greens.wait()
    tiles = green_ref[...].astype(jnp.float32)
    for comp in range(green_ref.shape[1]):
        tiles_ref[comp * width : (comp + 1) * width, :] = tiles[:, comp, :].astype(jnp.bfloat16)


def arrange_other_kernel(slip_ref, green_ref, block_ref, out_ref):
    core = lax.rem(lax.axis_index("patch"), 2)
    arrange_half(slip_ref, out_ref, core, 1 - core)


def in_hbm(*values):
    return [pltpu.with_memory_space_constraint(value, pltpu.HBM) for value in values]


def arrange_own(slips, slots, greens, chips, per_chip, capacity):
    patches, both, samples = slips.shape
    width, components, lags = greens.shape
    block = jax.ShapeDtypeStruct(
        (samples // BLOCK * both // 2, 2 * patches * BLOCK), jnp.bfloat16
    )
    return pl.pallas_call(
        functools.partial(arrange_own_kernel, chips, per_chip, capacity),
        in_specs=[pl.BlockSpec(memory_space=pltpu.HBM)] * 3,
        out_shape=(
            block,
            jax.ShapeDtypeStruct((chips * capacity, 2 * width), jnp.bfloat16),
            jax.ShapeDtypeStruct((chips * capacity, per_chip), jnp.bfloat16),
            jax.ShapeDtypeStruct((components * width, lags), jnp.bfloat16),
        ),
        scratch_shapes=[
            pltpu.VMEM(slips.shape, slips.dtype),
            pltpu.VMEM(slots.shape, slots.dtype),
            pltpu.VMEM(greens.shape, greens.dtype),
            pltpu.SemaphoreType.DMA((3,)),
        ],
        compiler_params=params(),
        name="arrange_own",
    )(*in_hbm(slips, slots, greens))


def arrange_other(slips, greens, block):
    return pl.pallas_call(
        arrange_other_kernel,
        in_specs=[
            pl.BlockSpec(memory_space=pltpu.VMEM),
            pl.BlockSpec(memory_space=pl.ANY),
            pl.BlockSpec(memory_space=pltpu.VMEM),
        ],
        out_shape=jax.ShapeDtypeStruct(block.shape, block.dtype),
        input_output_aliases={2: 0},
        compiler_params=params(),
        name="arrange_other",
    )(slips, greens, block)


def earlier_in_chip(count, per_chip):
    q = lax.broadcasted_iota(jnp.int32, (count, count), 0)
    p = lax.broadcasted_iota(jnp.int32, (count, count), 1)
    return ((q < p) & (q // per_chip == p // per_chip)).astype(jnp.float32).astype(jnp.bfloat16)


def one_hot(condition):
    return condition.astype(jnp.float32).astype(jnp.bfloat16)


def mark_tiles(chips, per_chip, capacity, width, slots_ref, send_ref, pick_ref):
    half = capacity // 2
    count = slots_ref.shape[1]
    own = lax.axis_index("patch")
    chip, core = own // 2, lax.rem(own, 2)
    slots = slots_ref[...]
    owner = slots // width
    mine = owner // 2 == chip
    place = slots % width + jnp.where(owner % 2 == core, 0, width)
    marks = jnp.broadcast_to(one_hot(mine), (16, count))
    rank = jnp.dot(marks, earlier_in_chip(count, per_chip), preferred_element_type=jnp.float32)
    rank = rank[:1].astype(jnp.int32)
    target = (lax.broadcasted_iota(jnp.int32, (1, count), 1) // per_chip) ^ chip
    code = jnp.where(mine, target * capacity + rank, -1)
    code_pick = one_hot(lax.broadcasted_iota(jnp.int32, (chips * capacity, count), 0) == code)
    slot_pick = one_hot(lax.broadcasted_iota(jnp.int32, (2 * width, count), 0) == place)
    send_ref[...] = lax.dot_general(
        code_pick, slot_pick, (((1,), (1,)), ((), ())), preferred_element_type=jnp.float32
    ).astype(jnp.bfloat16)
    here = pltpu.roll(slots, lax.rem(count - chip * per_chip, count), 1)[:, :per_chip]
    owner = (here // (2 * width)) ^ chip
    marks = lax.broadcasted_iota(jnp.int32, (round_up(chips, 16), per_chip), 0) == owner
    rank = jnp.dot(
        one_hot(marks), earlier_in_chip(per_chip, per_chip), preferred_element_type=jnp.float32
    )
    rank = jnp.sum(jnp.where(marks, rank, 0.0), axis=0, keepdims=True).astype(jnp.int32)
    from_other = jnp.where(owner == chips - 1, rank // half, 1 - owner % 2) != core
    base = (owner - jnp.where(owner == chips - 1, 0, 1 - owner % 2)) * capacity
    code = base + jnp.where(
        owner == chips - 1,
        jnp.where(from_other, half, 0) + rank % half,
        jnp.where(from_other, capacity, 0) + rank,
    )
    code = jnp.where(owner == 0, rank, code)
    pick_ref[...] = one_hot(lax.broadcasted_iota(jnp.int32, pick_ref.shape, 0) == code)


def route_kernel(chips, send_ref, own_ref, other_ref, after_ref, *out_refs):
    capacity = send_ref.shape[0] // chips
    half = capacity // 2
    core = lax.rem(lax.axis_index("patch"), 2)
    width, components, _ = other_ref.shape
    tiles = other_ref[...].astype(jnp.float32)
    by_comp = []
    for comp in range(components):
        both = jnp.concatenate(
            [own_ref[comp * width : (comp + 1) * width, :], tiles[:, comp, :].astype(jnp.bfloat16)],
            axis=0,
        )
        chosen = jnp.dot(send_ref[...], both, preferred_element_type=jnp.float32)
        chosen = [chosen[step * capacity : (step + 1) * capacity] for step in range(chips)]
        last = chosen[-1]
        sent = [chosen[0]]
        for step in range(1, chips - 1, 2):
            sent.append(jnp.where(core == 0, chosen[step], chosen[step + 1]))
        sent.append(jnp.where(core == 0, last[:half], last[half:]))
        by_comp.append(sent)
    for values, out_ref in zip(zip(*by_comp), out_refs):
        out_ref[...] = jnp.concatenate(values, axis=0).astype(jnp.bfloat16)


def route_tiles(send, own, other, after, chips):
    components, lags = other.shape[1:]
    rows = components * send.shape[0] // chips
    shape = jax.ShapeDtypeStruct((rows, lags), jnp.bfloat16)
    part = jax.ShapeDtypeStruct((rows // 2, lags), jnp.bfloat16)
    return pl.pallas_call(
        functools.partial(route_kernel, chips),
        in_specs=[pl.BlockSpec(memory_space=pltpu.VMEM)] * 3
        + [pl.BlockSpec(memory_space=pl.ANY)],
        out_shape=(shape,) * (chips // 2) + (part,),
        compiler_params=params(),
        name="route_tiles",
    )(send, own, other, after)


def pass_on(value, *others):
    def kernel(*refs):
        pass

    return pl.pallas_call(
        kernel,
        in_specs=[pl.BlockSpec(memory_space=pl.ANY)] * (1 + len(others)),
        out_specs=pl.BlockSpec(memory_space=pl.ANY),
        out_shape=jax.ShapeDtypeStruct(value.shape, value.dtype),
        input_output_aliases={0: 0},
        compiler_params=params(),
        name="pass_on",
    )(value, *others)


def shift_kernel(pick_ref, *refs):
    pieces, out_ref = refs[:-1], refs[-1]
    count = pick_ref.shape[1]
    components = sum(piece.shape[0] for piece in pieces) // pick_ref.shape[0]
    lags = pieces[0].shape[1]
    span = out_ref.shape[1] // components
    tail = jnp.zeros((BLOCK, span - lags), jnp.float32)
    for comp in range(components):
        arrived = []
        for piece in pieces:
            size = piece.shape[0] // components
            arrived.append(piece[...].astype(jnp.float32)[comp * size : (comp + 1) * size])
        arrived = jnp.concatenate(arrived, axis=0).astype(jnp.bfloat16)
        tiles = lax.dot_general(
            pick_ref[...], arrived, (((0,), (0,)), ((), ())), preferred_element_type=jnp.float32
        )
        for patch in range(count):
            row = jnp.broadcast_to(tiles[patch : patch + 1], (BLOCK, lags))
            wide = jnp.concatenate([row, tail], axis=1)
            moved = pltpu.roll(wide, 0, 1, stride=1, stride_axis=0)
            out_ref[
                patch * BLOCK : (patch + 1) * BLOCK, comp * span : (comp + 1) * span
            ] = moved.astype(jnp.bfloat16)


def shift_tiles(pick, pieces, components):
    lags = pieces[0].shape[1]
    span = round_up(lags + BLOCK, LANES)
    shape = jax.ShapeDtypeStruct((pick.shape[1] * BLOCK, components * span), jnp.bfloat16)
    return pl.pallas_call(
        shift_kernel, out_shape=shape, compiler_params=params(), name="shift_tiles"
    )(pick, *pieces)


def convolve_blocks(shifted_ref, slip_refs, stack_ref, product_ref, out_ref, rows):
    length = out_ref.shape[2]
    components = out_ref.shape[1] // rows
    height = slip_refs[0].shape[0]
    width = shifted_ref.shape[1] // components
    per_reg = LANES // BLOCK
    blocks = height // rows
    for step, ref in enumerate(slip_refs):
        stack_ref[step * height : (step + 1) * height] = ref[...]
    for comp in range(components):
        product_ref[...] = jnp.dot(
            stack_ref[...],
            shifted_ref[:, comp * width : (comp + 1) * width],
            preferred_element_type=jnp.float32,
        )
        for step in range(len(slip_refs)):
            total = None
            for inner in range(per_reg):
                part = None
                for outer in range(inner, blocks, per_reg):
                    lead = outer // per_reg * LANES
                    start = step * height + outer * rows
                    block = product_ref[start : start + rows, :]
                    pieces = [jnp.zeros((rows, lead), jnp.float32)] if lead else []
                    pieces.append(block[:, : min(width, length - lead)])
                    if length > lead + width:
                        pieces.append(jnp.zeros((rows, length - lead - width), jnp.float32))
                    block = jnp.concatenate(pieces, axis=1) if len(pieces) > 1 else pieces[0]
                    part = block if part is None else part + block
                if inner:
                    part = pltpu.roll(part, inner * BLOCK, 1)
                total = part if total is None else total + part
            out_ref[step, comp * rows : (comp + 1) * rows, :] = total


def unit_of(exponent):
    return jnp.exp2(exponent.astype(jnp.float32) * (1.0 / STEPS)) * (1.0 / LARGEST)


def as_sent(total, lanes):
    peak = jnp.maximum(jnp.max(jnp.abs(total), axis=1, keepdims=True), SMALLEST)
    exponent = jnp.ceil(jnp.log2(peak) * STEPS).astype(jnp.int32)
    whole = jnp.clip(jnp.round(total * (1.0 / unit_of(exponent))), -LARGEST, LARGEST)
    rest = jnp.broadcast_to(exponent, (total.shape[0], lanes - total.shape[1]))
    return jnp.concatenate([whole.astype(jnp.int32), rest], axis=1).astype(jnp.int16)


def convolve_first_kernel(rows, shifted_ref, *refs):
    slip_refs, (out_ref, sent_ref, stack_ref, product_ref) = refs[:-4], refs[-4:]
    convolve_blocks(shifted_ref, slip_refs, stack_ref, product_ref, out_ref, rows)
    for step in range(out_ref.shape[0]):
        sent_ref[step] = as_sent(out_ref[step], sent_ref.shape[2])


def convolve_scratch(shifted, count, height, depth, components):
    return [
        pltpu.VMEM((count * height, depth), jnp.bfloat16),
        pltpu.VMEM((count * height, shifted.shape[1] // components), jnp.float32),
    ]


def convolve_first(shifted, slips, rows, components, length):
    size = (len(slips), components * rows)
    lanes = round_up(length, LANES) + LANES
    return pl.pallas_call(
        functools.partial(convolve_first_kernel, rows),
        out_shape=(
            jax.ShapeDtypeStruct(size + (length,), jnp.float32),
            jax.ShapeDtypeStruct(size + (lanes,), jnp.int16),
        ),
        scratch_shapes=convolve_scratch(shifted, len(slips), *slips[0].shape, components),
        compiler_params=params(),
        name="convolve_first",
    )(shifted, *slips)


def convolve_last_kernel(rows, shifted_ref, slip_ref, first_ref, early_ref, *refs):
    out_refs, (stack_ref, product_ref, last_ref) = refs[:-3], refs[-3:]
    convolve_blocks(shifted_ref, [slip_ref], stack_ref, product_ref, last_ref, rows)
    count = first_ref.shape[0]
    turn = lax.axis_index("site") ^ (lax.axis_index("patch") // 2)
    last = last_ref[0]
    late = as_sent(last, early_ref.shape[2])
    for step, ref in enumerate(out_refs):
        source = step ^ turn
        before = jnp.minimum(source, count - 1)

        @pl.when(source == count)
        def _():
            ref[...] = late if step else last

        @pl.when(source < count)
        def _():
            ref[...] = early_ref[before] if step else first_ref[before]


def convolve_last(shifted, slip, first, early, rows, components):
    count, height, length = first.shape
    own = jax.ShapeDtypeStruct((height, length), jnp.float32)
    sent = jax.ShapeDtypeStruct(early.shape[1:], jnp.int16)
    return pl.pallas_call(
        functools.partial(convolve_last_kernel, rows),
        out_shape=(own,) + (sent,) * count,
        scratch_shapes=convolve_scratch(shifted, 1, *slip.shape, components)
        + [pltpu.VMEM((1, height, length), jnp.float32)],
        compiler_params=params(),
        name="convolve_last",
    )(shifted, slip, first, early)


def add_kernel(own_ref, *refs):
    sent_refs, out_ref = refs[:-1], refs[-1]
    part, components, length = out_ref.shape
    rows = own_ref.shape[0] // components
    total = own_ref[...]
    for ref in sent_refs:
        unit = unit_of(ref[:, length:].astype(jnp.int32)[:, :1])
        total = total + ref[:, :length].astype(jnp.int32).astype(jnp.float32) * unit
    for comp in range(components):
        out_ref[:, comp, :] = total[comp * rows : comp * rows + part]


def add_up(own, sent, part, components):
    return pl.pallas_call(
        add_kernel,
        out_shape=jax.ShapeDtypeStruct((part, components, own.shape[1]), jnp.float32),
        compiler_params=params(),
        name="add_up",
    )(own, *sent)


def local(slip_rates, green_tiles, patch_slot):
    devices = lax.axis_size("patch")
    sites = lax.axis_size("site")
    chips = devices // 2
    patches, held, samples = slip_rates.shape
    components, lags = green_tiles.shape[2:]
    length = samples + lags
    part = held // 2
    rows = round_up(part, ROWS)
    assert chips == sites and sites & (sites - 1) == 0

    def over_patch(value, offset):
        return lax.ppermute(value, "patch", [(i, i ^ offset) for i in range(devices)])

    slips = slip_rates
    if rows > part:
        slips = slips.reshape(patches, 2, part, samples)
        slips = jnp.pad(slips, ((0, 0), (0, 0), (0, rows - part), (0, 0)))
        slips = slips.reshape(patches, 2 * rows, samples)
    greens = green_tiles[0]
    other_tiles, other = over_patch(greens, 1), over_patch(slips, 1)
    share = 2 * max(1, patches // devices)
    capacity = round_up(4 * share, 16)
    block, send, pick, own_tiles = arrange_own(
        slips, patch_slot.reshape(1, -1), greens, chips, 2 * patches, capacity
    )
    block = arrange_other(other, other_tiles, block)

    pieces = list(route_tiles(send, own_tiles, other_tiles, block, chips))
    arrived = [None] * (len(pieces) - 1)
    for index in reversed(range(len(arrived))):
        hops = [(2 * index + 1, 2 * index + 2), (chips - 1, chips - 1)][index == len(arrived) - 1]
        arrived[index] = lax.ppermute(
            pieces[1 + index], "patch", [(i, i ^ (2 * hops[i % 2])) for i in range(devices)]
        )
    pieces = pieces[:1]
    for piece in arrived:
        pieces += [piece, over_patch(piece, 1)]

    blocks = {0: block}
    for step in [2**i for i in range(sites.bit_length())] + list(range(sites)):
        if 0 < step < sites and step not in blocks:
            low = step & -step
            blocks[step] = lax.ppermute(
                blocks[step - low], "site", [(i, i ^ low) for i in range(sites)]
            )
            if step == sites // 2:
                blocks[step] = pass_on(blocks[step], *arrived)
    shifted = shift_tiles(pick, pieces, components)

    slips = [blocks[step] for step in range(sites)]
    first, early = convolve_first(shifted, slips[:-1], rows, components, length)
    sums = convolve_last(shifted, slips[-1], first, early, rows, components)
    order = [1, chips - 1] + list(range(2, chips - 1))
    sent = [over_patch(sums[step], 2 * step) for step in order]
    return add_up(sums[0], sent, part, components)[None]


def solution(mesh):
    in_specs = (P("patch", "site", None), P("site", "patch", None, None), P())
    out_specs = P("site", "patch", None, None)
    return jax.shard_map(local, mesh=mesh, in_specs=in_specs, out_specs=out_specs, check_vma=False)
```

```python
import functools

import jax
import jax.numpy as jnp
from jax import lax
from jax.experimental import pallas as pl
from jax.experimental.pallas import tpu as pltpu
from jax.sharding import PartitionSpec as P

BLOCK = 16
LANES = 128
ROWS = 8
VMEM_LIMIT = 32 * 1024 * 1024
LARGEST = 32767.0
STEPS = 16
SMALLEST = 1e-30


def round_up(value, unit):
    return -(-value // unit) * unit


def params(limit=VMEM_LIMIT):
    return pltpu.CompilerParams(vmem_limit_bytes=limit)


def arrange_half(slip_ref, out_ref, core, owner, fetches=()):
    patches, both, samples = slip_ref.shape
    rows = both // 2
    per_reg = LANES // BLOCK
    blocks = samples // BLOCK
    depth = patches * BLOCK
    lane_block = lax.broadcasted_iota(jnp.int32, (rows, LANES), 1) // BLOCK
    for group in range(depth // LANES):
        done = {}
        for fetch in fetches[group * len(fetches) * LANES // depth :][: len(fetches) * LANES // depth]:
            fetch.wait()
        for place in range(per_reg):
            full = slip_ref[group * per_reg + place].astype(jnp.float32)
            source = jnp.where(core == 0, full[:rows], full[rows:])
            for reg in range(samples // LANES):
                piece = source[:, reg * LANES : (reg + 1) * LANES]
                for inner in range(per_reg):
                    turn = (place - inner) % per_reg * BLOCK
                    moved = pltpu.roll(piece, turn, 1) if turn else piece
                    block = reg * per_reg + inner
                    if block in done:
                        moved = jnp.where(lane_block == place, moved, done[block])
                    done[block] = moved
        lanes = pl.ds(pl.multiple_of(owner * depth + group * LANES, LANES), LANES)
        for block in range(0, blocks, 2):
            pair = jnp.concatenate([done[block], done[block + 1]], axis=0)
            out_ref[block * rows : (block + 2) * rows, lanes] = pair.astype(jnp.bfloat16)


def arrange_own_kernel(
    chips,
    per_chip,
    capacity,
    slip_hbm,
    slots_hbm,
    green_hbm,
    out_ref,
    send_ref,
    pick_ref,
    tiles_ref,
    slip_ref,
    slots_ref,
    green_ref,
    sems,
):
    width = green_ref.shape[0]
    parts = sems.shape[0] - 2
    size = slip_ref.shape[0] // parts
    fetch_slots = pltpu.make_async_copy(slots_hbm, slots_ref, sems.at[parts])
    fetch_greens = pltpu.make_async_copy(green_hbm, green_ref, sems.at[parts + 1])
    fetch_slips = []
    for part in range(parts):
        some = pl.ds(part * size, size)
        fetch_slips.append(
            pltpu.make_async_copy(slip_hbm.at[some], slip_ref.at[some], sems.at[part])
        )
    fetch_slots.start()
    for fetch in fetch_slips:
        fetch.start()
    fetch_greens.start()
    fetch_slots.wait()
    mark_tiles(chips, per_chip, capacity, width, slots_ref, send_ref, pick_ref)
    core = lax.rem(lax.axis_index("patch"), 2)
    arrange_half(slip_ref, out_ref, core, core, fetch_slips)
    fetch_greens.wait()
    tiles = green_ref[...].astype(jnp.float32)
    for comp in range(green_ref.shape[1]):
        tiles_ref[comp * width : (comp + 1) * width, :] = tiles[:, comp, :].astype(jnp.bfloat16)


def arrange_other_kernel(slip_ref, green_ref, block_ref, out_ref):
    core = lax.rem(lax.axis_index("patch"), 2)
    arrange_half(slip_ref, out_ref, core, 1 - core)


def in_hbm(*values):
    return [pltpu.with_memory_space_constraint(value, pltpu.HBM) for value in values]


def arrange_own(slips, slots, greens, chips, per_chip, capacity):
    patches, both, samples = slips.shape
    width, components, lags = greens.shape
    block = jax.ShapeDtypeStruct(
        (samples // BLOCK * both // 2, 2 * patches * BLOCK), jnp.bfloat16
    )
    return pl.pallas_call(
        functools.partial(arrange_own_kernel, chips, per_chip, capacity),
        in_specs=[pl.BlockSpec(memory_space=pltpu.HBM)] * 3,
        out_shape=(
            block,
            jax.ShapeDtypeStruct((chips * capacity, 2 * width), jnp.bfloat16),
            jax.ShapeDtypeStruct((chips * capacity, per_chip), jnp.bfloat16),
            jax.ShapeDtypeStruct((components * width, lags), jnp.bfloat16),
        ),
        scratch_shapes=[
            pltpu.VMEM(slips.shape, slips.dtype),
            pltpu.VMEM(slots.shape, slots.dtype),
            pltpu.VMEM(greens.shape, greens.dtype),
            pltpu.SemaphoreType.DMA((2 * patches * BLOCK // LANES + 2,)),
        ],
        compiler_params=params(),
        name="arrange_own",
    )(*in_hbm(slips, slots, greens))


def arrange_other(slips, greens, block):
    return pl.pallas_call(
        arrange_other_kernel,
        in_specs=[
            pl.BlockSpec(memory_space=pltpu.VMEM),
            pl.BlockSpec(memory_space=pl.ANY),
            pl.BlockSpec(memory_space=pltpu.VMEM),
        ],
        out_shape=jax.ShapeDtypeStruct(block.shape, block.dtype),
        input_output_aliases={2: 0},
        compiler_params=params(),
        name="arrange_other",
    )(slips, greens, block)


def earlier_in_chip(count, per_chip):
    q = lax.broadcasted_iota(jnp.int32, (count, count), 0)
    p = lax.broadcasted_iota(jnp.int32, (count, count), 1)
    return ((q < p) & (q // per_chip == p // per_chip)).astype(jnp.float32).astype(jnp.bfloat16)


def one_hot(condition):
    return condition.astype(jnp.float32).astype(jnp.bfloat16)


def mark_tiles(chips, per_chip, capacity, width, slots_ref, send_ref, pick_ref):
    half = capacity // 2
    count = slots_ref.shape[1]
    own = lax.axis_index("patch")
    chip, core = own // 2, lax.rem(own, 2)
    slots = slots_ref[...]
    owner = slots // width
    mine = owner // 2 == chip
    place = slots % width + jnp.where(owner % 2 == core, 0, width)
    marks = jnp.broadcast_to(one_hot(mine), (16, count))
    rank = jnp.dot(marks, earlier_in_chip(count, per_chip), preferred_element_type=jnp.float32)
    rank = rank[:1].astype(jnp.int32)
    target = (lax.broadcasted_iota(jnp.int32, (1, count), 1) // per_chip) ^ chip
    code = jnp.where(mine, target * capacity + rank, -1)
    code_pick = one_hot(lax.broadcasted_iota(jnp.int32, (chips * capacity, count), 0) == code)
    slot_pick = one_hot(lax.broadcasted_iota(jnp.int32, (2 * width, count), 0) == place)
    send_ref[...] = lax.dot_general(
        code_pick, slot_pick, (((1,), (1,)), ((), ())), preferred_element_type=jnp.float32
    ).astype(jnp.bfloat16)
    here = pltpu.roll(slots, lax.rem(count - chip * per_chip, count), 1)[:, :per_chip]
    owner = (here // (2 * width)) ^ chip
    marks = lax.broadcasted_iota(jnp.int32, (round_up(chips, 16), per_chip), 0) == owner
    rank = jnp.dot(
        one_hot(marks), earlier_in_chip(per_chip, per_chip), preferred_element_type=jnp.float32
    )
    rank = jnp.sum(jnp.where(marks, rank, 0.0), axis=0, keepdims=True).astype(jnp.int32)
    from_other = jnp.where(owner == chips - 1, rank // half, 1 - owner % 2) != core
    base = (owner - jnp.where(owner == chips - 1, 0, 1 - owner % 2)) * capacity
    code = base + jnp.where(
        owner == chips - 1,
        jnp.where(from_other, half, 0) + rank % half,
        jnp.where(from_other, capacity, 0) + rank,
    )
    code = jnp.where(owner == 0, rank, code)
    pick_ref[...] = one_hot(lax.broadcasted_iota(jnp.int32, pick_ref.shape, 0) == code)


def route_kernel(chips, send_ref, own_ref, other_ref, after_ref, *out_refs):
    capacity = send_ref.shape[0] // chips
    half = capacity // 2
    core = lax.rem(lax.axis_index("patch"), 2)
    width, components, _ = other_ref.shape
    tiles = other_ref[...].astype(jnp.float32)
    by_comp = []
    for comp in range(components):
        both = jnp.concatenate(
            [own_ref[comp * width : (comp + 1) * width, :], tiles[:, comp, :].astype(jnp.bfloat16)],
            axis=0,
        )
        chosen = jnp.dot(send_ref[...], both, preferred_element_type=jnp.float32)
        chosen = [chosen[step * capacity : (step + 1) * capacity] for step in range(chips)]
        last = chosen[-1]
        sent = [chosen[0]]
        for step in range(1, chips - 1, 2):
            sent.append(jnp.where(core == 0, chosen[step], chosen[step + 1]))
        sent.append(jnp.where(core == 0, last[:half], last[half:]))
        by_comp.append(sent)
    for values, out_ref in zip(zip(*by_comp), out_refs):
        out_ref[...] = jnp.concatenate(values, axis=0).astype(jnp.bfloat16)


def route_tiles(send, own, other, after, chips):
    components, lags = other.shape[1:]
    rows = components * send.shape[0] // chips
    shape = jax.ShapeDtypeStruct((rows, lags), jnp.bfloat16)
    part = jax.ShapeDtypeStruct((rows // 2, lags), jnp.bfloat16)
    return pl.pallas_call(
        functools.partial(route_kernel, chips),
        in_specs=[pl.BlockSpec(memory_space=pltpu.VMEM)] * 3
        + [pl.BlockSpec(memory_space=pl.ANY)],
        out_shape=(shape,) * (chips // 2) + (part,),
        compiler_params=params(),
        name="route_tiles",
    )(send, own, other, after)


def pass_on(value, *others):
    def kernel(*refs):
        pass

    return pl.pallas_call(
        kernel,
        in_specs=[pl.BlockSpec(memory_space=pl.ANY)] * (1 + len(others)),
        out_specs=pl.BlockSpec(memory_space=pl.ANY),
        out_shape=jax.ShapeDtypeStruct(value.shape, value.dtype),
        input_output_aliases={0: 0},
        compiler_params=params(),
        name="pass_on",
    )(value, *others)


def shift_kernel(pick_ref, *refs):
    pieces, out_ref = refs[:-1], refs[-1]
    count = pick_ref.shape[1]
    components = sum(piece.shape[0] for piece in pieces) // pick_ref.shape[0]
    lags = pieces[0].shape[1]
    span = out_ref.shape[1] // components
    tail = jnp.zeros((BLOCK, span - lags), jnp.float32)
    for comp in range(components):
        arrived = []
        for piece in pieces:
            size = piece.shape[0] // components
            arrived.append(piece[...].astype(jnp.float32)[comp * size : (comp + 1) * size])
        arrived = jnp.concatenate(arrived, axis=0).astype(jnp.bfloat16)
        tiles = lax.dot_general(
            pick_ref[...], arrived, (((0,), (0,)), ((), ())), preferred_element_type=jnp.float32
        )
        for patch in range(count):
            row = jnp.broadcast_to(tiles[patch : patch + 1], (BLOCK, lags))
            wide = jnp.concatenate([row, tail], axis=1)
            moved = pltpu.roll(wide, 0, 1, stride=1, stride_axis=0)
            out_ref[
                patch * BLOCK : (patch + 1) * BLOCK, comp * span : (comp + 1) * span
            ] = moved.astype(jnp.bfloat16)


def shift_tiles(pick, pieces, components):
    lags = pieces[0].shape[1]
    span = round_up(lags + BLOCK, LANES)
    shape = jax.ShapeDtypeStruct((pick.shape[1] * BLOCK, components * span), jnp.bfloat16)
    return pl.pallas_call(
        shift_kernel, out_shape=shape, compiler_params=params(), name="shift_tiles"
    )(pick, *pieces)


def convolve_blocks(shifted_ref, slip_refs, stack_ref, product_ref, out_ref, rows):
    length = out_ref.shape[2]
    components = out_ref.shape[1] // rows
    height = slip_refs[0].shape[0]
    width = shifted_ref.shape[1] // components
    per_reg = LANES // BLOCK
    blocks = height // rows
    for step, ref in enumerate(slip_refs):
        stack_ref[step * height : (step + 1) * height] = ref[...]
    for comp in range(components):
        product_ref[...] = jnp.dot(
            stack_ref[...],
            shifted_ref[:, comp * width : (comp + 1) * width],
            preferred_element_type=jnp.float32,
        )
        for step in range(len(slip_refs)):
            total = None
            for inner in range(per_reg):
                part = None
                for outer in range(inner, blocks, per_reg):
                    lead = outer // per_reg * LANES
                    start = step * height + outer * rows
                    block = product_ref[start : start + rows, :]
                    pieces = [jnp.zeros((rows, lead), jnp.float32)] if lead else []
                    pieces.append(block[:, : min(width, length - lead)])
                    if length > lead + width:
                        pieces.append(jnp.zeros((rows, length - lead - width), jnp.float32))
                    block = jnp.concatenate(pieces, axis=1) if len(pieces) > 1 else pieces[0]
                    part = block if part is None else part + block
                if inner:
                    part = pltpu.roll(part, inner * BLOCK, 1)
                total = part if total is None else total + part
            out_ref[step, comp * rows : (comp + 1) * rows, :] = total


def unit_of(exponent):
    return jnp.exp2(exponent.astype(jnp.float32) * (1.0 / STEPS)) * (1.0 / LARGEST)


def as_sent(total, lanes):
    peak = jnp.maximum(jnp.max(jnp.abs(total), axis=1, keepdims=True), SMALLEST)
    exponent = jnp.ceil(jnp.log2(peak) * STEPS).astype(jnp.int32)
    whole = jnp.clip(jnp.round(total * (1.0 / unit_of(exponent))), -LARGEST, LARGEST)
    rest = jnp.broadcast_to(exponent, (total.shape[0], lanes - total.shape[1]))
    return jnp.concatenate([whole.astype(jnp.int32), rest], axis=1).astype(jnp.int16)


def convolve_first_kernel(rows, shifted_ref, *refs):
    slip_refs, (out_ref, sent_ref, stack_ref, product_ref) = refs[:-4], refs[-4:]
    convolve_blocks(shifted_ref, slip_refs, stack_ref, product_ref, out_ref, rows)
    for step in range(out_ref.shape[0]):
        sent_ref[step] = as_sent(out_ref[step], sent_ref.shape[2])


def convolve_scratch(shifted, count, height, depth, components):
    return [
        pltpu.VMEM((count * height, depth), jnp.bfloat16),
        pltpu.VMEM((count * height, shifted.shape[1] // components), jnp.float32),
    ]


def convolve_first(shifted, slips, rows, components, length):
    size = (len(slips), components * rows)
    lanes = round_up(length, LANES) + LANES
    return pl.pallas_call(
        functools.partial(convolve_first_kernel, rows),
        out_shape=(
            jax.ShapeDtypeStruct(size + (length,), jnp.float32),
            jax.ShapeDtypeStruct(size + (lanes,), jnp.int16),
        ),
        scratch_shapes=convolve_scratch(shifted, len(slips), *slips[0].shape, components),
        compiler_params=params(),
        name="convolve_first",
    )(shifted, *slips)


def convolve_last_kernel(rows, shifted_ref, slip_ref, first_ref, early_ref, *refs):
    out_refs, (stack_ref, product_ref, last_ref) = refs[:-3], refs[-3:]
    convolve_blocks(shifted_ref, [slip_ref], stack_ref, product_ref, last_ref, rows)
    count = first_ref.shape[0]
    turn = lax.axis_index("site") ^ (lax.axis_index("patch") // 2)
    last = last_ref[0]
    late = as_sent(last, early_ref.shape[2])
    for step, ref in enumerate(out_refs):
        source = step ^ turn
        before = jnp.minimum(source, count - 1)

        @pl.when(source == count)
        def _():
            ref[...] = late if step else last

        @pl.when(source < count)
        def _():
            ref[...] = early_ref[before] if step else first_ref[before]


def convolve_last(shifted, slip, first, early, rows, components):
    count, height, length = first.shape
    own = jax.ShapeDtypeStruct((height, length), jnp.float32)
    sent = jax.ShapeDtypeStruct(early.shape[1:], jnp.int16)
    return pl.pallas_call(
        functools.partial(convolve_last_kernel, rows),
        out_shape=(own,) + (sent,) * count,
        scratch_shapes=convolve_scratch(shifted, 1, *slip.shape, components)
        + [pltpu.VMEM((1, height, length), jnp.float32)],
        compiler_params=params(),
        name="convolve_last",
    )(shifted, slip, first, early)


def with_sent(total, sent_refs):
    length = total.shape[1]
    for ref in sent_refs:
        unit = unit_of(ref[:, length:].astype(jnp.int32)[:, :1])
        total = total + ref[:, :length].astype(jnp.int32).astype(jnp.float32) * unit
    return total


def add_early_kernel(own_ref, *refs):
    refs[-1][...] = with_sent(own_ref[...], refs[:-1])


def add_early(own, sent):
    return pl.pallas_call(
        add_early_kernel,
        out_shape=jax.ShapeDtypeStruct(own.shape, own.dtype),
        compiler_params=params(),
        name="add_early",
    )(own, *sent)


def add_kernel(own_ref, *refs):
    sent_refs, out_ref = refs[:-1], refs[-1]
    part, components, length = out_ref.shape
    rows = own_ref.shape[0] // components
    total = with_sent(own_ref[...], sent_refs)
    for comp in range(components):
        out_ref[:, comp, :] = total[comp * rows : comp * rows + part]


def add_up(own, sent, part, components):
    return pl.pallas_call(
        add_kernel,
        out_shape=jax.ShapeDtypeStruct((part, components, own.shape[1]), jnp.float32),
        compiler_params=params(),
        name="add_up",
    )(own, *sent)


def local(slip_rates, green_tiles, patch_slot):
    devices = lax.axis_size("patch")
    sites = lax.axis_size("site")
    chips = devices // 2
    patches, held, samples = slip_rates.shape
    components, lags = green_tiles.shape[2:]
    length = samples + lags
    part = held // 2
    rows = round_up(part, ROWS)
    assert chips == sites and sites & (sites - 1) == 0

    def over_patch(value, offset):
        return lax.ppermute(value, "patch", [(i, i ^ offset) for i in range(devices)])

    slips = slip_rates
    if rows > part:
        slips = slips.reshape(patches, 2, part, samples)
        slips = jnp.pad(slips, ((0, 0), (0, 0), (0, rows - part), (0, 0)))
        slips = slips.reshape(patches, 2 * rows, samples)
    greens = green_tiles[0]
    other_tiles, other = over_patch(greens, 1), over_patch(slips, 1)
    share = 2 * max(1, patches // devices)
    capacity = round_up(4 * share, 16)
    block, send, pick, own_tiles = arrange_own(
        slips, patch_slot.reshape(1, -1), greens, chips, 2 * patches, capacity
    )
    block = arrange_other(other, other_tiles, block)

    pieces = list(route_tiles(send, own_tiles, other_tiles, block, chips))
    arrived = [None] * (len(pieces) - 1)
    for index in reversed(range(len(arrived))):
        hops = [(2 * index + 1, 2 * index + 2), (chips - 1, chips - 1)][index == len(arrived) - 1]
        arrived[index] = lax.ppermute(
            pieces[1 + index], "patch", [(i, i ^ (2 * hops[i % 2])) for i in range(devices)]
        )
    pieces = pieces[:1]
    for piece in arrived:
        pieces += [piece, over_patch(piece, 1)]

    blocks = {0: block}
    for step in [2**i for i in range(sites.bit_length())] + list(range(sites)):
        if 0 < step < sites and step not in blocks:
            low = step & -step
            blocks[step] = lax.ppermute(
                blocks[step - low], "site", [(i, i ^ low) for i in range(sites)]
            )
            if step == sites // 2:
                blocks[step] = pass_on(blocks[step], *arrived)
    shifted = shift_tiles(pick, pieces, components)

    slips = [blocks[step] for step in range(sites)]
    first, early = convolve_first(shifted, slips[:-1], rows, components, length)
    sums = convolve_last(shifted, slips[-1], first, early, rows, components)
    order = [1, chips - 1] + list(range(2, chips - 1))
    sent = [over_patch(sums[step], 2 * step) for step in order]
    early = add_early(sums[0], sent[1:][::-1])
    return add_up(early, sent[:1], part, components)[None]


def solution(mesh):
    in_specs = (P("patch", "site", None), P("site", "patch", None, None), P())
    out_specs = P("site", "patch", None, None)
    return jax.shard_map(local, mesh=mesh, in_specs=in_specs, out_specs=out_specs, check_vma=False)
```

```python
import functools

import jax
import jax.numpy as jnp
from jax import lax
from jax.experimental import pallas as pl
from jax.experimental.pallas import tpu as pltpu
from jax.sharding import PartitionSpec as P

BLOCK = 16
LANES = 128
ROWS = 8
VMEM_LIMIT = 32 * 1024 * 1024
LARGEST = 32767.0
STEPS = 16
SMALLEST = 1e-30


def round_up(value, unit):
    return -(-value // unit) * unit


def params(limit=VMEM_LIMIT):
    return pltpu.CompilerParams(vmem_limit_bytes=limit)


def arrange_half(slip_ref, out_ref, core, owner):
    patches, both, samples = slip_ref.shape
    rows = both // 2
    per_reg = LANES // BLOCK
    blocks = samples // BLOCK
    depth = patches * BLOCK
    lane_block = lax.broadcasted_iota(jnp.int32, (rows, LANES), 1) // BLOCK
    for group in range(depth // LANES):
        done = {}
        for place in range(per_reg):
            full = slip_ref[group * per_reg + place].astype(jnp.float32)
            source = jnp.where(core == 0, full[:rows], full[rows:])
            for reg in range(samples // LANES):
                piece = source[:, reg * LANES : (reg + 1) * LANES]
                for inner in range(per_reg):
                    turn = (place - inner) % per_reg * BLOCK
                    moved = pltpu.roll(piece, turn, 1) if turn else piece
                    block = reg * per_reg + inner
                    if block in done:
                        moved = jnp.where(lane_block == place, moved, done[block])
                    done[block] = moved
        lanes = pl.ds(pl.multiple_of(owner * depth + group * LANES, LANES), LANES)
        for block in range(0, blocks, 2):
            pair = jnp.concatenate([done[block], done[block + 1]], axis=0)
            out_ref[block * rows : (block + 2) * rows, lanes] = pair.astype(jnp.bfloat16)


def arrange_own_kernel(
    chips,
    per_chip,
    capacity,
    slip_hbm,
    slots_hbm,
    green_hbm,
    out_ref,
    send_ref,
    pick_ref,
    tiles_ref,
    slip_ref,
    slots_ref,
    green_ref,
    sems,
):
    width = green_ref.shape[0]
    fetch_slips = pltpu.make_async_copy(slip_hbm, slip_ref, sems.at[0])
    fetch_slots = pltpu.make_async_copy(slots_hbm, slots_ref, sems.at[1])
    fetch_greens = pltpu.make_async_copy(green_hbm, green_ref, sems.at[2])
    fetch_slots.start()
    fetch_slips.start()
    fetch_greens.start()
    fetch_slots.wait()
    mark_tiles(chips, per_chip, capacity, width, slots_ref, send_ref, pick_ref)
    fetch_slips.wait()
    core = lax.rem(lax.axis_index("patch"), 2)
    arrange_half(slip_ref, out_ref, core, core)
    fetch_greens.wait()
    tiles = green_ref[...].astype(jnp.float32)
    for comp in range(green_ref.shape[1]):
        tiles_ref[comp * width : (comp + 1) * width, :] = tiles[:, comp, :].astype(jnp.bfloat16)


def arrange_other_kernel(slip_ref, green_ref, block_ref, out_ref):
    core = lax.rem(lax.axis_index("patch"), 2)
    arrange_half(slip_ref, out_ref, core, 1 - core)


def in_hbm(*values):
    return [pltpu.with_memory_space_constraint(value, pltpu.HBM) for value in values]


def arrange_own(slips, slots, greens, chips, per_chip, capacity):
    patches, both, samples = slips.shape
    width, components, lags = greens.shape
    block = jax.ShapeDtypeStruct(
        (samples // BLOCK * both // 2, 2 * patches * BLOCK), jnp.bfloat16
    )
    return pl.pallas_call(
        functools.partial(arrange_own_kernel, chips, per_chip, capacity),
        in_specs=[pl.BlockSpec(memory_space=pltpu.HBM)] * 3,
        out_shape=(
            block,
            jax.ShapeDtypeStruct((chips * capacity, 2 * width), jnp.bfloat16),
            jax.ShapeDtypeStruct((chips * capacity, per_chip), jnp.bfloat16),
            jax.ShapeDtypeStruct((components * width, lags), jnp.bfloat16),
        ),
        scratch_shapes=[
            pltpu.VMEM(slips.shape, slips.dtype),
            pltpu.VMEM(slots.shape, slots.dtype),
            pltpu.VMEM(greens.shape, greens.dtype),
            pltpu.SemaphoreType.DMA((3,)),
        ],
        compiler_params=params(),
        name="arrange_own",
    )(*in_hbm(slips, slots, greens))


def arrange_other(slips, greens, block):
    return pl.pallas_call(
        arrange_other_kernel,
        in_specs=[
            pl.BlockSpec(memory_space=pltpu.VMEM),
            pl.BlockSpec(memory_space=pl.ANY),
            pl.BlockSpec(memory_space=pltpu.VMEM),
        ],
        out_shape=jax.ShapeDtypeStruct(block.shape, block.dtype),
        input_output_aliases={2: 0},
        compiler_params=params(),
        name="arrange_other",
    )(slips, greens, block)


def earlier_in_chip(count, per_chip):
    q = lax.broadcasted_iota(jnp.int32, (count, count), 0)
    p = lax.broadcasted_iota(jnp.int32, (count, count), 1)
    return ((q < p) & (q // per_chip == p // per_chip)).astype(jnp.float32).astype(jnp.bfloat16)


def one_hot(condition):
    return condition.astype(jnp.float32).astype(jnp.bfloat16)


def mark_tiles(chips, per_chip, capacity, width, slots_ref, send_ref, pick_ref):
    count = slots_ref.shape[1]
    own = lax.axis_index("patch")
    chip, core = own // 2, lax.rem(own, 2)
    slots = slots_ref[...]
    owner = slots // width
    mine = owner // 2 == chip
    place = slots % width + jnp.where(owner % 2 == core, 0, width)
    marks = jnp.broadcast_to(one_hot(mine), (16, count))
    rank = jnp.dot(marks, earlier_in_chip(count, per_chip), preferred_element_type=jnp.float32)
    rank = rank[:1].astype(jnp.int32)
    target = (lax.broadcasted_iota(jnp.int32, (1, count), 1) // per_chip) ^ chip
    code = jnp.where(mine, target * capacity + rank, -1)
    code_pick = one_hot(lax.broadcasted_iota(jnp.int32, (chips * capacity, count), 0) == code)
    slot_pick = one_hot(lax.broadcasted_iota(jnp.int32, (2 * width, count), 0) == place)
    send_ref[...] = lax.dot_general(
        code_pick, slot_pick, (((1,), (1,)), ((), ())), preferred_element_type=jnp.float32
    ).astype(jnp.bfloat16)
    here = pltpu.roll(slots, lax.rem(count - chip * per_chip, count), 1)[:, :per_chip]
    owner = (here // (2 * width)) ^ chip
    marks = lax.broadcasted_iota(jnp.int32, (round_up(chips, 16), per_chip), 0) == owner
    rank = jnp.dot(
        one_hot(marks), earlier_in_chip(per_chip, per_chip), preferred_element_type=jnp.float32
    )
    rank = jnp.sum(jnp.where(marks, rank, 0.0), axis=0, keepdims=True).astype(jnp.int32)
    other = (owner > 0) & (owner < chips - 1) & (1 - owner % 2 != core)
    base = owner - jnp.where((owner > 0) & (owner < chips - 1), 1 - owner % 2, 0)
    code = (base + jnp.where(other, 1, 0)) * capacity + rank
    pick_ref[...] = one_hot(lax.broadcasted_iota(jnp.int32, pick_ref.shape, 0) == code)


def route_kernel(chips, send_ref, own_ref, other_ref, after_ref, *out_refs):
    capacity = send_ref.shape[0] // chips
    core = lax.rem(lax.axis_index("patch"), 2)
    width, components, _ = other_ref.shape
    tiles = other_ref[...].astype(jnp.float32)
    by_comp = []
    for comp in range(components):
        both = jnp.concatenate(
            [own_ref[comp * width : (comp + 1) * width, :], tiles[:, comp, :].astype(jnp.bfloat16)],
            axis=0,
        )
        chosen = jnp.dot(send_ref[...], both, preferred_element_type=jnp.float32)
        chosen = [chosen[step * capacity : (step + 1) * capacity] for step in range(chips)]
        sent = [chosen[0]]
        for step in range(1, chips - 1, 2):
            sent.append(jnp.where(core == 0, chosen[step], chosen[step + 1]))
        sent.append(chosen[-1])
        by_comp.append(sent)
    for values, out_ref in zip(zip(*by_comp), out_refs):
        out_ref[...] = jnp.concatenate(values, axis=0).astype(jnp.bfloat16)


def route_tiles(send, own, other, after, chips):
    components, lags = other.shape[1:]
    rows = components * send.shape[0] // chips
    shape = jax.ShapeDtypeStruct((rows, lags), jnp.bfloat16)
    return pl.pallas_call(
        functools.partial(route_kernel, chips),
        in_specs=[pl.BlockSpec(memory_space=pltpu.VMEM)] * 3
        + [pl.BlockSpec(memory_space=pl.ANY)],
        out_shape=(shape,) * (1 + chips // 2),
        compiler_params=params(),
        name="route_tiles",
    )(send, own, other, after)


def pass_on(value, *others):
    def kernel(*refs):
        pass

    return pl.pallas_call(
        kernel,
        in_specs=[pl.BlockSpec(memory_space=pl.ANY)] * (1 + len(others)),
        out_specs=pl.BlockSpec(memory_space=pl.ANY),
        out_shape=jax.ShapeDtypeStruct(value.shape, value.dtype),
        input_output_aliases={0: 0},
        compiler_params=params(),
        name="pass_on",
    )(value, *others)


def shift_kernel(pick_ref, *refs):
    pieces, out_ref = refs[:-1], refs[-1]
    count = pick_ref.shape[1]
    capacity = pick_ref.shape[0] // len(pieces)
    components = pieces[0].shape[0] // capacity
    lags = pieces[0].shape[1]
    span = out_ref.shape[1] // components
    tail = jnp.zeros((BLOCK, span - lags), jnp.float32)
    for comp in range(components):
        arrived = jnp.concatenate(
            [piece[comp * capacity : (comp + 1) * capacity, :] for piece in pieces], axis=0
        )
        tiles = lax.dot_general(
            pick_ref[...], arrived, (((0,), (0,)), ((), ())), preferred_element_type=jnp.float32
        )
        for patch in range(count):
            row = jnp.broadcast_to(tiles[patch : patch + 1], (BLOCK, lags))
            wide = jnp.concatenate([row, tail], axis=1)
            moved = pltpu.roll(wide, 0, 1, stride=1, stride_axis=0)
            out_ref[
                patch * BLOCK : (patch + 1) * BLOCK, comp * span : (comp + 1) * span
            ] = moved.astype(jnp.bfloat16)


def shift_tiles(pick, pieces, components):
    lags = pieces[0].shape[1]
    span = round_up(lags + BLOCK, LANES)
    shape = jax.ShapeDtypeStruct((pick.shape[1] * BLOCK, components * span), jnp.bfloat16)
    return pl.pallas_call(
        shift_kernel, out_shape=shape, compiler_params=params(), name="shift_tiles"
    )(pick, *pieces)


def convolve_blocks(shifted_ref, slip_refs, stack_ref, product_ref, out_ref, rows):
    length = out_ref.shape[2]
    components = out_ref.shape[1] // rows
    height = slip_refs[0].shape[0]
    width = shifted_ref.shape[1] // components
    per_reg = LANES // BLOCK
    blocks = height // rows
    for step, ref in enumerate(slip_refs):
        stack_ref[step * height : (step + 1) * height] = ref[...]
    for comp in range(components):
        product_ref[...] = jnp.dot(
            stack_ref[...],
            shifted_ref[:, comp * width : (comp + 1) * width],
            preferred_element_type=jnp.float32,
        )
        for step in range(len(slip_refs)):
            total = None
            for inner in range(per_reg):
                part = None
                for outer in range(inner, blocks, per_reg):
                    lead = outer // per_reg * LANES
                    start = step * height + outer * rows
                    block = product_ref[start : start + rows, :]
                    pieces = [jnp.zeros((rows, lead), jnp.float32)] if lead else []
                    pieces.append(block[:, : min(width, length - lead)])
                    if length > lead + width:
                        pieces.append(jnp.zeros((rows, length - lead - width), jnp.float32))
                    block = jnp.concatenate(pieces, axis=1) if len(pieces) > 1 else pieces[0]
                    part = block if part is None else part + block
                if inner:
                    part = pltpu.roll(part, inner * BLOCK, 1)
                total = part if total is None else total + part
            out_ref[step, comp * rows : (comp + 1) * rows, :] = total


def unit_of(exponent):
    return jnp.exp2(exponent.astype(jnp.float32) * (1.0 / STEPS)) * (1.0 / LARGEST)


def as_sent(total, lanes):
    peak = jnp.maximum(jnp.max(jnp.abs(total), axis=1, keepdims=True), SMALLEST)
    exponent = jnp.ceil(jnp.log2(peak) * STEPS).astype(jnp.int32)
    whole = jnp.clip(jnp.round(total * (1.0 / unit_of(exponent))), -LARGEST, LARGEST)
    rest = jnp.broadcast_to(exponent, (total.shape[0], lanes - total.shape[1]))
    return jnp.concatenate([whole.astype(jnp.int32), rest], axis=1).astype(jnp.int16)


def convolve_first_kernel(rows, shifted_ref, *refs):
    slip_refs, (out_ref, sent_ref, stack_ref, product_ref) = refs[:-4], refs[-4:]
    convolve_blocks(shifted_ref, slip_refs, stack_ref, product_ref, out_ref, rows)
    for step in range(out_ref.shape[0]):
        sent_ref[step] = as_sent(out_ref[step], sent_ref.shape[2])


def convolve_scratch(shifted, count, height, depth, components):
    return [
        pltpu.VMEM((count * height, depth), jnp.bfloat16),
        pltpu.VMEM((count * height, shifted.shape[1] // components), jnp.float32),
    ]


def convolve_first(shifted, slips, rows, components, length):
    size = (len(slips), components * rows)
    lanes = round_up(length, LANES) + LANES
    return pl.pallas_call(
        functools.partial(convolve_first_kernel, rows),
        out_shape=(
            jax.ShapeDtypeStruct(size + (length,), jnp.float32),
            jax.ShapeDtypeStruct(size + (lanes,), jnp.int16),
        ),
        scratch_shapes=convolve_scratch(shifted, len(slips), *slips[0].shape, components),
        compiler_params=params(),
        name="convolve_first",
    )(shifted, *slips)


def convolve_last_kernel(rows, shifted_ref, slip_ref, first_ref, early_ref, *refs):
    out_refs, (stack_ref, product_ref, last_ref) = refs[:-3], refs[-3:]
    convolve_blocks(shifted_ref, [slip_ref], stack_ref, product_ref, last_ref, rows)
    count = first_ref.shape[0]
    turn = lax.axis_index("site") ^ (lax.axis_index("patch") // 2)
    last = last_ref[0]
    late = as_sent(last, early_ref.shape[2])
    for step, ref in enumerate(out_refs):
        source = step ^ turn
        before = jnp.minimum(source, count - 1)

        @pl.when(source == count)
        def _():
            ref[...] = late if step else last

        @pl.when(source < count)
        def _():
            ref[...] = early_ref[before] if step else first_ref[before]


def convolve_last(shifted, slip, first, early, rows, components):
    count, height, length = first.shape
    own = jax.ShapeDtypeStruct((height, length), jnp.float32)
    sent = jax.ShapeDtypeStruct(early.shape[1:], jnp.int16)
    return pl.pallas_call(
        functools.partial(convolve_last_kernel, rows),
        out_shape=(own,) + (sent,) * count,
        scratch_shapes=convolve_scratch(shifted, 1, *slip.shape, components)
        + [pltpu.VMEM((1, height, length), jnp.float32)],
        compiler_params=params(),
        name="convolve_last",
    )(shifted, slip, first, early)


def add_kernel(own_ref, *refs):
    sent_refs, out_ref = refs[:-1], refs[-1]
    part, components, length = out_ref.shape
    rows = own_ref.shape[0] // components
    total = own_ref[...]
    for ref in sent_refs:
        unit = unit_of(ref[:, length:].astype(jnp.int32)[:, :1])
        total = total + ref[:, :length].astype(jnp.int32).astype(jnp.float32) * unit
    for comp in range(components):
        out_ref[:, comp, :] = total[comp * rows : comp * rows + part]


def add_up(own, sent, part, components):
    return pl.pallas_call(
        add_kernel,
        out_shape=jax.ShapeDtypeStruct((part, components, own.shape[1]), jnp.float32),
        compiler_params=params(),
        name="add_up",
    )(own, *sent)


def local(slip_rates, green_tiles, patch_slot):
    devices = lax.axis_size("patch")
    sites = lax.axis_size("site")
    chips = devices // 2
    patches, held, samples = slip_rates.shape
    components, lags = green_tiles.shape[2:]
    length = samples + lags
    part = held // 2
    rows = round_up(part, ROWS)
    assert chips == sites and sites & (sites - 1) == 0

    def over_patch(value, offset):
        return lax.ppermute(value, "patch", [(i, i ^ offset) for i in range(devices)])

    slips = slip_rates
    if rows > part:
        slips = slips.reshape(patches, 2, part, samples)
        slips = jnp.pad(slips, ((0, 0), (0, 0), (0, rows - part), (0, 0)))
        slips = slips.reshape(patches, 2 * rows, samples)
    greens = green_tiles[0]
    other_tiles, other = over_patch(greens, 1), over_patch(slips, 1)
    share = 2 * max(1, patches // devices)
    capacity = round_up(4 * share, 16)
    block, send, pick, own_tiles = arrange_own(
        slips, patch_slot.reshape(1, -1), greens, chips, 2 * patches, capacity
    )
    block = arrange_other(other, other_tiles, block)

    pieces = list(route_tiles(send, own_tiles, other_tiles, block, chips))
    arrived = [None] * (len(pieces) - 1)
    for index in reversed(range(len(arrived))):
        hops = [(2 * index + 1, 2 * index + 2), (chips - 1, chips - 1)][index == len(arrived) - 1]
        arrived[index] = lax.ppermute(
            pieces[1 + index], "patch", [(i, i ^ (2 * hops[i % 2])) for i in range(devices)]
        )
    pieces = pieces[:1]
    for piece in arrived[:-1]:
        pieces += [piece, over_patch(piece, 1)]
    pieces.append(arrived[-1])

    blocks = {0: block}
    for step in [2**i for i in range(sites.bit_length())] + list(range(sites)):
        if 0 < step < sites and step not in blocks:
            low = step & -step
            blocks[step] = lax.ppermute(
                blocks[step - low], "site", [(i, i ^ low) for i in range(sites)]
            )
            if step == sites // 2:
                blocks[step] = pass_on(pass_on(pass_on(blocks[step], arrived[-1]), arrived[-1]), *arrived)
    shifted = shift_tiles(pick, pieces, components)

    slips = [blocks[step] for step in range(sites)]
    first, early = convolve_first(shifted, slips[:-1], rows, components, length)
    sums = convolve_last(shifted, slips[-1], first, early, rows, components)
    order = list(range(1, chips))
    sent = [over_patch(sums[step], 2 * step) for step in order]
    return add_up(sums[0], sent, part, components)[None]


def solution(mesh):
    in_specs = (P("patch", "site", None), P("site", "patch", None, None), P())
    out_specs = P("site", "patch", None, None)
    return jax.shard_map(local, mesh=mesh, in_specs=in_specs, out_specs=out_specs, check_vma=False)
```

```python
import functools

import jax
import jax.numpy as jnp
from jax import lax
from jax.experimental import pallas as pl
from jax.experimental.pallas import tpu as pltpu
from jax.sharding import PartitionSpec as P

BLOCK = 16
LANES = 128
ROWS = 8
VMEM_LIMIT = 32 * 1024 * 1024
LARGEST = 32767.0
STEPS = 16
SMALLEST = 1e-30


def round_up(value, unit):
    return -(-value // unit) * unit


def params(limit=VMEM_LIMIT):
    return pltpu.CompilerParams(vmem_limit_bytes=limit)


def arrange_half(slip_ref, out_ref, core, owner):
    patches, both, samples = slip_ref.shape
    rows = both // 2
    per_reg = LANES // BLOCK
    blocks = samples // BLOCK
    depth = patches * BLOCK
    lane_block = lax.broadcasted_iota(jnp.int32, (rows, LANES), 1) // BLOCK
    for group in range(depth // LANES):
        done = {}
        for place in range(per_reg):
            full = slip_ref[group * per_reg + place].astype(jnp.float32)
            source = jnp.where(core == 0, full[:rows], full[rows:])
            for reg in range(samples // LANES):
                piece = source[:, reg * LANES : (reg + 1) * LANES]
                for inner in range(per_reg):
                    turn = (place - inner) % per_reg * BLOCK
                    moved = pltpu.roll(piece, turn, 1) if turn else piece
                    block = reg * per_reg + inner
                    if block in done:
                        moved = jnp.where(lane_block == place, moved, done[block])
                    done[block] = moved
        lanes = pl.ds(pl.multiple_of(owner * depth + group * LANES, LANES), LANES)
        for block in range(0, blocks, 2):
            pair = jnp.concatenate([done[block], done[block + 1]], axis=0)
            out_ref[block * rows : (block + 2) * rows, lanes] = pair.astype(jnp.bfloat16)


def arrange_own_kernel(
    chips,
    per_chip,
    capacity,
    slip_hbm,
    slots_hbm,
    green_hbm,
    out_ref,
    send_ref,
    pick_ref,
    tiles_ref,
    slip_ref,
    slots_ref,
    green_ref,
    sems,
):
    width = green_ref.shape[0]
    fetch_slips = pltpu.make_async_copy(slip_hbm, slip_ref, sems.at[0])
    fetch_slots = pltpu.make_async_copy(slots_hbm, slots_ref, sems.at[1])
    fetch_greens = pltpu.make_async_copy(green_hbm, green_ref, sems.at[2])
    fetch_slots.start()
    fetch_slips.start()
    fetch_greens.start()
    fetch_slots.wait()
    mark_tiles(chips, per_chip, capacity, width, slots_ref, send_ref, pick_ref)
    fetch_slips.wait()
    core = lax.rem(lax.axis_index("patch"), 2)
    arrange_half(slip_ref, out_ref, core, core)
    fetch_greens.wait()
    tiles = green_ref[...].astype(jnp.float32)
    for comp in range(green_ref.shape[1]):
        tiles_ref[comp * width : (comp + 1) * width, :] = tiles[:, comp, :].astype(jnp.bfloat16)


def arrange_other_kernel(slip_ref, green_ref, block_ref, out_ref):
    core = lax.rem(lax.axis_index("patch"), 2)
    arrange_half(slip_ref, out_ref, core, 1 - core)


def in_hbm(*values):
    return [pltpu.with_memory_space_constraint(value, pltpu.HBM) for value in values]


def arrange_own(slips, slots, greens, chips, per_chip, capacity):
    patches, both, samples = slips.shape
    width, components, lags = greens.shape
    block = jax.ShapeDtypeStruct(
        (samples // BLOCK * both // 2, 2 * patches * BLOCK), jnp.bfloat16
    )
    return pl.pallas_call(
        functools.partial(arrange_own_kernel, chips, per_chip, capacity),
        in_specs=[pl.BlockSpec(memory_space=pltpu.HBM)] * 3,
        out_shape=(
            block,
            jax.ShapeDtypeStruct((chips * capacity, 2 * width), jnp.bfloat16),
            jax.ShapeDtypeStruct((chips * capacity, per_chip), jnp.bfloat16),
            jax.ShapeDtypeStruct((components * width, lags), jnp.bfloat16),
        ),
        scratch_shapes=[
            pltpu.VMEM(slips.shape, slips.dtype),
            pltpu.VMEM(slots.shape, slots.dtype),
            pltpu.VMEM(greens.shape, greens.dtype),
            pltpu.SemaphoreType.DMA((3,)),
        ],
        compiler_params=params(),
        name="arrange_own",
    )(*in_hbm(slips, slots, greens))


def arrange_other(slips, greens, block):
    return pl.pallas_call(
        arrange_other_kernel,
        in_specs=[
            pl.BlockSpec(memory_space=pltpu.VMEM),
            pl.BlockSpec(memory_space=pl.ANY),
            pl.BlockSpec(memory_space=pltpu.VMEM),
        ],
        out_shape=jax.ShapeDtypeStruct(block.shape, block.dtype),
        input_output_aliases={2: 0},
        compiler_params=params(),
        name="arrange_other",
    )(slips, greens, block)


def earlier_in_chip(count, per_chip):
    q = lax.broadcasted_iota(jnp.int32, (count, count), 0)
    p = lax.broadcasted_iota(jnp.int32, (count, count), 1)
    return ((q < p) & (q // per_chip == p // per_chip)).astype(jnp.float32).astype(jnp.bfloat16)


def one_hot(condition):
    return condition.astype(jnp.float32).astype(jnp.bfloat16)


def mark_tiles(chips, per_chip, capacity, width, slots_ref, send_ref, pick_ref):
    count = slots_ref.shape[1]
    own = lax.axis_index("patch")
    chip, core = own // 2, lax.rem(own, 2)
    slots = slots_ref[...]
    owner = slots // width
    mine = owner // 2 == chip
    place = slots % width + jnp.where(owner % 2 == core, 0, width)
    marks = jnp.broadcast_to(one_hot(mine), (16, count))
    rank = jnp.dot(marks, earlier_in_chip(count, per_chip), preferred_element_type=jnp.float32)
    rank = rank[:1].astype(jnp.int32)
    target = (lax.broadcasted_iota(jnp.int32, (1, count), 1) // per_chip) ^ chip
    code = jnp.where(mine, target * capacity + rank, -1)
    code_pick = one_hot(lax.broadcasted_iota(jnp.int32, (chips * capacity, count), 0) == code)
    slot_pick = one_hot(lax.broadcasted_iota(jnp.int32, (2 * width, count), 0) == place)
    send_ref[...] = lax.dot_general(
        code_pick, slot_pick, (((1,), (1,)), ((), ())), preferred_element_type=jnp.float32
    ).astype(jnp.bfloat16)
    here = pltpu.roll(slots, lax.rem(count - chip * per_chip, count), 1)[:, :per_chip]
    owner = (here // (2 * width)) ^ chip
    marks = lax.broadcasted_iota(jnp.int32, (round_up(chips, 16), per_chip), 0) == owner
    rank = jnp.dot(
        one_hot(marks), earlier_in_chip(per_chip, per_chip), preferred_element_type=jnp.float32
    )
    rank = jnp.sum(jnp.where(marks, rank, 0.0), axis=0, keepdims=True).astype(jnp.int32)
    other = (owner > 0) & (owner < chips - 1) & (1 - owner % 2 != core)
    base = owner - jnp.where((owner > 0) & (owner < chips - 1), 1 - owner % 2, 0)
    code = (base + jnp.where(other, 1, 0)) * capacity + rank
    pick_ref[...] = one_hot(lax.broadcasted_iota(jnp.int32, pick_ref.shape, 0) == code)


def route_kernel(chips, send_ref, own_ref, other_ref, after_ref, *out_refs):
    capacity = send_ref.shape[0] // chips
    core = lax.rem(lax.axis_index("patch"), 2)
    width, components, _ = other_ref.shape
    tiles = other_ref[...].astype(jnp.float32)
    by_comp = []
    for comp in range(components):
        both = jnp.concatenate(
            [own_ref[comp * width : (comp + 1) * width, :], tiles[:, comp, :].astype(jnp.bfloat16)],
            axis=0,
        )
        chosen = jnp.dot(send_ref[...], both, preferred_element_type=jnp.float32)
        chosen = [chosen[step * capacity : (step + 1) * capacity] for step in range(chips)]
        sent = [chosen[0]]
        for step in range(1, chips - 1, 2):
            sent.append(jnp.where(core == 0, chosen[step], chosen[step + 1]))
        sent.append(chosen[-1])
        by_comp.append(sent)
    for values, out_ref in zip(zip(*by_comp), out_refs):
        out_ref[...] = jnp.concatenate(values, axis=0).astype(jnp.bfloat16)


def route_tiles(send, own, other, after, chips):
    components, lags = other.shape[1:]
    rows = components * send.shape[0] // chips
    shape = jax.ShapeDtypeStruct((rows, lags), jnp.bfloat16)
    return pl.pallas_call(
        functools.partial(route_kernel, chips),
        in_specs=[pl.BlockSpec(memory_space=pltpu.VMEM)] * 3
        + [pl.BlockSpec(memory_space=pl.ANY)],
        out_shape=(shape,) * (1 + chips // 2),
        compiler_params=params(),
        name="route_tiles",
    )(send, own, other, after)


def pass_on(value, *others):
    def kernel(*refs):
        pass

    return pl.pallas_call(
        kernel,
        in_specs=[pl.BlockSpec(memory_space=pl.ANY)] * (1 + len(others)),
        out_specs=pl.BlockSpec(memory_space=pl.ANY),
        out_shape=jax.ShapeDtypeStruct(value.shape, value.dtype),
        input_output_aliases={0: 0},
        compiler_params=params(),
        name="pass_on",
    )(value, *others)


def shift_kernel(pick_ref, *refs):
    pieces, out_ref = refs[:-1], refs[-1]
    count = pick_ref.shape[1]
    capacity = pick_ref.shape[0] // len(pieces)
    components = pieces[0].shape[0] // capacity
    lags = pieces[0].shape[1]
    span = out_ref.shape[1] // components
    tail = jnp.zeros((BLOCK, span - lags), jnp.float32)
    for comp in range(components):
        arrived = jnp.concatenate(
            [piece[comp * capacity : (comp + 1) * capacity, :] for piece in pieces], axis=0
        )
        tiles = lax.dot_general(
            pick_ref[...], arrived, (((0,), (0,)), ((), ())), preferred_element_type=jnp.float32
        )
        for patch in range(count):
            row = jnp.broadcast_to(tiles[patch : patch + 1], (BLOCK, lags))
            wide = jnp.concatenate([row, tail], axis=1)
            moved = pltpu.roll(wide, 0, 1, stride=1, stride_axis=0)
            out_ref[
                patch * BLOCK : (patch + 1) * BLOCK, comp * span : (comp + 1) * span
            ] = moved.astype(jnp.bfloat16)


def shift_tiles(pick, pieces, components):
    lags = pieces[0].shape[1]
    span = round_up(lags + BLOCK, LANES)
    shape = jax.ShapeDtypeStruct((pick.shape[1] * BLOCK, components * span), jnp.bfloat16)
    return pl.pallas_call(
        shift_kernel, out_shape=shape, compiler_params=params(), name="shift_tiles"
    )(pick, *pieces)


def convolve_blocks(shifted_ref, slip_refs, stack_ref, product_ref, out_ref, rows):
    length = out_ref.shape[2]
    components = out_ref.shape[1] // rows
    height = slip_refs[0].shape[0]
    width = shifted_ref.shape[1] // components
    per_reg = LANES // BLOCK
    blocks = height // rows
    for step, ref in enumerate(slip_refs):
        stack_ref[step * height : (step + 1) * height] = ref[...]
    for comp in range(components):
        product_ref[...] = jnp.dot(
            stack_ref[...],
            shifted_ref[:, comp * width : (comp + 1) * width],
            preferred_element_type=jnp.float32,
        )
        for step in range(len(slip_refs)):
            total = None
            for inner in range(per_reg):
                part = None
                for outer in range(inner, blocks, per_reg):
                    lead = outer // per_reg * LANES
                    start = step * height + outer * rows
                    block = product_ref[start : start + rows, :]
                    pieces = [jnp.zeros((rows, lead), jnp.float32)] if lead else []
                    pieces.append(block[:, : min(width, length - lead)])
                    if length > lead + width:
                        pieces.append(jnp.zeros((rows, length - lead - width), jnp.float32))
                    block = jnp.concatenate(pieces, axis=1) if len(pieces) > 1 else pieces[0]
                    part = block if part is None else part + block
                if inner:
                    part = pltpu.roll(part, inner * BLOCK, 1)
                total = part if total is None else total + part
            out_ref[step, comp * rows : (comp + 1) * rows, :] = total


def unit_of(exponent):
    return jnp.exp2(exponent.astype(jnp.float32) * (1.0 / STEPS)) * (1.0 / LARGEST)


def as_sent(total, lanes):
    peak = jnp.maximum(jnp.max(jnp.abs(total), axis=1, keepdims=True), SMALLEST)
    exponent = jnp.ceil(jnp.log2(peak) * STEPS).astype(jnp.int32)
    whole = jnp.clip(jnp.round(total * (1.0 / unit_of(exponent))), -LARGEST, LARGEST)
    rest = jnp.broadcast_to(exponent, (total.shape[0], lanes - total.shape[1]))
    return jnp.concatenate([whole.astype(jnp.int32), rest], axis=1).astype(jnp.int16)


def convolve_first_kernel(rows, shifted_ref, *refs):
    slip_refs, (out_ref, sent_ref, stack_ref, product_ref) = refs[:-4], refs[-4:]
    convolve_blocks(shifted_ref, slip_refs, stack_ref, product_ref, out_ref, rows)
    for step in range(out_ref.shape[0]):
        sent_ref[step] = as_sent(out_ref[step], sent_ref.shape[2])


def convolve_scratch(shifted, count, height, depth, components):
    return [
        pltpu.VMEM((count * height, depth), jnp.bfloat16),
        pltpu.VMEM((count * height, shifted.shape[1] // components), jnp.float32),
    ]


def convolve_first(shifted, slips, rows, components, length):
    size = (len(slips), components * rows)
    lanes = round_up(length, LANES) + LANES
    return pl.pallas_call(
        functools.partial(convolve_first_kernel, rows),
        out_shape=(
            jax.ShapeDtypeStruct(size + (length,), jnp.float32),
            jax.ShapeDtypeStruct(size + (lanes,), jnp.int16),
        ),
        scratch_shapes=convolve_scratch(shifted, len(slips), *slips[0].shape, components),
        compiler_params=params(),
        name="convolve_first",
    )(shifted, *slips)


def convolve_last_kernel(rows, shifted_ref, slip_ref, first_ref, early_ref, *refs):
    out_refs, (stack_ref, product_ref, last_ref) = refs[:-3], refs[-3:]
    convolve_blocks(shifted_ref, [slip_ref], stack_ref, product_ref, last_ref, rows)
    count = first_ref.shape[0]
    turn = lax.axis_index("site") ^ (lax.axis_index("patch") // 2)
    last = last_ref[0]
    late = as_sent(last, early_ref.shape[2])
    for step, ref in enumerate(out_refs):
        source = step ^ turn
        before = jnp.minimum(source, count - 1)

        @pl.when(source == count)
        def _():
            ref[...] = late if step else last

        @pl.when(source < count)
        def _():
            ref[...] = early_ref[before] if step else first_ref[before]


def convolve_last(shifted, slip, first, early, rows, components):
    count, height, length = first.shape
    own = jax.ShapeDtypeStruct((height, length), jnp.float32)
    sent = jax.ShapeDtypeStruct(early.shape[1:], jnp.int16)
    return pl.pallas_call(
        functools.partial(convolve_last_kernel, rows),
        out_shape=(own,) + (sent,) * count,
        scratch_shapes=convolve_scratch(shifted, 1, *slip.shape, components)
        + [pltpu.VMEM((1, height, length), jnp.float32)],
        compiler_params=params(),
        name="convolve_last",
    )(shifted, slip, first, early)


def add_kernel(own_ref, *refs):
    sent_refs, out_ref = refs[:-1], refs[-1]
    part, components, length = out_ref.shape
    rows = own_ref.shape[0] // components
    total = own_ref[...]
    for ref in sent_refs:
        unit = unit_of(ref[:, length:].astype(jnp.int32)[:, :1])
        total = total + ref[:, :length].astype(jnp.int32).astype(jnp.float32) * unit
    for comp in range(components):
        out_ref[:, comp, :] = total[comp * rows : comp * rows + part]


def add_up(own, sent, part, components):
    return pl.pallas_call(
        add_kernel,
        out_shape=jax.ShapeDtypeStruct((part, components, own.shape[1]), jnp.float32),
        compiler_params=params(),
        name="add_up",
    )(own, *sent)


def local(slip_rates, green_tiles, patch_slot):
    devices = lax.axis_size("patch")
    sites = lax.axis_size("site")
    chips = devices // 2
    patches, held, samples = slip_rates.shape
    components, lags = green_tiles.shape[2:]
    length = samples + lags
    part = held // 2
    rows = round_up(part, ROWS)
    assert chips == sites and sites & (sites - 1) == 0

    def over_patch(value, offset):
        return lax.ppermute(value, "patch", [(i, i ^ offset) for i in range(devices)])

    slips = slip_rates
    if rows > part:
        slips = slips.reshape(patches, 2, part, samples)
        slips = jnp.pad(slips, ((0, 0), (0, 0), (0, rows - part), (0, 0)))
        slips = slips.reshape(patches, 2 * rows, samples)
    greens = green_tiles[0]
    other_tiles, other = over_patch(greens, 1), over_patch(slips, 1)
    share = 2 * max(1, patches // devices)
    capacity = round_up(4 * share, 16)
    block, send, pick, own_tiles = arrange_own(
        slips, patch_slot.reshape(1, -1), greens, chips, 2 * patches, capacity
    )
    block = arrange_other(other, other_tiles, block)

    pieces = list(route_tiles(send, own_tiles, other_tiles, block, chips))
    arrived = [None] * (len(pieces) - 1)
    for index in reversed(range(len(arrived))):
        hops = [(2 * index + 1, 2 * index + 2), (chips - 1, chips - 1)][index == len(arrived) - 1]
        arrived[index] = lax.ppermute(
            pieces[1 + index], "patch", [(i, i ^ (2 * hops[i % 2])) for i in range(devices)]
        )
    pieces = pieces[:1]
    for piece in arrived[:-1]:
        piece = pass_on(piece, arrived[-1])
        pieces += [piece, over_patch(piece, 1)]
    pieces.append(arrived[-1])

    blocks = {0: block}
    for step in [2**i for i in range(sites.bit_length())] + list(range(sites)):
        if 0 < step < sites and step not in blocks:
            low = step & -step
            blocks[step] = lax.ppermute(
                blocks[step - low], "site", [(i, i ^ low) for i in range(sites)]
            )
    shifted = shift_tiles(pick, pieces, components)

    slips = [blocks[step] for step in range(sites)]
    first, early = convolve_first(shifted, slips[:-1], rows, components, length)
    sums = convolve_last(shifted, slips[-1], first, early, rows, components)
    order = list(range(1, chips))
    sent = [over_patch(sums[step], 2 * step) for step in order]
    return add_up(sums[0], sent, part, components)[None]


def solution(mesh):
    in_specs = (P("patch", "site", None), P("site", "patch", None, None), P())
    out_specs = P("site", "patch", None, None)
    return jax.shard_map(local, mesh=mesh, in_specs=in_specs, out_specs=out_specs, check_vma=False)
```

```python
import functools

import jax
import jax.numpy as jnp
from jax import lax
from jax.experimental import pallas as pl
from jax.experimental.pallas import tpu as pltpu
from jax.sharding import PartitionSpec as P

BLOCK = 16
LANES = 128
ROWS = 8
VMEM_LIMIT = 32 * 1024 * 1024
LARGEST = 32767.0
STEPS = 16
SMALLEST = 1e-30


def round_up(value, unit):
    return -(-value // unit) * unit


def params(limit=VMEM_LIMIT):
    return pltpu.CompilerParams(vmem_limit_bytes=limit)


def arrange_half(slip_ref, out_ref, core, owner):
    patches, both, samples = slip_ref.shape
    rows = both // 2
    per_reg = LANES // BLOCK
    blocks = samples // BLOCK
    depth = patches * BLOCK
    lane_block = lax.broadcasted_iota(jnp.int32, (rows, LANES), 1) // BLOCK
    for group in range(depth // LANES):
        done = {}
        for place in range(per_reg):
            full = slip_ref[group * per_reg + place].astype(jnp.float32)
            source = jnp.where(core == 0, full[:rows], full[rows:])
            for reg in range(samples // LANES):
                piece = source[:, reg * LANES : (reg + 1) * LANES]
                for inner in range(per_reg):
                    turn = (place - inner) % per_reg * BLOCK
                    moved = pltpu.roll(piece, turn, 1) if turn else piece
                    block = reg * per_reg + inner
                    if block in done:
                        moved = jnp.where(lane_block == place, moved, done[block])
                    done[block] = moved
        lanes = pl.ds(pl.multiple_of(owner * depth + group * LANES, LANES), LANES)
        for block in range(0, blocks, 2):
            pair = jnp.concatenate([done[block], done[block + 1]], axis=0)
            out_ref[block * rows : (block + 2) * rows, lanes] = pair.astype(jnp.bfloat16)


def arrange_own_kernel(
    chips,
    per_chip,
    capacity,
    slip_hbm,
    slots_hbm,
    green_hbm,
    out_ref,
    send_ref,
    pick_ref,
    green_ref,
    slip_ref,
    slots_ref,
    sems,
):
    width = green_ref.shape[0]
    fetch_slips = pltpu.make_async_copy(slip_hbm, slip_ref, sems.at[0])
    fetch_slots = pltpu.make_async_copy(slots_hbm, slots_ref, sems.at[1])
    fetch_greens = pltpu.make_async_copy(green_hbm, green_ref, sems.at[2])
    fetch_slots.start()
    fetch_slips.start()
    fetch_greens.start()
    fetch_slots.wait()
    mark_tiles(chips, per_chip, capacity, width, slots_ref, send_ref, pick_ref)
    fetch_slips.wait()
    core = lax.rem(lax.axis_index("patch"), 2)
    arrange_half(slip_ref, out_ref, core, core)
    fetch_greens.wait()


def arrange_other_kernel(slip_ref, block_ref, out_ref):
    core = lax.rem(lax.axis_index("patch"), 2)
    arrange_half(slip_ref, out_ref, core, 1 - core)


def in_hbm(*values):
    return [pltpu.with_memory_space_constraint(value, pltpu.HBM) for value in values]


def arrange_own(slips, slots, greens, chips, per_chip, capacity):
    patches, both, samples = slips.shape
    width = greens.shape[0]
    block = jax.ShapeDtypeStruct(
        (samples // BLOCK * both // 2, 2 * patches * BLOCK), jnp.bfloat16
    )
    return pl.pallas_call(
        functools.partial(arrange_own_kernel, chips, per_chip, capacity),
        in_specs=[pl.BlockSpec(memory_space=pltpu.HBM)] * 3,
        out_shape=(
            block,
            jax.ShapeDtypeStruct((chips * capacity, 2 * width), jnp.bfloat16),
            jax.ShapeDtypeStruct((chips * capacity, per_chip), jnp.bfloat16),
            jax.ShapeDtypeStruct(greens.shape, greens.dtype),
        ),
        scratch_shapes=[
            pltpu.VMEM(slips.shape, slips.dtype),
            pltpu.VMEM(slots.shape, slots.dtype),
            pltpu.SemaphoreType.DMA((3,)),
        ],
        compiler_params=params(),
        name="arrange_own",
    )(*in_hbm(slips, slots, greens))


def arrange_other(slips, block):
    return pl.pallas_call(
        arrange_other_kernel,
        out_shape=jax.ShapeDtypeStruct(block.shape, block.dtype),
        input_output_aliases={1: 0},
        compiler_params=params(),
        name="arrange_other",
    )(slips, block)


def earlier_in_chip(count, per_chip):
    q = lax.broadcasted_iota(jnp.int32, (count, count), 0)
    p = lax.broadcasted_iota(jnp.int32, (count, count), 1)
    return ((q < p) & (q // per_chip == p // per_chip)).astype(jnp.float32).astype(jnp.bfloat16)


def one_hot(condition):
    return condition.astype(jnp.float32).astype(jnp.bfloat16)


def mark_tiles(chips, per_chip, capacity, width, slots_ref, send_ref, pick_ref):
    count = slots_ref.shape[1]
    own = lax.axis_index("patch")
    chip, core = own // 2, lax.rem(own, 2)
    slots = slots_ref[...]
    owner = slots // width
    mine = owner // 2 == chip
    place = slots % width + jnp.where(owner % 2 == core, 0, width)
    marks = jnp.broadcast_to(one_hot(mine), (16, count))
    rank = jnp.dot(marks, earlier_in_chip(count, per_chip), preferred_element_type=jnp.float32)
    rank = rank[:1].astype(jnp.int32)
    target = (lax.broadcasted_iota(jnp.int32, (1, count), 1) // per_chip) ^ chip
    code = jnp.where(mine, target * capacity + rank, -1)
    code_pick = one_hot(lax.broadcasted_iota(jnp.int32, (chips * capacity, count), 0) == code)
    slot_pick = one_hot(lax.broadcasted_iota(jnp.int32, (2 * width, count), 0) == place)
    send_ref[...] = lax.dot_general(
        code_pick, slot_pick, (((1,), (1,)), ((), ())), preferred_element_type=jnp.float32
    ).astype(jnp.bfloat16)
    here = pltpu.roll(slots, lax.rem(count - chip * per_chip, count), 1)[:, :per_chip]
    owner = (here // (2 * width)) ^ chip
    marks = lax.broadcasted_iota(jnp.int32, (round_up(chips, 16), per_chip), 0) == owner
    rank = jnp.dot(
        one_hot(marks), earlier_in_chip(per_chip, per_chip), preferred_element_type=jnp.float32
    )
    rank = jnp.sum(jnp.where(marks, rank, 0.0), axis=0, keepdims=True).astype(jnp.int32)
    other = (owner > 0) & (owner < chips - 1) & (1 - owner % 2 != core)
    base = owner - jnp.where((owner > 0) & (owner < chips - 1), 1 - owner % 2, 0)
    code = (base + jnp.where(other, 1, 0)) * capacity + rank
    pick_ref[...] = one_hot(lax.broadcasted_iota(jnp.int32, pick_ref.shape, 0) == code)


def route_kernel(chips, send_ref, own_ref, other_ref, after_ref, *out_refs):
    capacity = send_ref.shape[0] // chips
    core = lax.rem(lax.axis_index("patch"), 2)
    tiles = jnp.concatenate([own_ref[...], other_ref[...]], axis=0).astype(jnp.float32)
    by_comp = []
    for comp in range(own_ref.shape[1]):
        both = tiles[:, comp, :].astype(jnp.bfloat16)
        chosen = jnp.dot(send_ref[...], both, preferred_element_type=jnp.float32)
        chosen = [chosen[step * capacity : (step + 1) * capacity] for step in range(chips)]
        sent = [chosen[0]]
        for step in range(1, chips - 1, 2):
            sent.append(jnp.where(core == 0, chosen[step], chosen[step + 1]))
        sent.append(chosen[-1])
        by_comp.append(sent)
    for values, out_ref in zip(zip(*by_comp), out_refs):
        out_ref[...] = jnp.concatenate(values, axis=0).astype(jnp.bfloat16)


def route_tiles(send, own, other, after, chips):
    components, lags = other.shape[1:]
    rows = components * send.shape[0] // chips
    shape = jax.ShapeDtypeStruct((rows, lags), jnp.bfloat16)
    return pl.pallas_call(
        functools.partial(route_kernel, chips),
        in_specs=[pl.BlockSpec(memory_space=pltpu.VMEM)] * 3
        + [pl.BlockSpec(memory_space=pl.ANY)],
        out_shape=(shape,) * (1 + chips // 2),
        compiler_params=params(),
        name="route_tiles",
    )(send, own, other, after)


def pass_on(value, *others):
    def kernel(*refs):
        pass

    return pl.pallas_call(
        kernel,
        in_specs=[pl.BlockSpec(memory_space=pl.ANY)] * (1 + len(others)),
        out_specs=pl.BlockSpec(memory_space=pl.ANY),
        out_shape=jax.ShapeDtypeStruct(value.shape, value.dtype),
        input_output_aliases={0: 0},
        compiler_params=params(),
        name="pass_on",
    )(value, *others)


def shift_kernel(pick_ref, *refs):
    pieces, out_ref = refs[:-1], refs[-1]
    count = pick_ref.shape[1]
    capacity = pick_ref.shape[0] // len(pieces)
    components = pieces[0].shape[0] // capacity
    lags = pieces[0].shape[1]
    span = out_ref.shape[1] // components
    tail = jnp.zeros((BLOCK, span - lags), jnp.float32)
    for comp in range(components):
        arrived = jnp.concatenate(
            [piece[comp * capacity : (comp + 1) * capacity, :] for piece in pieces], axis=0
        )
        tiles = lax.dot_general(
            pick_ref[...], arrived, (((0,), (0,)), ((), ())), preferred_element_type=jnp.float32
        )
        for patch in range(count):
            row = jnp.broadcast_to(tiles[patch : patch + 1], (BLOCK, lags))
            wide = jnp.concatenate([row, tail], axis=1)
            moved = pltpu.roll(wide, 0, 1, stride=1, stride_axis=0)
            out_ref[
                patch * BLOCK : (patch + 1) * BLOCK, comp * span : (comp + 1) * span
            ] = moved.astype(jnp.bfloat16)


def shift_tiles(pick, pieces, components):
    lags = pieces[0].shape[1]
    span = round_up(lags + BLOCK, LANES)
    shape = jax.ShapeDtypeStruct((pick.shape[1] * BLOCK, components * span), jnp.bfloat16)
    return pl.pallas_call(
        shift_kernel, out_shape=shape, compiler_params=params(), name="shift_tiles"
    )(pick, *pieces)


def convolve_blocks(shifted_ref, slip_refs, stack_ref, product_ref, out_ref, rows):
    length = out_ref.shape[2]
    components = out_ref.shape[1] // rows
    height = slip_refs[0].shape[0]
    width = shifted_ref.shape[1] // components
    per_reg = LANES // BLOCK
    blocks = height // rows
    for step, ref in enumerate(slip_refs):
        stack_ref[step * height : (step + 1) * height] = ref[...]
    for comp in range(components):
        product_ref[...] = jnp.dot(
            stack_ref[...],
            shifted_ref[:, comp * width : (comp + 1) * width],
            preferred_element_type=jnp.float32,
        )
        for step in range(len(slip_refs)):
            total = None
            for inner in range(per_reg):
                part = None
                for outer in range(inner, blocks, per_reg):
                    lead = outer // per_reg * LANES
                    start = step * height + outer * rows
                    block = product_ref[start : start + rows, :]
                    pieces = [jnp.zeros((rows, lead), jnp.float32)] if lead else []
                    pieces.append(block[:, : min(width, length - lead)])
                    if length > lead + width:
                        pieces.append(jnp.zeros((rows, length - lead - width), jnp.float32))
                    block = jnp.concatenate(pieces, axis=1) if len(pieces) > 1 else pieces[0]
                    part = block if part is None else part + block
                if inner:
                    part = pltpu.roll(part, inner * BLOCK, 1)
                total = part if total is None else total + part
            out_ref[step, comp * rows : (comp + 1) * rows, :] = total


def unit_of(exponent):
    return jnp.exp2(exponent.astype(jnp.float32) * (1.0 / STEPS)) * (1.0 / LARGEST)


def as_sent(total, lanes):
    peak = jnp.maximum(jnp.max(jnp.abs(total), axis=1, keepdims=True), SMALLEST)
    exponent = jnp.ceil(jnp.log2(peak) * STEPS).astype(jnp.int32)
    whole = jnp.clip(jnp.round(total * (1.0 / unit_of(exponent))), -LARGEST, LARGEST)
    rest = jnp.broadcast_to(exponent, (total.shape[0], lanes - total.shape[1]))
    return jnp.concatenate([whole.astype(jnp.int32), rest], axis=1).astype(jnp.int16)


def convolve_first_kernel(rows, shifted_ref, *refs):
    slip_refs, (out_ref, sent_ref, stack_ref, product_ref) = refs[:-4], refs[-4:]
    convolve_blocks(shifted_ref, slip_refs, stack_ref, product_ref, out_ref, rows)
    for step in range(out_ref.shape[0]):
        sent_ref[step] = as_sent(out_ref[step], sent_ref.shape[2])


def convolve_scratch(shifted, count, height, depth, components):
    return [
        pltpu.VMEM((count * height, depth), jnp.bfloat16),
        pltpu.VMEM((count * height, shifted.shape[1] // components), jnp.float32),
    ]


def convolve_first(shifted, slips, rows, components, length):
    size = (len(slips), components * rows)
    lanes = round_up(length, LANES) + LANES
    return pl.pallas_call(
        functools.partial(convolve_first_kernel, rows),
        out_shape=(
            jax.ShapeDtypeStruct(size + (length,), jnp.float32),
            jax.ShapeDtypeStruct(size + (lanes,), jnp.int16),
        ),
        scratch_shapes=convolve_scratch(shifted, len(slips), *slips[0].shape, components),
        compiler_params=params(),
        name="convolve_first",
    )(shifted, *slips)


def convolve_last_kernel(rows, shifted_ref, slip_ref, first_ref, early_ref, *refs):
    out_refs, (stack_ref, product_ref, last_ref) = refs[:-3], refs[-3:]
    convolve_blocks(shifted_ref, [slip_ref], stack_ref, product_ref, last_ref, rows)
    count = first_ref.shape[0]
    turn = lax.axis_index("site") ^ (lax.axis_index("patch") // 2)
    last = last_ref[0]
    late = as_sent(last, early_ref.shape[2])
    for step, ref in enumerate(out_refs):
        source = step ^ turn
        before = jnp.minimum(source, count - 1)

        @pl.when(source == count)
        def _():
            ref[...] = late if step else last

        @pl.when(source < count)
        def _():
            ref[...] = early_ref[before] if step else first_ref[before]


def convolve_last(shifted, slip, first, early, rows, components):
    count, height, length = first.shape
    own = jax.ShapeDtypeStruct((height, length), jnp.float32)
    sent = jax.ShapeDtypeStruct(early.shape[1:], jnp.int16)
    return pl.pallas_call(
        functools.partial(convolve_last_kernel, rows),
        out_shape=(own,) + (sent,) * count,
        scratch_shapes=convolve_scratch(shifted, 1, *slip.shape, components)
        + [pltpu.VMEM((1, height, length), jnp.float32)],
        compiler_params=params(),
        name="convolve_last",
    )(shifted, slip, first, early)


def add_kernel(own_ref, *refs):
    sent_refs, out_ref = refs[:-1], refs[-1]
    part, components, length = out_ref.shape
    rows = own_ref.shape[0] // components
    total = own_ref[...]
    for ref in sent_refs:
        unit = unit_of(ref[:, length:].astype(jnp.int32)[:, :1])
        total = total + ref[:, :length].astype(jnp.int32).astype(jnp.float32) * unit
    for comp in range(components):
        out_ref[:, comp, :] = total[comp * rows : comp * rows + part]


def add_up(own, sent, part, components):
    return pl.pallas_call(
        add_kernel,
        out_shape=jax.ShapeDtypeStruct((part, components, own.shape[1]), jnp.float32),
        compiler_params=params(),
        name="add_up",
    )(own, *sent)


def local(slip_rates, green_tiles, patch_slot):
    devices = lax.axis_size("patch")
    sites = lax.axis_size("site")
    chips = devices // 2
    patches, held, samples = slip_rates.shape
    components, lags = green_tiles.shape[2:]
    length = samples + lags
    part = held // 2
    rows = round_up(part, ROWS)
    assert chips == sites and sites & (sites - 1) == 0

    def over_patch(value, offset):
        return lax.ppermute(value, "patch", [(i, i ^ offset) for i in range(devices)])

    slips = slip_rates
    if rows > part:
        slips = slips.reshape(patches, 2, part, samples)
        slips = jnp.pad(slips, ((0, 0), (0, 0), (0, rows - part), (0, 0)))
        slips = slips.reshape(patches, 2 * rows, samples)
    greens = green_tiles[0]
    other_tiles, other = over_patch(greens, 1), over_patch(slips, 1)
    share = 2 * max(1, patches // devices)
    capacity = round_up(4 * share, 16)
    block, send, pick, own_tiles = arrange_own(
        slips, patch_slot.reshape(1, -1), greens, chips, 2 * patches, capacity
    )
    block = arrange_other(other, block)

    pieces = list(route_tiles(send, own_tiles, other_tiles, block, chips))
    arrived = [None] * (len(pieces) - 1)
    for index in reversed(range(len(arrived))):
        hops = [(2 * index + 1, 2 * index + 2), (chips - 1, chips - 1)][index == len(arrived) - 1]
        arrived[index] = lax.ppermute(
            pieces[1 + index], "patch", [(i, i ^ (2 * hops[i % 2])) for i in range(devices)]
        )
    pieces = pieces[:1]
    for piece in arrived[:-1]:
        piece = pass_on(piece, arrived[-1])
        pieces += [piece, over_patch(piece, 1)]
    pieces.append(arrived[-1])

    blocks = {0: block}
    for step in [2**i for i in range(sites.bit_length())] + list(range(sites)):
        if 0 < step < sites and step not in blocks:
            low = step & -step
            blocks[step] = lax.ppermute(
                blocks[step - low], "site", [(i, i ^ low) for i in range(sites)]
            )
    shifted = shift_tiles(pick, pieces, components)

    slips = [blocks[step] for step in range(sites)]
    first, early = convolve_first(shifted, slips[:-1], rows, components, length)
    sums = convolve_last(shifted, slips[-1], first, early, rows, components)
    order = list(range(1, chips))
    sent = [over_patch(sums[step], 2 * step) for step in order]
    return add_up(sums[0], sent, part, components)[None]


def solution(mesh):
    in_specs = (P("patch", "site", None), P("site", "patch", None, None), P())
    out_specs = P("site", "patch", None, None)
    return jax.shard_map(local, mesh=mesh, in_specs=in_specs, out_specs=out_specs, check_vma=False)
```

```python
import functools

import jax
import jax.numpy as jnp
from jax import lax
from jax.experimental import pallas as pl
from jax.experimental.pallas import tpu as pltpu
from jax.sharding import PartitionSpec as P

BLOCK = 16
LANES = 128
ROWS = 8
VMEM_LIMIT = 32 * 1024 * 1024
LARGEST = 32767.0
STEPS = 16
SMALLEST = 1e-30


def round_up(value, unit):
    return -(-value // unit) * unit


def params(limit=VMEM_LIMIT):
    return pltpu.CompilerParams(vmem_limit_bytes=limit)


def arrange_half(slip_ref, out_ref, core, owner):
    patches, both, samples = slip_ref.shape
    rows = both // 2
    per_reg = LANES // BLOCK
    blocks = samples // BLOCK
    depth = patches * BLOCK
    lane_block = lax.broadcasted_iota(jnp.int32, (rows, LANES), 1) // BLOCK
    for group in range(depth // LANES):
        done = {}
        for place in range(per_reg):
            full = slip_ref[group * per_reg + place].astype(jnp.float32)
            source = jnp.where(core == 0, full[:rows], full[rows:])
            for reg in range(samples // LANES):
                piece = source[:, reg * LANES : (reg + 1) * LANES]
                for inner in range(per_reg):
                    turn = (place - inner) % per_reg * BLOCK
                    moved = pltpu.roll(piece, turn, 1) if turn else piece
                    block = reg * per_reg + inner
                    if block in done:
                        moved = jnp.where(lane_block == place, moved, done[block])
                    done[block] = moved
        lanes = pl.ds(pl.multiple_of(owner * depth + group * LANES, LANES), LANES)
        for block in range(0, blocks, 2):
            pair = jnp.concatenate([done[block], done[block + 1]], axis=0)
            out_ref[block * rows : (block + 2) * rows, lanes] = pair.astype(jnp.bfloat16)


def arrange_own_kernel(
    chips,
    per_chip,
    capacity,
    slip_hbm,
    slots_hbm,
    green_hbm,
    out_ref,
    send_ref,
    pick_ref,
    green_ref,
    slip_ref,
    slots_ref,
    sems,
):
    width = green_ref.shape[0]
    fetch_slips = pltpu.make_async_copy(slip_hbm, slip_ref, sems.at[0])
    fetch_slots = pltpu.make_async_copy(slots_hbm, slots_ref, sems.at[1])
    fetch_greens = pltpu.make_async_copy(green_hbm, green_ref, sems.at[2])
    fetch_slots.start()
    fetch_slips.start()
    fetch_greens.start()
    fetch_slots.wait()
    mark_tiles(chips, per_chip, capacity, width, slots_ref, send_ref, pick_ref)
    fetch_slips.wait()
    core = lax.rem(lax.axis_index("patch"), 2)
    arrange_half(slip_ref, out_ref, core, core)
    fetch_greens.wait()


def arrange_other_kernel(slip_ref, block_ref, out_ref):
    core = lax.rem(lax.axis_index("patch"), 2)
    arrange_half(slip_ref, out_ref, core, 1 - core)


def in_hbm(*values):
    return [pltpu.with_memory_space_constraint(value, pltpu.HBM) for value in values]


def arrange_own(slips, slots, greens, chips, per_chip, capacity):
    patches, both, samples = slips.shape
    width = greens.shape[0]
    block = jax.ShapeDtypeStruct(
        (samples // BLOCK * both // 2, 2 * patches * BLOCK), jnp.bfloat16
    )
    return pl.pallas_call(
        functools.partial(arrange_own_kernel, chips, per_chip, capacity),
        in_specs=[pl.BlockSpec(memory_space=pltpu.HBM)] * 3,
        out_shape=(
            block,
            jax.ShapeDtypeStruct((chips * capacity, 2 * width), jnp.bfloat16),
            jax.ShapeDtypeStruct((chips * capacity, per_chip), jnp.bfloat16),
            jax.ShapeDtypeStruct(greens.shape, greens.dtype),
        ),
        scratch_shapes=[
            pltpu.VMEM(slips.shape, slips.dtype),
            pltpu.VMEM(slots.shape, slots.dtype),
            pltpu.SemaphoreType.DMA((3,)),
        ],
        compiler_params=params(),
        name="arrange_own",
    )(*in_hbm(slips, slots, greens))


def arrange_other(slips, block):
    return pl.pallas_call(
        arrange_other_kernel,
        out_shape=jax.ShapeDtypeStruct(block.shape, block.dtype),
        input_output_aliases={1: 0},
        compiler_params=params(),
        name="arrange_other",
    )(slips, block)


def earlier_in_chip(count, per_chip):
    q = lax.broadcasted_iota(jnp.int32, (count, count), 0)
    p = lax.broadcasted_iota(jnp.int32, (count, count), 1)
    return ((q < p) & (q // per_chip == p // per_chip)).astype(jnp.float32).astype(jnp.bfloat16)


def one_hot(condition):
    return condition.astype(jnp.float32).astype(jnp.bfloat16)


def mark_tiles(chips, per_chip, capacity, width, slots_ref, send_ref, pick_ref):
    half = capacity // 2
    count = slots_ref.shape[1]
    own = lax.axis_index("patch")
    chip, core = own // 2, lax.rem(own, 2)
    slots = slots_ref[...]
    owner = slots // width
    mine = owner // 2 == chip
    place = slots % width + jnp.where(owner % 2 == core, 0, width)
    marks = jnp.broadcast_to(one_hot(mine), (16, count))
    rank = jnp.dot(marks, earlier_in_chip(count, per_chip), preferred_element_type=jnp.float32)
    rank = rank[:1].astype(jnp.int32)
    target = (lax.broadcasted_iota(jnp.int32, (1, count), 1) // per_chip) ^ chip
    code = jnp.where(mine, target * capacity + rank, -1)
    code_pick = one_hot(lax.broadcasted_iota(jnp.int32, (chips * capacity, count), 0) == code)
    slot_pick = one_hot(lax.broadcasted_iota(jnp.int32, (2 * width, count), 0) == place)
    send_ref[...] = lax.dot_general(
        code_pick, slot_pick, (((1,), (1,)), ((), ())), preferred_element_type=jnp.float32
    ).astype(jnp.bfloat16)
    here = pltpu.roll(slots, lax.rem(count - chip * per_chip, count), 1)[:, :per_chip]
    owner = (here // (2 * width)) ^ chip
    marks = lax.broadcasted_iota(jnp.int32, (round_up(chips, 16), per_chip), 0) == owner
    rank = jnp.dot(
        one_hot(marks), earlier_in_chip(per_chip, per_chip), preferred_element_type=jnp.float32
    )
    rank = jnp.sum(jnp.where(marks, rank, 0.0), axis=0, keepdims=True).astype(jnp.int32)
    from_other = jnp.where(owner == chips - 1, rank // half, 1 - owner % 2) != core
    base = (owner - jnp.where(owner == chips - 1, 0, 1 - owner % 2)) * capacity
    code = base + jnp.where(
        owner == chips - 1,
        jnp.where(from_other, half, 0) + rank % half,
        jnp.where(from_other, capacity, 0) + rank,
    )
    code = jnp.where(owner == 0, rank, code)
    pick_ref[...] = one_hot(lax.broadcasted_iota(jnp.int32, pick_ref.shape, 0) == code)


def route_kernel(chips, send_ref, own_ref, other_ref, after_ref, *out_refs):
    capacity = send_ref.shape[0] // chips
    half = capacity // 2
    core = lax.rem(lax.axis_index("patch"), 2)
    tiles = jnp.concatenate([own_ref[...], other_ref[...]], axis=0).astype(jnp.float32)
    by_comp = []
    for comp in range(own_ref.shape[1]):
        both = tiles[:, comp, :].astype(jnp.bfloat16)
        chosen = jnp.dot(send_ref[...], both, preferred_element_type=jnp.float32)
        chosen = [chosen[step * capacity : (step + 1) * capacity] for step in range(chips)]
        last = chosen[-1]
        sent = [chosen[0]]
        for step in range(1, chips - 1, 2):
            sent.append(jnp.where(core == 0, chosen[step], chosen[step + 1]))
        sent.append(jnp.where(core == 0, last[:half], last[half:]))
        by_comp.append(sent)
    for values, out_ref in zip(zip(*by_comp), out_refs):
        out_ref[...] = jnp.concatenate(values, axis=0).astype(jnp.bfloat16)


def route_tiles(send, own, other, after, chips):
    components, lags = other.shape[1:]
    rows = components * send.shape[0] // chips
    shape = jax.ShapeDtypeStruct((rows, lags), jnp.bfloat16)
    part = jax.ShapeDtypeStruct((rows // 2, lags), jnp.bfloat16)
    return pl.pallas_call(
        functools.partial(route_kernel, chips),
        in_specs=[pl.BlockSpec(memory_space=pltpu.VMEM)] * 3
        + [pl.BlockSpec(memory_space=pl.ANY)],
        out_shape=(shape,) * (chips // 2) + (part,),
        compiler_params=params(),
        name="route_tiles",
    )(send, own, other, after)


def pass_on(value, *others):
    def kernel(*refs):
        pass

    return pl.pallas_call(
        kernel,
        in_specs=[pl.BlockSpec(memory_space=pl.ANY)] * (1 + len(others)),
        out_specs=pl.BlockSpec(memory_space=pl.ANY),
        out_shape=jax.ShapeDtypeStruct(value.shape, value.dtype),
        input_output_aliases={0: 0},
        compiler_params=params(),
        name="pass_on",
    )(value, *others)


def shift_kernel(pick_ref, *refs):
    pieces, out_ref = refs[:-1], refs[-1]
    count = pick_ref.shape[1]
    components = sum(piece.shape[0] for piece in pieces) // pick_ref.shape[0]
    lags = pieces[0].shape[1]
    span = out_ref.shape[1] // components
    tail = jnp.zeros((BLOCK, span - lags), jnp.float32)
    for comp in range(components):
        arrived = []
        for piece in pieces:
            size = piece.shape[0] // components
            arrived.append(piece[...].astype(jnp.float32)[comp * size : (comp + 1) * size])
        arrived = jnp.concatenate(arrived, axis=0).astype(jnp.bfloat16)
        tiles = lax.dot_general(
            pick_ref[...], arrived, (((0,), (0,)), ((), ())), preferred_element_type=jnp.float32
        )
        for patch in range(count):
            row = jnp.broadcast_to(tiles[patch : patch + 1], (BLOCK, lags))
            wide = jnp.concatenate([row, tail], axis=1)
            moved = pltpu.roll(wide, 0, 1, stride=1, stride_axis=0)
            out_ref[
                patch * BLOCK : (patch + 1) * BLOCK, comp * span : (comp + 1) * span
            ] = moved.astype(jnp.bfloat16)


def shift_tiles(pick, pieces, components):
    lags = pieces[0].shape[1]
    span = round_up(lags + BLOCK, LANES)
    shape = jax.ShapeDtypeStruct((pick.shape[1] * BLOCK, components * span), jnp.bfloat16)
    return pl.pallas_call(
        shift_kernel, out_shape=shape, compiler_params=params(), name="shift_tiles"
    )(pick, *pieces)


def convolve_blocks(shifted_ref, slip_refs, stack_ref, product_ref, out_ref, rows):
    length = out_ref.shape[2]
    components = out_ref.shape[1] // rows
    height = slip_refs[0].shape[0]
    width = shifted_ref.shape[1] // components
    per_reg = LANES // BLOCK
    blocks = height // rows
    for step, ref in enumerate(slip_refs):
        stack_ref[step * height : (step + 1) * height] = ref[...]
    for comp in range(components):
        product_ref[...] = jnp.dot(
            stack_ref[...],
            shifted_ref[:, comp * width : (comp + 1) * width],
            preferred_element_type=jnp.float32,
        )
        for step in range(len(slip_refs)):
            total = None
            for inner in range(per_reg):
                part = None
                for outer in range(inner, blocks, per_reg):
                    lead = outer // per_reg * LANES
                    start = step * height + outer * rows
                    block = product_ref[start : start + rows, :]
                    pieces = [jnp.zeros((rows, lead), jnp.float32)] if lead else []
                    pieces.append(block[:, : min(width, length - lead)])
                    if length > lead + width:
                        pieces.append(jnp.zeros((rows, length - lead - width), jnp.float32))
                    block = jnp.concatenate(pieces, axis=1) if len(pieces) > 1 else pieces[0]
                    part = block if part is None else part + block
                if inner:
                    part = pltpu.roll(part, inner * BLOCK, 1)
                total = part if total is None else total + part
            out_ref[step, comp * rows : (comp + 1) * rows, :] = total


def unit_of(exponent):
    return jnp.exp2(exponent.astype(jnp.float32) * (1.0 / STEPS)) * (1.0 / LARGEST)


def as_sent(total, lanes):
    peak = jnp.maximum(jnp.max(jnp.abs(total), axis=1, keepdims=True), SMALLEST)
    exponent = jnp.ceil(jnp.log2(peak) * STEPS).astype(jnp.int32)
    whole = jnp.clip(jnp.round(total * (1.0 / unit_of(exponent))), -LARGEST, LARGEST)
    rest = jnp.broadcast_to(exponent, (total.shape[0], lanes - total.shape[1]))
    return jnp.concatenate([whole.astype(jnp.int32), rest], axis=1).astype(jnp.int16)


def convolve_first_kernel(rows, shifted_ref, *refs):
    slip_refs, (out_ref, sent_ref, stack_ref, product_ref) = refs[:-4], refs[-4:]
    convolve_blocks(shifted_ref, slip_refs, stack_ref, product_ref, out_ref, rows)
    for step in range(out_ref.shape[0]):
        sent_ref[step] = as_sent(out_ref[step], sent_ref.shape[2])


def convolve_scratch(shifted, count, height, depth, components):
    return [
        pltpu.VMEM((count * height, depth), jnp.bfloat16),
        pltpu.VMEM((count * height, shifted.shape[1] // components), jnp.float32),
    ]


def convolve_first(shifted, slips, rows, components, length):
    size = (len(slips), components * rows)
    lanes = round_up(length, LANES) + LANES
    return pl.pallas_call(
        functools.partial(convolve_first_kernel, rows),
        out_shape=(
            jax.ShapeDtypeStruct(size + (length,), jnp.float32),
            jax.ShapeDtypeStruct(size + (lanes,), jnp.int16),
        ),
        scratch_shapes=convolve_scratch(shifted, len(slips), *slips[0].shape, components),
        compiler_params=params(),
        name="convolve_first",
    )(shifted, *slips)


def convolve_last_kernel(rows, shifted_ref, slip_ref, first_ref, early_ref, *refs):
    out_refs, (stack_ref, product_ref, last_ref) = refs[:-3], refs[-3:]
    convolve_blocks(shifted_ref, [slip_ref], stack_ref, product_ref, last_ref, rows)
    count = first_ref.shape[0]
    turn = lax.axis_index("site") ^ (lax.axis_index("patch") // 2)
    last = last_ref[0]
    late = as_sent(last, early_ref.shape[2])
    for step, ref in enumerate(out_refs):
        source = step ^ turn
        before = jnp.minimum(source, count - 1)

        @pl.when(source == count)
        def _():
            ref[...] = late if step else last

        @pl.when(source < count)
        def _():
            ref[...] = early_ref[before] if step else first_ref[before]


def convolve_last(shifted, slip, first, early, rows, components):
    count, height, length = first.shape
    own = jax.ShapeDtypeStruct((height, length), jnp.float32)
    sent = jax.ShapeDtypeStruct(early.shape[1:], jnp.int16)
    return pl.pallas_call(
        functools.partial(convolve_last_kernel, rows),
        out_shape=(own,) + (sent,) * count,
        scratch_shapes=convolve_scratch(shifted, 1, *slip.shape, components)
        + [pltpu.VMEM((1, height, length), jnp.float32)],
        compiler_params=params(),
        name="convolve_last",
    )(shifted, slip, first, early)


def add_kernel(own_ref, *refs):
    sent_refs, out_ref = refs[:-1], refs[-1]
    part, components, length = out_ref.shape
    rows = own_ref.shape[0] // components
    total = own_ref[...]
    for ref in sent_refs:
        unit = unit_of(ref[:, length:].astype(jnp.int32)[:, :1])
        total = total + ref[:, :length].astype(jnp.int32).astype(jnp.float32) * unit
    for comp in range(components):
        out_ref[:, comp, :] = total[comp * rows : comp * rows + part]


def add_up(own, sent, part, components):
    return pl.pallas_call(
        add_kernel,
        out_shape=jax.ShapeDtypeStruct((part, components, own.shape[1]), jnp.float32),
        compiler_params=params(),
        name="add_up",
    )(own, *sent)


def local(slip_rates, green_tiles, patch_slot):
    devices = lax.axis_size("patch")
    sites = lax.axis_size("site")
    chips = devices // 2
    patches, held, samples = slip_rates.shape
    components, lags = green_tiles.shape[2:]
    length = samples + lags
    part = held // 2
    rows = round_up(part, ROWS)
    assert chips == sites and sites & (sites - 1) == 0

    def over_patch(value, offset):
        return lax.ppermute(value, "patch", [(i, i ^ offset) for i in range(devices)])

    slips = slip_rates
    if rows > part:
        slips = slips.reshape(patches, 2, part, samples)
        slips = jnp.pad(slips, ((0, 0), (0, 0), (0, rows - part), (0, 0)))
        slips = slips.reshape(patches, 2 * rows, samples)
    greens = green_tiles[0]
    other_tiles, other = over_patch(greens, 1), over_patch(slips, 1)
    share = 2 * max(1, patches // devices)
    capacity = round_up(4 * share, 16)
    block, send, pick, own_tiles = arrange_own(
        slips, patch_slot.reshape(1, -1), greens, chips, 2 * patches, capacity
    )
    block = arrange_other(other, block)

    pieces = list(route_tiles(send, own_tiles, other_tiles, block, chips))
    arrived = [None] * (len(pieces) - 1)
    for index in reversed(range(len(arrived))):
        hops = [(2 * index + 1, 2 * index + 2), (chips - 1, chips - 1)][index == len(arrived) - 1]
        arrived[index] = lax.ppermute(
            pieces[1 + index], "patch", [(i, i ^ (2 * hops[i % 2])) for i in range(devices)]
        )
    pieces = pieces[:1]
    for piece in arrived:
        pieces += [piece, over_patch(piece, 1)]

    blocks = {0: block}
    for step in [2**i for i in range(sites.bit_length())] + list(range(sites)):
        if 0 < step < sites and step not in blocks:
            low = step & -step
            blocks[step] = lax.ppermute(
                blocks[step - low], "site", [(i, i ^ low) for i in range(sites)]
            )
            if step == sites // 2:
                blocks[step] = pass_on(blocks[step], *arrived)
    shifted = shift_tiles(pick, pieces, components)

    slips = [blocks[step] for step in range(sites)]
    first, early = convolve_first(shifted, slips[:-1], rows, components, length)
    sums = convolve_last(shifted, slips[-1], first, early, rows, components)
    order = [1, chips - 1] + list(range(2, chips - 1))
    sent = [over_patch(sums[step], 2 * step) for step in order]
    return add_up(sums[0], sent, part, components)[None]


def solution(mesh):
    in_specs = (P("patch", "site", None), P("site", "patch", None, None), P())
    out_specs = P("site", "patch", None, None)
    return jax.shard_map(local, mesh=mesh, in_specs=in_specs, out_specs=out_specs, check_vma=False)
```

```python
import functools

import jax
import jax.numpy as jnp
from jax import lax
from jax.experimental import pallas as pl
from jax.experimental.pallas import tpu as pltpu
from jax.sharding import PartitionSpec as P

BLOCK = 16
LANES = 128
ROWS = 8
VMEM_LIMIT = 32 * 1024 * 1024
LARGEST = 32767.0
STEPS = 16
SMALLEST = 1e-30


def round_up(value, unit):
    return -(-value // unit) * unit


def params(limit=VMEM_LIMIT):
    return pltpu.CompilerParams(vmem_limit_bytes=limit)


def arrange_half(slip_ref, out_ref, core, owner):
    patches, both, samples = slip_ref.shape
    rows = both // 2
    per_reg = LANES // BLOCK
    blocks = samples // BLOCK
    depth = patches * BLOCK
    lane_block = lax.broadcasted_iota(jnp.int32, (rows, LANES), 1) // BLOCK
    for group in range(depth // LANES):
        done = {}
        for place in range(per_reg):
            full = slip_ref[group * per_reg + place].astype(jnp.float32)
            source = jnp.where(core == 0, full[:rows], full[rows:])
            for reg in range(samples // LANES):
                piece = source[:, reg * LANES : (reg + 1) * LANES]
                for inner in range(per_reg):
                    turn = (place - inner) % per_reg * BLOCK
                    moved = pltpu.roll(piece, turn, 1) if turn else piece
                    block = reg * per_reg + inner
                    if block in done:
                        moved = jnp.where(lane_block == place, moved, done[block])
                    done[block] = moved
        lanes = pl.ds(pl.multiple_of(owner * depth + group * LANES, LANES), LANES)
        for block in range(0, blocks, 2):
            pair = jnp.concatenate([done[block], done[block + 1]], axis=0)
            out_ref[block * rows : (block + 2) * rows, lanes] = pair.astype(jnp.bfloat16)


def arrange_own_kernel(
    chips,
    per_chip,
    capacity,
    slip_hbm,
    slots_hbm,
    green_hbm,
    out_ref,
    send_ref,
    pick_ref,
    green_ref,
    slip_ref,
    slots_ref,
    sems,
):
    width = green_ref.shape[0]
    fetch_slips = pltpu.make_async_copy(slip_hbm, slip_ref, sems.at[0])
    fetch_slots = pltpu.make_async_copy(slots_hbm, slots_ref, sems.at[1])
    fetch_greens = pltpu.make_async_copy(green_hbm, green_ref, sems.at[2])
    fetch_slots.start()
    fetch_slips.start()
    fetch_greens.start()
    fetch_slots.wait()
    mark_tiles(chips, per_chip, capacity, width, slots_ref, send_ref, pick_ref)
    fetch_slips.wait()
    core = lax.rem(lax.axis_index("patch"), 2)
    arrange_half(slip_ref, out_ref, core, core)
    fetch_greens.wait()


def arrange_other_kernel(slip_ref, block_ref, out_ref):
    core = lax.rem(lax.axis_index("patch"), 2)
    arrange_half(slip_ref, out_ref, core, 1 - core)


def in_hbm(*values):
    return [pltpu.with_memory_space_constraint(value, pltpu.HBM) for value in values]


def arrange_own(slips, slots, greens, chips, per_chip, capacity):
    patches, both, samples = slips.shape
    width = greens.shape[0]
    block = jax.ShapeDtypeStruct(
        (samples // BLOCK * both // 2, 2 * patches * BLOCK), jnp.bfloat16
    )
    return pl.pallas_call(
        functools.partial(arrange_own_kernel, chips, per_chip, capacity),
        in_specs=[pl.BlockSpec(memory_space=pltpu.HBM)] * 3,
        out_shape=(
            block,
            jax.ShapeDtypeStruct((chips * capacity, 2 * width), jnp.bfloat16),
            jax.ShapeDtypeStruct((chips * capacity, per_chip), jnp.bfloat16),
            jax.ShapeDtypeStruct(greens.shape, greens.dtype),
        ),
        scratch_shapes=[
            pltpu.VMEM(slips.shape, slips.dtype),
            pltpu.VMEM(slots.shape, slots.dtype),
            pltpu.SemaphoreType.DMA((3,)),
        ],
        compiler_params=params(),
        name="arrange_own",
    )(*in_hbm(slips, slots, greens))


def arrange_other(slips, block):
    return pl.pallas_call(
        arrange_other_kernel,
        out_shape=jax.ShapeDtypeStruct(block.shape, block.dtype),
        input_output_aliases={1: 0},
        compiler_params=params(),
        name="arrange_other",
    )(slips, block)


def earlier_in_chip(count, per_chip):
    q = lax.broadcasted_iota(jnp.int32, (count, count), 0)
    p = lax.broadcasted_iota(jnp.int32, (count, count), 1)
    return ((q < p) & (q // per_chip == p // per_chip)).astype(jnp.float32).astype(jnp.bfloat16)


def one_hot(condition):
    return condition.astype(jnp.float32).astype(jnp.bfloat16)


def mark_tiles(chips, per_chip, capacity, width, slots_ref, send_ref, pick_ref):
    half = capacity // 2
    count = slots_ref.shape[1]
    own = lax.axis_index("patch")
    chip, core = own // 2, lax.rem(own, 2)
    slots = slots_ref[...]
    owner = slots // width
    mine = owner // 2 == chip
    place = slots % width + jnp.where(owner % 2 == core, 0, width)
    marks = jnp.broadcast_to(one_hot(mine), (16, count))
    rank = jnp.dot(marks, earlier_in_chip(count, per_chip), preferred_element_type=jnp.float32)
    rank = rank[:1].astype(jnp.int32)
    target = (lax.broadcasted_iota(jnp.int32, (1, count), 1) // per_chip) ^ chip
    code = jnp.where(mine, target * capacity + rank, -1)
    code_pick = one_hot(lax.broadcasted_iota(jnp.int32, (chips * capacity, count), 0) == code)
    slot_pick = one_hot(lax.broadcasted_iota(jnp.int32, (2 * width, count), 0) == place)
    send_ref[...] = lax.dot_general(
        code_pick, slot_pick, (((1,), (1,)), ((), ())), preferred_element_type=jnp.float32
    ).astype(jnp.bfloat16)
    here = pltpu.roll(slots, lax.rem(count - chip * per_chip, count), 1)[:, :per_chip]
    owner = (here // (2 * width)) ^ chip
    marks = lax.broadcasted_iota(jnp.int32, (round_up(chips, 16), per_chip), 0) == owner
    rank = jnp.dot(
        one_hot(marks), earlier_in_chip(per_chip, per_chip), preferred_element_type=jnp.float32
    )
    rank = jnp.sum(jnp.where(marks, rank, 0.0), axis=0, keepdims=True).astype(jnp.int32)
    from_other = jnp.where(owner == chips - 1, rank // half, 1 - owner % 2) != core
    base = (owner - jnp.where(owner == chips - 1, 0, 1 - owner % 2)) * capacity
    code = base + jnp.where(
        owner == chips - 1,
        jnp.where(from_other, half, 0) + rank % half,
        jnp.where(from_other, capacity, 0) + rank,
    )
    code = jnp.where(owner == 0, rank, code)
    pick_ref[...] = one_hot(lax.broadcasted_iota(jnp.int32, pick_ref.shape, 0) == code)


def route_kernel(chips, send_ref, own_ref, other_ref, after_ref, *out_refs):
    capacity = send_ref.shape[0] // chips
    half = capacity // 2
    core = lax.rem(lax.axis_index("patch"), 2)
    tiles = jnp.concatenate([own_ref[...], other_ref[...]], axis=0).astype(jnp.float32)
    by_comp = []
    for comp in range(own_ref.shape[1]):
        both = tiles[:, comp, :].astype(jnp.bfloat16)
        chosen = jnp.dot(send_ref[...], both, preferred_element_type=jnp.float32)
        chosen = [chosen[step * capacity : (step + 1) * capacity] for step in range(chips)]
        last = chosen[-1]
        sent = [chosen[0]]
        for step in range(1, chips - 1, 2):
            sent.append(jnp.where(core == 0, chosen[step], chosen[step + 1]))
        sent.append(jnp.where(core == 0, last[:half], last[half:]))
        by_comp.append(sent)
    for values, out_ref in zip(zip(*by_comp), out_refs):
        out_ref[...] = jnp.concatenate(values, axis=0).astype(jnp.bfloat16)


def route_tiles(send, own, other, after, chips):
    components, lags = other.shape[1:]
    rows = components * send.shape[0] // chips
    shape = jax.ShapeDtypeStruct((rows, lags), jnp.bfloat16)
    part = jax.ShapeDtypeStruct((rows // 2, lags), jnp.bfloat16)
    return pl.pallas_call(
        functools.partial(route_kernel, chips),
        in_specs=[pl.BlockSpec(memory_space=pltpu.VMEM)] * 3
        + [pl.BlockSpec(memory_space=pl.ANY)],
        out_shape=(shape,) * (chips // 2) + (part,),
        compiler_params=params(),
        name="route_tiles",
    )(send, own, other, after)


def pass_on(value, *others):
    def kernel(*refs):
        pass

    return pl.pallas_call(
        kernel,
        in_specs=[pl.BlockSpec(memory_space=pl.ANY)] * (1 + len(others)),
        out_specs=pl.BlockSpec(memory_space=pl.ANY),
        out_shape=jax.ShapeDtypeStruct(value.shape, value.dtype),
        input_output_aliases={0: 0},
        compiler_params=params(),
        name="pass_on",
    )(value, *others)


def shift_kernel(pick_ref, *refs):
    pieces, out_ref = refs[:-1], refs[-1]
    count = pick_ref.shape[1]
    components = sum(piece.shape[0] for piece in pieces) // pick_ref.shape[0]
    lags = pieces[0].shape[1]
    span = out_ref.shape[1] // components
    tail = jnp.zeros((BLOCK, span - lags), jnp.float32)
    for comp in range(components):
        arrived = []
        for piece in pieces:
            size = piece.shape[0] // components
            arrived.append(piece[...].astype(jnp.float32)[comp * size : (comp + 1) * size])
        arrived = jnp.concatenate(arrived, axis=0).astype(jnp.bfloat16)
        tiles = lax.dot_general(
            pick_ref[...], arrived, (((0,), (0,)), ((), ())), preferred_element_type=jnp.float32
        )
        for patch in range(count):
            row = jnp.broadcast_to(tiles[patch : patch + 1], (BLOCK, lags))
            wide = jnp.concatenate([row, tail], axis=1)
            moved = pltpu.roll(wide, 0, 1, stride=1, stride_axis=0)
            out_ref[
                patch * BLOCK : (patch + 1) * BLOCK, comp * span : (comp + 1) * span
            ] = moved.astype(jnp.bfloat16)


def shift_tiles(pick, pieces, components):
    lags = pieces[0].shape[1]
    span = round_up(lags + BLOCK, LANES)
    shape = jax.ShapeDtypeStruct((pick.shape[1] * BLOCK, components * span), jnp.bfloat16)
    return pl.pallas_call(
        shift_kernel, out_shape=shape, compiler_params=params(), name="shift_tiles"
    )(pick, *pieces)


def convolve_blocks(shifted_ref, slip_refs, stack_ref, product_ref, out_ref, rows):
    length = out_ref.shape[2]
    components = out_ref.shape[1] // rows
    height = slip_refs[0].shape[0]
    width = shifted_ref.shape[1] // components
    per_reg = LANES // BLOCK
    blocks = height // rows
    for step, ref in enumerate(slip_refs):
        stack_ref[step * height : (step + 1) * height] = ref[...]
    for comp in range(components):
        product_ref[comp] = jnp.dot(
            stack_ref[...],
            shifted_ref[:, comp * width : (comp + 1) * width],
            preferred_element_type=jnp.float32,
        )
    for comp in range(components):
        for step in range(len(slip_refs)):
            total = None
            for inner in range(per_reg):
                part = None
                for outer in range(inner, blocks, per_reg):
                    lead = outer // per_reg * LANES
                    start = step * height + outer * rows
                    block = product_ref[comp, start : start + rows, :]
                    pieces = [jnp.zeros((rows, lead), jnp.float32)] if lead else []
                    pieces.append(block[:, : min(width, length - lead)])
                    if length > lead + width:
                        pieces.append(jnp.zeros((rows, length - lead - width), jnp.float32))
                    block = jnp.concatenate(pieces, axis=1) if len(pieces) > 1 else pieces[0]
                    part = block if part is None else part + block
                if inner:
                    part = pltpu.roll(part, inner * BLOCK, 1)
                total = part if total is None else total + part
            out_ref[step, comp * rows : (comp + 1) * rows, :] = total


def unit_of(exponent):
    return jnp.exp2(exponent.astype(jnp.float32) * (1.0 / STEPS)) * (1.0 / LARGEST)


def as_sent(total, lanes):
    peak = jnp.maximum(jnp.max(jnp.abs(total), axis=1, keepdims=True), SMALLEST)
    exponent = jnp.ceil(jnp.log2(peak) * STEPS).astype(jnp.int32)
    whole = jnp.clip(jnp.round(total * (1.0 / unit_of(exponent))), -LARGEST, LARGEST)
    rest = jnp.broadcast_to(exponent, (total.shape[0], lanes - total.shape[1]))
    return jnp.concatenate([whole.astype(jnp.int32), rest], axis=1).astype(jnp.int16)


def convolve_first_kernel(rows, shifted_ref, *refs):
    slip_refs, (out_ref, sent_ref, stack_ref, product_ref) = refs[:-4], refs[-4:]
    convolve_blocks(shifted_ref, slip_refs, stack_ref, product_ref, out_ref, rows)
    for step in range(out_ref.shape[0]):
        sent_ref[step] = as_sent(out_ref[step], sent_ref.shape[2])


def convolve_scratch(shifted, count, height, depth, components):
    return [
        pltpu.VMEM((count * height, depth), jnp.bfloat16),
        pltpu.VMEM((components, count * height, shifted.shape[1] // components), jnp.float32),
    ]


def convolve_first(shifted, slips, rows, components, length):
    size = (len(slips), components * rows)
    lanes = round_up(length, LANES) + LANES
    return pl.pallas_call(
        functools.partial(convolve_first_kernel, rows),
        out_shape=(
            jax.ShapeDtypeStruct(size + (length,), jnp.float32),
            jax.ShapeDtypeStruct(size + (lanes,), jnp.int16),
        ),
        scratch_shapes=convolve_scratch(shifted, len(slips), *slips[0].shape, components),
        compiler_params=params(),
        name="convolve_first",
    )(shifted, *slips)


def convolve_last_kernel(rows, shifted_ref, slip_ref, first_ref, early_ref, *refs):
    out_refs, (stack_ref, product_ref, last_ref) = refs[:-3], refs[-3:]
    convolve_blocks(shifted_ref, [slip_ref], stack_ref, product_ref, last_ref, rows)
    count = first_ref.shape[0]
    turn = lax.axis_index("site") ^ (lax.axis_index("patch") // 2)
    last = last_ref[0]
    late = as_sent(last, early_ref.shape[2])
    for step, ref in enumerate(out_refs):
        source = step ^ turn
        before = jnp.minimum(source, count - 1)

        @pl.when(source == count)
        def _():
            ref[...] = late if step else last

        @pl.when(source < count)
        def _():
            ref[...] = early_ref[before] if step else first_ref[before]


def convolve_last(shifted, slip, first, early, rows, components):
    count, height, length = first.shape
    own = jax.ShapeDtypeStruct((height, length), jnp.float32)
    sent = jax.ShapeDtypeStruct(early.shape[1:], jnp.int16)
    return pl.pallas_call(
        functools.partial(convolve_last_kernel, rows),
        out_shape=(own,) + (sent,) * count,
        scratch_shapes=convolve_scratch(shifted, 1, *slip.shape, components)
        + [pltpu.VMEM((1, height, length), jnp.float32)],
        compiler_params=params(),
        name="convolve_last",
    )(shifted, slip, first, early)


def add_kernel(own_ref, *refs):
    sent_refs, out_ref = refs[:-1], refs[-1]
    part, components, length = out_ref.shape
    rows = own_ref.shape[0] // components
    total = own_ref[...]
    for ref in sent_refs:
        unit = unit_of(ref[:, length:].astype(jnp.int32)[:, :1])
        total = total + ref[:, :length].astype(jnp.int32).astype(jnp.float32) * unit
    for comp in range(components):
        out_ref[:, comp, :] = total[comp * rows : comp * rows + part]


def add_up(own, sent, part, components):
    return pl.pallas_call(
        add_kernel,
        out_shape=jax.ShapeDtypeStruct((part, components, own.shape[1]), jnp.float32),
        compiler_params=params(),
        name="add_up",
    )(own, *sent)


def local(slip_rates, green_tiles, patch_slot):
    devices = lax.axis_size("patch")
    sites = lax.axis_size("site")
    chips = devices // 2
    patches, held, samples = slip_rates.shape
    components, lags = green_tiles.shape[2:]
    length = samples + lags
    part = held // 2
    rows = round_up(part, ROWS)
    assert chips == sites and sites & (sites - 1) == 0

    def over_patch(value, offset):
        return lax.ppermute(value, "patch", [(i, i ^ offset) for i in range(devices)])

    slips = slip_rates
    if rows > part:
        slips = slips.reshape(patches, 2, part, samples)
        slips = jnp.pad(slips, ((0, 0), (0, 0), (0, rows - part), (0, 0)))
        slips = slips.reshape(patches, 2 * rows, samples)
    greens = green_tiles[0]
    other_tiles, other = over_patch(greens, 1), over_patch(slips, 1)
    share = 2 * max(1, patches // devices)
    capacity = round_up(4 * share, 16)
    block, send, pick, own_tiles = arrange_own(
        slips, patch_slot.reshape(1, -1), greens, chips, 2 * patches, capacity
    )
    block = arrange_other(other, block)

    pieces = list(route_tiles(send, own_tiles, other_tiles, block, chips))
    arrived = [None] * (len(pieces) - 1)
    for index in reversed(range(len(arrived))):
        hops = [(2 * index + 1, 2 * index + 2), (chips - 1, chips - 1)][index == len(arrived) - 1]
        arrived[index] = lax.ppermute(
            pieces[1 + index], "patch", [(i, i ^ (2 * hops[i % 2])) for i in range(devices)]
        )
    pieces = pieces[:1]
    for piece in arrived:
        pieces += [piece, over_patch(piece, 1)]

    blocks = {0: block}
    for step in [2**i for i in range(sites.bit_length())] + list(range(sites)):
        if 0 < step < sites and step not in blocks:
            low = step & -step
            blocks[step] = lax.ppermute(
                blocks[step - low], "site", [(i, i ^ low) for i in range(sites)]
            )
            if step == sites // 2:
                blocks[step] = pass_on(blocks[step], *arrived)
    shifted = shift_tiles(pick, pieces, components)

    slips = [blocks[step] for step in range(sites)]
    first, early = convolve_first(shifted, slips[:-1], rows, components, length)
    sums = convolve_last(shifted, slips[-1], first, early, rows, components)
    order = [1, chips - 1] + list(range(2, chips - 1))
    sent = [over_patch(sums[step], 2 * step) for step in order]
    return add_up(sums[0], sent, part, components)[None]


def solution(mesh):
    in_specs = (P("patch", "site", None), P("site", "patch", None, None), P())
    out_specs = P("site", "patch", None, None)
    return jax.shard_map(local, mesh=mesh, in_specs=in_specs, out_specs=out_specs, check_vma=False)
```

```python
import functools

import jax
import jax.numpy as jnp
from jax import lax
from jax.experimental import pallas as pl
from jax.experimental.pallas import tpu as pltpu
from jax.sharding import PartitionSpec as P

BLOCK = 16
LANES = 128
ROWS = 8
VMEM_LIMIT = 32 * 1024 * 1024
LARGEST = 32767.0
STEPS = 16
SMALLEST = 1e-30


def round_up(value, unit):
    return -(-value // unit) * unit


def params(limit=VMEM_LIMIT):
    return pltpu.CompilerParams(vmem_limit_bytes=limit)


def arrange_half(slip_ref, out_ref, core, owner):
    patches, both, samples = slip_ref.shape
    rows = both // 2
    per_reg = LANES // BLOCK
    blocks = samples // BLOCK
    depth = patches * BLOCK
    lane_block = lax.broadcasted_iota(jnp.int32, (rows, LANES), 1) // BLOCK
    for group in range(depth // LANES):
        done = {}
        for place in range(per_reg):
            full = slip_ref[group * per_reg + place].astype(jnp.float32)
            source = jnp.where(core == 0, full[:rows], full[rows:])
            for reg in range(samples // LANES):
                piece = source[:, reg * LANES : (reg + 1) * LANES]
                for inner in range(per_reg):
                    turn = (place - inner) % per_reg * BLOCK
                    moved = pltpu.roll(piece, turn, 1) if turn else piece
                    block = reg * per_reg + inner
                    if block in done:
                        moved = jnp.where(lane_block == place, moved, done[block])
                    done[block] = moved
        lanes = pl.ds(pl.multiple_of(owner * depth + group * LANES, LANES), LANES)
        for block in range(0, blocks, 2):
            pair = jnp.concatenate([done[block], done[block + 1]], axis=0)
            out_ref[block * rows : (block + 2) * rows, lanes] = pair.astype(jnp.bfloat16)


def arrange_own_kernel(
    chips,
    per_chip,
    capacity,
    slip_hbm,
    slots_hbm,
    green_hbm,
    out_ref,
    send_ref,
    pick_ref,
    green_ref,
    slip_ref,
    slots_ref,
    sems,
):
    width = green_ref.shape[0]
    fetch_slips = pltpu.make_async_copy(slip_hbm, slip_ref, sems.at[0])
    fetch_slots = pltpu.make_async_copy(slots_hbm, slots_ref, sems.at[1])
    fetch_greens = pltpu.make_async_copy(green_hbm, green_ref, sems.at[2])
    fetch_slots.start()
    fetch_slips.start()
    fetch_greens.start()
    fetch_slots.wait()
    mark_tiles(chips, per_chip, capacity, width, slots_ref, send_ref, pick_ref)
    fetch_slips.wait()
    core = lax.rem(lax.axis_index("patch"), 2)
    arrange_half(slip_ref, out_ref, core, core)
    fetch_greens.wait()


def arrange_other_kernel(slip_ref, block_ref, out_ref):
    core = lax.rem(lax.axis_index("patch"), 2)
    arrange_half(slip_ref, out_ref, core, 1 - core)


def in_hbm(*values):
    return [pltpu.with_memory_space_constraint(value, pltpu.HBM) for value in values]


def arrange_own(slips, slots, greens, chips, per_chip, capacity):
    patches, both, samples = slips.shape
    width = greens.shape[0]
    block = jax.ShapeDtypeStruct(
        (samples // BLOCK * both // 2, 2 * patches * BLOCK), jnp.bfloat16
    )
    return pl.pallas_call(
        functools.partial(arrange_own_kernel, chips, per_chip, capacity),
        in_specs=[pl.BlockSpec(memory_space=pltpu.HBM)] * 3,
        out_shape=(
            block,
            jax.ShapeDtypeStruct((chips * capacity, 2 * width), jnp.bfloat16),
            jax.ShapeDtypeStruct((chips * capacity, per_chip), jnp.bfloat16),
            jax.ShapeDtypeStruct(greens.shape, greens.dtype),
        ),
        scratch_shapes=[
            pltpu.VMEM(slips.shape, slips.dtype),
            pltpu.VMEM(slots.shape, slots.dtype),
            pltpu.SemaphoreType.DMA((3,)),
        ],
        compiler_params=params(),
        name="arrange_own",
    )(*in_hbm(slips, slots, greens))


def arrange_other(slips, block):
    return pl.pallas_call(
        arrange_other_kernel,
        out_shape=jax.ShapeDtypeStruct(block.shape, block.dtype),
        input_output_aliases={1: 0},
        compiler_params=params(),
        name="arrange_other",
    )(slips, block)


def earlier_in_chip(count, per_chip):
    q = lax.broadcasted_iota(jnp.int32, (count, count), 0)
    p = lax.broadcasted_iota(jnp.int32, (count, count), 1)
    return ((q < p) & (q // per_chip == p // per_chip)).astype(jnp.float32).astype(jnp.bfloat16)


def one_hot(condition):
    return condition.astype(jnp.float32).astype(jnp.bfloat16)


def mark_tiles(chips, per_chip, capacity, width, slots_ref, send_ref, pick_ref):
    half = capacity // 2
    count = slots_ref.shape[1]
    own = lax.axis_index("patch")
    chip, core = own // 2, lax.rem(own, 2)
    slots = slots_ref[...]
    owner = slots // width
    mine = owner // 2 == chip
    place = slots % width + jnp.where(owner % 2 == core, 0, width)
    marks = jnp.broadcast_to(one_hot(mine), (16, count))
    rank = jnp.dot(marks, earlier_in_chip(count, per_chip), preferred_element_type=jnp.float32)
    rank = rank[:1].astype(jnp.int32)
    target = (lax.broadcasted_iota(jnp.int32, (1, count), 1) // per_chip) ^ chip
    code = jnp.where(mine, target * capacity + rank, -1)
    code_pick = one_hot(lax.broadcasted_iota(jnp.int32, (chips * capacity, count), 0) == code)
    slot_pick = one_hot(lax.broadcasted_iota(jnp.int32, (2 * width, count), 0) == place)
    send_ref[...] = lax.dot_general(
        code_pick, slot_pick, (((1,), (1,)), ((), ())), preferred_element_type=jnp.float32
    ).astype(jnp.bfloat16)
    here = pltpu.roll(slots, lax.rem(count - chip * per_chip, count), 1)[:, :per_chip]
    owner = (here // (2 * width)) ^ chip
    marks = lax.broadcasted_iota(jnp.int32, (round_up(chips, 16), per_chip), 0) == owner
    rank = jnp.dot(
        one_hot(marks), earlier_in_chip(per_chip, per_chip), preferred_element_type=jnp.float32
    )
    rank = jnp.sum(jnp.where(marks, rank, 0.0), axis=0, keepdims=True).astype(jnp.int32)
    from_other = jnp.where(owner == chips - 1, rank // half, 1 - owner % 2) != core
    base = (owner - jnp.where(owner == chips - 1, 0, 1 - owner % 2)) * capacity
    code = base + jnp.where(
        owner == chips - 1,
        jnp.where(from_other, half, 0) + rank % half,
        jnp.where(from_other, capacity, 0) + rank,
    )
    code = jnp.where(owner == 0, rank, code)
    pick_ref[...] = one_hot(lax.broadcasted_iota(jnp.int32, pick_ref.shape, 0) == code)


def route_kernel(chips, send_ref, own_ref, other_ref, after_ref, *out_refs):
    capacity = send_ref.shape[0] // chips
    half = capacity // 2
    core = lax.rem(lax.axis_index("patch"), 2)
    tiles = jnp.concatenate([own_ref[...], other_ref[...]], axis=0).astype(jnp.float32)
    by_comp = []
    for comp in range(own_ref.shape[1]):
        both = tiles[:, comp, :].astype(jnp.bfloat16)
        chosen = jnp.dot(send_ref[...], both, preferred_element_type=jnp.float32)
        chosen = [chosen[step * capacity : (step + 1) * capacity] for step in range(chips)]
        last = chosen[-1]
        sent = [chosen[0]]
        for step in range(1, chips - 1, 2):
            sent.append(jnp.where(core == 0, chosen[step], chosen[step + 1]))
        sent.append(jnp.where(core == 0, last[:half], last[half:]))
        by_comp.append(sent)
    for values, out_ref in zip(zip(*by_comp), out_refs):
        out_ref[...] = jnp.concatenate(values, axis=0).astype(jnp.bfloat16)


def route_tiles(send, own, other, after, chips):
    components, lags = other.shape[1:]
    rows = components * send.shape[0] // chips
    shape = jax.ShapeDtypeStruct((rows, lags), jnp.bfloat16)
    part = jax.ShapeDtypeStruct((rows // 2, lags), jnp.bfloat16)
    return pl.pallas_call(
        functools.partial(route_kernel, chips),
        in_specs=[pl.BlockSpec(memory_space=pltpu.VMEM)] * 3
        + [pl.BlockSpec(memory_space=pl.ANY)],
        out_shape=(shape,) * (chips // 2) + (part,),
        compiler_params=params(),
        name="route_tiles",
    )(send, own, other, after)


def pass_on(value, *others):
    def kernel(*refs):
        pass

    return pl.pallas_call(
        kernel,
        in_specs=[pl.BlockSpec(memory_space=pl.ANY)] * (1 + len(others)),
        out_specs=pl.BlockSpec(memory_space=pl.ANY),
        out_shape=jax.ShapeDtypeStruct(value.shape, value.dtype),
        input_output_aliases={0: 0},
        compiler_params=params(),
        name="pass_on",
    )(value, *others)


def shift_kernel(pick_ref, *refs):
    pieces, out_ref = refs[:-1], refs[-1]
    count = pick_ref.shape[1]
    components = sum(piece.shape[0] for piece in pieces) // pick_ref.shape[0]
    lags = pieces[0].shape[1]
    span = out_ref.shape[1] // components
    tail = jnp.zeros((BLOCK, span - lags), jnp.float32)
    for comp in range(components):
        arrived = []
        for piece in pieces:
            size = piece.shape[0] // components
            arrived.append(piece[...].astype(jnp.float32)[comp * size : (comp + 1) * size])
        arrived = jnp.concatenate(arrived, axis=0).astype(jnp.bfloat16)
        tiles = lax.dot_general(
            pick_ref[...], arrived, (((0,), (0,)), ((), ())), preferred_element_type=jnp.float32
        )
        for patch in range(count):
            row = jnp.broadcast_to(tiles[patch : patch + 1], (BLOCK, lags))
            wide = jnp.concatenate([row, tail], axis=1)
            moved = pltpu.roll(wide, 0, 1, stride=1, stride_axis=0)
            out_ref[
                patch * BLOCK : (patch + 1) * BLOCK, comp * span : (comp + 1) * span
            ] = moved.astype(jnp.bfloat16)


def shift_tiles(pick, pieces, components):
    lags = pieces[0].shape[1]
    span = round_up(lags + BLOCK, LANES)
    shape = jax.ShapeDtypeStruct((pick.shape[1] * BLOCK, components * span), jnp.bfloat16)
    return pl.pallas_call(
        shift_kernel, out_shape=shape, compiler_params=params(), name="shift_tiles"
    )(pick, *pieces)


def convolve_blocks(shifted_ref, slip_refs, stack_ref, product_ref, out_ref, rows):
    length = out_ref.shape[2]
    components = out_ref.shape[1] // rows
    height = slip_refs[0].shape[0]
    width = shifted_ref.shape[1] // components
    per_reg = LANES // BLOCK
    blocks = height // rows
    for step, ref in enumerate(slip_refs):
        stack_ref[step * height : (step + 1) * height] = ref[...]
    for comp in range(components):
        product_ref[comp] = jnp.dot(
            stack_ref[...],
            shifted_ref[:, comp * width : (comp + 1) * width],
            preferred_element_type=jnp.float32,
        )
    for comp in range(components):
        for step in range(len(slip_refs)):
            total = None
            for inner in range(per_reg):
                part = None
                for outer in range(inner, blocks, per_reg):
                    lead = outer // per_reg * LANES
                    start = step * height + outer * rows
                    block = product_ref[comp, start : start + rows, :]
                    pieces = [jnp.zeros((rows, lead), jnp.float32)] if lead else []
                    pieces.append(block[:, : min(width, length - lead)])
                    if length > lead + width:
                        pieces.append(jnp.zeros((rows, length - lead - width), jnp.float32))
                    block = jnp.concatenate(pieces, axis=1) if len(pieces) > 1 else pieces[0]
                    part = block if part is None else part + block
                if inner:
                    part = pltpu.roll(part, inner * BLOCK, 1)
                total = part if total is None else total + part
            out_ref[step, comp * rows : (comp + 1) * rows, :] = total


def unit_of(exponent):
    return jnp.exp2(exponent.astype(jnp.float32) * (1.0 / STEPS)) * (1.0 / LARGEST)


def as_sent(total, lanes):
    peak = jnp.maximum(jnp.max(jnp.abs(total), axis=1, keepdims=True), SMALLEST)
    exponent = jnp.ceil(jnp.log2(peak) * STEPS).astype(jnp.int32)
    whole = jnp.clip(jnp.round(total * (1.0 / unit_of(exponent))), -LARGEST, LARGEST)
    rest = jnp.broadcast_to(exponent, (total.shape[0], lanes - total.shape[1]))
    return jnp.concatenate([whole.astype(jnp.int32), rest], axis=1).astype(jnp.int16)


def convolve_first_kernel(rows, shifted_ref, *refs):
    slip_refs, (out_ref, stack_ref, product_ref) = refs[:-3], refs[-3:]
    convolve_blocks(shifted_ref, slip_refs, stack_ref, product_ref, out_ref, rows)


def convolve_scratch(shifted, count, height, depth, components):
    return [
        pltpu.VMEM((count * height, depth), jnp.bfloat16),
        pltpu.VMEM((components, count * height, shifted.shape[1] // components), jnp.float32),
    ]


def convolve_first(shifted, slips, rows, components, length):
    shape = jax.ShapeDtypeStruct((len(slips), components * rows, length), jnp.float32)
    return pl.pallas_call(
        functools.partial(convolve_first_kernel, rows),
        out_shape=shape,
        scratch_shapes=convolve_scratch(shifted, len(slips), *slips[0].shape, components),
        compiler_params=params(),
        name="convolve_first",
    )(shifted, *slips)


def convolve_last_kernel(rows, shifted_ref, slip_ref, first_ref, *refs):
    out_refs, (stack_ref, product_ref, last_ref) = refs[:-3], refs[-3:]
    convolve_blocks(shifted_ref, [slip_ref], stack_ref, product_ref, last_ref, rows)
    count = first_ref.shape[0]
    turn = lax.axis_index("site") ^ (lax.axis_index("patch") // 2)
    last = last_ref[0]
    for step, ref in enumerate(out_refs):
        source = step ^ turn
        total = jnp.where(source == count, last, first_ref[jnp.minimum(source, count - 1)])
        ref[...] = as_sent(total, ref.shape[1]) if step else total


def convolve_last(shifted, slip, first, rows, components):
    count, height, length = first.shape
    own = jax.ShapeDtypeStruct((height, length), jnp.float32)
    sent = jax.ShapeDtypeStruct((height, round_up(length, LANES) + LANES), jnp.int16)
    return pl.pallas_call(
        functools.partial(convolve_last_kernel, rows),
        out_shape=(own,) + (sent,) * count,
        scratch_shapes=convolve_scratch(shifted, 1, *slip.shape, components)
        + [pltpu.VMEM((1, height, length), jnp.float32)],
        compiler_params=params(),
        name="convolve_last",
    )(shifted, slip, first)


def add_kernel(own_ref, *refs):
    sent_refs, out_ref = refs[:-1], refs[-1]
    part, components, length = out_ref.shape
    rows = own_ref.shape[0] // components
    total = own_ref[...]
    for ref in sent_refs:
        unit = unit_of(ref[:, length:].astype(jnp.int32)[:, :1])
        total = total + ref[:, :length].astype(jnp.int32).astype(jnp.float32) * unit
    for comp in range(components):
        out_ref[:, comp, :] = total[comp * rows : comp * rows + part]


def add_up(own, sent, part, components):
    return pl.pallas_call(
        add_kernel,
        out_shape=jax.ShapeDtypeStruct((part, components, own.shape[1]), jnp.float32),
        compiler_params=params(),
        name="add_up",
    )(own, *sent)


def local(slip_rates, green_tiles, patch_slot):
    devices = lax.axis_size("patch")
    sites = lax.axis_size("site")
    chips = devices // 2
    patches, held, samples = slip_rates.shape
    components, lags = green_tiles.shape[2:]
    length = samples + lags
    part = held // 2
    rows = round_up(part, ROWS)
    assert chips == sites and sites & (sites - 1) == 0

    def over_patch(value, offset):
        return lax.ppermute(value, "patch", [(i, i ^ offset) for i in range(devices)])

    slips = slip_rates
    if rows > part:
        slips = slips.reshape(patches, 2, part, samples)
        slips = jnp.pad(slips, ((0, 0), (0, 0), (0, rows - part), (0, 0)))
        slips = slips.reshape(patches, 2 * rows, samples)
    greens = green_tiles[0]
    other_tiles, other = over_patch(greens, 1), over_patch(slips, 1)
    share = 2 * max(1, patches // devices)
    capacity = round_up(4 * share, 16)
    block, send, pick, own_tiles = arrange_own(
        slips, patch_slot.reshape(1, -1), greens, chips, 2 * patches, capacity
    )
    block = arrange_other(other, block)

    pieces = list(route_tiles(send, own_tiles, other_tiles, block, chips))
    arrived = [None] * (len(pieces) - 1)
    for index in reversed(range(len(arrived))):
        hops = [(2 * index + 1, 2 * index + 2), (chips - 1, chips - 1)][index == len(arrived) - 1]
        arrived[index] = lax.ppermute(
            pieces[1 + index], "patch", [(i, i ^ (2 * hops[i % 2])) for i in range(devices)]
        )
    pieces = pieces[:1]
    for piece in arrived:
        pieces += [piece, over_patch(piece, 1)]

    blocks = {0: block}
    for step in [2**i for i in range(sites.bit_length())] + list(range(sites)):
        if 0 < step < sites and step not in blocks:
            low = step & -step
            blocks[step] = lax.ppermute(
                blocks[step - low], "site", [(i, i ^ low) for i in range(sites)]
            )
            if step == sites // 2:
                blocks[step] = pass_on(blocks[step], *arrived)
    shifted = shift_tiles(pick, pieces, components)

    slips = [blocks[step] for step in range(sites)]
    first = convolve_first(shifted, slips[:-1], rows, components, length)
    sums = convolve_last(shifted, slips[-1], first, rows, components)
    order = [1, chips - 1] + list(range(2, chips - 1))
    sent = [over_patch(sums[step], 2 * step) for step in order]
    return add_up(sums[0], sent, part, components)[None]


def solution(mesh):
    in_specs = (P("patch", "site", None), P("site", "patch", None, None), P())
    out_specs = P("site", "patch", None, None)
    return jax.shard_map(local, mesh=mesh, in_specs=in_specs, out_specs=out_specs, check_vma=False)
```

```python
import functools

import jax
import jax.numpy as jnp
from jax import lax
from jax.experimental import pallas as pl
from jax.experimental.pallas import tpu as pltpu
from jax.sharding import PartitionSpec as P

BLOCK = 16
LANES = 128
ROWS = 8
VMEM_LIMIT = 32 * 1024 * 1024
LARGEST = 32767.0
STEPS = 16
SMALLEST = 1e-30


def round_up(value, unit):
    return -(-value // unit) * unit


def params(limit=VMEM_LIMIT):
    return pltpu.CompilerParams(vmem_limit_bytes=limit)


def arrange_half(slip_ref, out_ref, core, owner):
    patches, both, samples = slip_ref.shape
    rows = both // 2
    per_reg = LANES // BLOCK
    blocks = samples // BLOCK
    depth = patches * BLOCK
    lane_block = lax.broadcasted_iota(jnp.int32, (rows, LANES), 1) // BLOCK
    for group in range(depth // LANES):
        done = {}
        for place in range(per_reg):
            full = slip_ref[group * per_reg + place].astype(jnp.float32)
            source = jnp.where(core == 0, full[:rows], full[rows:])
            for reg in range(samples // LANES):
                piece = source[:, reg * LANES : (reg + 1) * LANES]
                for inner in range(per_reg):
                    turn = (place - inner) % per_reg * BLOCK
                    moved = pltpu.roll(piece, turn, 1) if turn else piece
                    block = reg * per_reg + inner
                    if block in done:
                        moved = jnp.where(lane_block == place, moved, done[block])
                    done[block] = moved
        lanes = pl.ds(pl.multiple_of(owner * depth + group * LANES, LANES), LANES)
        for block in range(0, blocks, 2):
            pair = jnp.concatenate([done[block], done[block + 1]], axis=0)
            out_ref[block * rows : (block + 2) * rows, lanes] = pair.astype(jnp.bfloat16)


def arrange_own_kernel(
    chips,
    per_chip,
    capacity,
    slip_hbm,
    slots_hbm,
    green_hbm,
    out_ref,
    send_ref,
    pick_ref,
    green_ref,
    slip_ref,
    slots_ref,
    sems,
):
    width = green_ref.shape[0]
    fetch_slips = pltpu.make_async_copy(slip_hbm, slip_ref, sems.at[0])
    fetch_slots = pltpu.make_async_copy(slots_hbm, slots_ref, sems.at[1])
    fetch_greens = pltpu.make_async_copy(green_hbm, green_ref, sems.at[2])
    fetch_slots.start()
    fetch_slips.start()
    fetch_greens.start()
    fetch_slots.wait()
    mark_tiles(chips, per_chip, capacity, width, slots_ref, send_ref, pick_ref)
    fetch_slips.wait()
    core = lax.rem(lax.axis_index("patch"), 2)
    arrange_half(slip_ref, out_ref, core, core)
    fetch_greens.wait()


def arrange_other_kernel(slip_ref, block_ref, out_ref):
    core = lax.rem(lax.axis_index("patch"), 2)
    arrange_half(slip_ref, out_ref, core, 1 - core)


def in_hbm(*values):
    return [pltpu.with_memory_space_constraint(value, pltpu.HBM) for value in values]


def arrange_own(slips, slots, greens, chips, per_chip, capacity):
    patches, both, samples = slips.shape
    width = greens.shape[0]
    block = jax.ShapeDtypeStruct(
        (samples // BLOCK * both // 2, 2 * patches * BLOCK), jnp.bfloat16
    )
    return pl.pallas_call(
        functools.partial(arrange_own_kernel, chips, per_chip, capacity),
        in_specs=[pl.BlockSpec(memory_space=pltpu.HBM)] * 3,
        out_shape=(
            block,
            jax.ShapeDtypeStruct((chips * capacity, 2 * width), jnp.bfloat16),
            jax.ShapeDtypeStruct((chips * capacity, per_chip), jnp.bfloat16),
            jax.ShapeDtypeStruct(greens.shape, greens.dtype),
        ),
        scratch_shapes=[
            pltpu.VMEM(slips.shape, slips.dtype),
            pltpu.VMEM(slots.shape, slots.dtype),
            pltpu.SemaphoreType.DMA((3,)),
        ],
        compiler_params=params(),
        name="arrange_own",
    )(*in_hbm(slips, slots, greens))


def arrange_other(slips, block):
    return pl.pallas_call(
        arrange_other_kernel,
        out_shape=jax.ShapeDtypeStruct(block.shape, block.dtype),
        input_output_aliases={1: 0},
        compiler_params=params(),
        name="arrange_other",
    )(slips, block)


def earlier_in_chip(count, per_chip):
    q = lax.broadcasted_iota(jnp.int32, (count, count), 0)
    p = lax.broadcasted_iota(jnp.int32, (count, count), 1)
    return ((q < p) & (q // per_chip == p // per_chip)).astype(jnp.float32).astype(jnp.bfloat16)


def one_hot(condition):
    return condition.astype(jnp.float32).astype(jnp.bfloat16)


def mark_tiles(chips, per_chip, capacity, width, slots_ref, send_ref, pick_ref):
    count = slots_ref.shape[1]
    own = lax.axis_index("patch")
    chip, core = own // 2, lax.rem(own, 2)
    slots = slots_ref[...]
    owner = slots // width
    mine = owner // 2 == chip
    place = slots % width + jnp.where(owner % 2 == core, 0, width)
    marks = jnp.broadcast_to(one_hot(mine), (16, count))
    rank = jnp.dot(marks, earlier_in_chip(count, per_chip), preferred_element_type=jnp.float32)
    rank = rank[:1].astype(jnp.int32)
    target = (lax.broadcasted_iota(jnp.int32, (1, count), 1) // per_chip) ^ chip
    code = jnp.where(mine, target * capacity + rank, -1)
    code_pick = one_hot(lax.broadcasted_iota(jnp.int32, (chips * capacity, count), 0) == code)
    slot_pick = one_hot(lax.broadcasted_iota(jnp.int32, (2 * width, count), 0) == place)
    send_ref[...] = lax.dot_general(
        code_pick, slot_pick, (((1,), (1,)), ((), ())), preferred_element_type=jnp.float32
    ).astype(jnp.bfloat16)
    here = pltpu.roll(slots, lax.rem(count - chip * per_chip, count), 1)[:, :per_chip]
    owner = (here // (2 * width)) ^ chip
    marks = lax.broadcasted_iota(jnp.int32, (round_up(chips, 16), per_chip), 0) == owner
    rank = jnp.dot(
        one_hot(marks), earlier_in_chip(per_chip, per_chip), preferred_element_type=jnp.float32
    )
    rank = jnp.sum(jnp.where(marks, rank, 0.0), axis=0, keepdims=True).astype(jnp.int32)
    other = (owner > 0) & (owner < chips - 1) & (1 - owner % 2 != core)
    base = owner - jnp.where((owner > 0) & (owner < chips - 1), 1 - owner % 2, 0)
    code = (base + jnp.where(other, 1, 0)) * capacity + rank
    pick_ref[...] = one_hot(lax.broadcasted_iota(jnp.int32, pick_ref.shape, 0) == code)


def route_kernel(chips, send_ref, own_ref, other_ref, after_ref, *out_refs):
    capacity = send_ref.shape[0] // chips
    core = lax.rem(lax.axis_index("patch"), 2)
    tiles = jnp.concatenate([own_ref[...], other_ref[...]], axis=0).astype(jnp.float32)
    by_comp = []
    for comp in range(own_ref.shape[1]):
        both = tiles[:, comp, :].astype(jnp.bfloat16)
        chosen = jnp.dot(send_ref[...], both, preferred_element_type=jnp.float32)
        chosen = [chosen[step * capacity : (step + 1) * capacity] for step in range(chips)]
        sent = [chosen[0]]
        for step in range(1, chips - 1, 2):
            sent.append(jnp.where(core == 0, chosen[step], chosen[step + 1]))
        sent.append(chosen[-1])
        by_comp.append(sent)
    for values, out_ref in zip(zip(*by_comp), out_refs):
        out_ref[...] = jnp.concatenate(values, axis=0).astype(jnp.bfloat16)


def route_tiles(send, own, other, after, chips):
    components, lags = other.shape[1:]
    rows = components * send.shape[0] // chips
    shape = jax.ShapeDtypeStruct((rows, lags), jnp.bfloat16)
    return pl.pallas_call(
        functools.partial(route_kernel, chips),
        in_specs=[pl.BlockSpec(memory_space=pltpu.VMEM)] * 3
        + [pl.BlockSpec(memory_space=pl.ANY)],
        out_shape=(shape,) * (1 + chips // 2),
        compiler_params=params(),
        name="route_tiles",
    )(send, own, other, after)


def pass_on(value, *others):
    def kernel(*refs):
        pass

    return pl.pallas_call(
        kernel,
        in_specs=[pl.BlockSpec(memory_space=pl.ANY)] * (1 + len(others)),
        out_specs=pl.BlockSpec(memory_space=pl.ANY),
        out_shape=jax.ShapeDtypeStruct(value.shape, value.dtype),
        input_output_aliases={0: 0},
        compiler_params=params(),
        name="pass_on",
    )(value, *others)


def shift_kernel(pick_ref, *refs):
    pieces, out_ref = refs[:-1], refs[-1]
    count = pick_ref.shape[1]
    capacity = pick_ref.shape[0] // len(pieces)
    components = pieces[0].shape[0] // capacity
    lags = pieces[0].shape[1]
    span = out_ref.shape[1] // components
    tail = jnp.zeros((BLOCK, span - lags), jnp.float32)
    for comp in range(components):
        arrived = jnp.concatenate(
            [piece[comp * capacity : (comp + 1) * capacity, :] for piece in pieces], axis=0
        )
        tiles = lax.dot_general(
            pick_ref[...], arrived, (((0,), (0,)), ((), ())), preferred_element_type=jnp.float32
        )
        for patch in range(count):
            row = jnp.broadcast_to(tiles[patch : patch + 1], (BLOCK, lags))
            wide = jnp.concatenate([row, tail], axis=1)
            moved = pltpu.roll(wide, 0, 1, stride=1, stride_axis=0)
            out_ref[
                patch * BLOCK : (patch + 1) * BLOCK, comp * span : (comp + 1) * span
            ] = moved.astype(jnp.bfloat16)


def shift_tiles(pick, pieces, components):
    lags = pieces[0].shape[1]
    span = round_up(lags + BLOCK, LANES)
    shape = jax.ShapeDtypeStruct((pick.shape[1] * BLOCK, components * span), jnp.bfloat16)
    return pl.pallas_call(
        shift_kernel, out_shape=shape, compiler_params=params(), name="shift_tiles"
    )(pick, *pieces)


def convolve_blocks(shifted_ref, slip_refs, stack_ref, product_ref, out_ref, rows):
    length = out_ref.shape[2]
    components = out_ref.shape[1] // rows
    height = slip_refs[0].shape[0]
    width = shifted_ref.shape[1] // components
    per_reg = LANES // BLOCK
    blocks = height // rows
    for step, ref in enumerate(slip_refs):
        stack_ref[step * height : (step + 1) * height] = ref[...]
    for comp in range(components):
        product_ref[...] = jnp.dot(
            stack_ref[...],
            shifted_ref[:, comp * width : (comp + 1) * width],
            preferred_element_type=jnp.float32,
        )
        for step in range(len(slip_refs)):
            total = None
            for inner in range(per_reg):
                part = None
                for outer in range(inner, blocks, per_reg):
                    lead = outer // per_reg * LANES
                    start = step * height + outer * rows
                    block = product_ref[start : start + rows, :]
                    pieces = [jnp.zeros((rows, lead), jnp.float32)] if lead else []
                    pieces.append(block[:, : min(width, length - lead)])
                    if length > lead + width:
                        pieces.append(jnp.zeros((rows, length - lead - width), jnp.float32))
                    block = jnp.concatenate(pieces, axis=1) if len(pieces) > 1 else pieces[0]
                    part = block if part is None else part + block
                if inner:
                    part = pltpu.roll(part, inner * BLOCK, 1)
                total = part if total is None else total + part
            out_ref[step, comp * rows : (comp + 1) * rows, :] = total


def unit_of(exponent):
    return jnp.exp2(exponent.astype(jnp.float32) * (1.0 / STEPS)) * (1.0 / LARGEST)


def as_sent(total, lanes):
    peak = jnp.maximum(jnp.max(jnp.abs(total), axis=1, keepdims=True), SMALLEST)
    exponent = jnp.ceil(jnp.log2(peak) * STEPS).astype(jnp.int32)
    whole = jnp.clip(jnp.round(total * (1.0 / unit_of(exponent))), -LARGEST, LARGEST)
    rest = jnp.broadcast_to(exponent, (total.shape[0], lanes - total.shape[1]))
    return jnp.concatenate([whole.astype(jnp.int32), rest], axis=1).astype(jnp.int16)


def convolve_first_kernel(rows, shifted_ref, *refs):
    slip_refs, (out_ref, sent_ref, stack_ref, product_ref) = refs[:-4], refs[-4:]
    convolve_blocks(shifted_ref, slip_refs, stack_ref, product_ref, out_ref, rows)
    for step in range(out_ref.shape[0]):
        sent_ref[step] = as_sent(out_ref[step], sent_ref.shape[2])


def convolve_scratch(shifted, count, height, depth, components):
    return [
        pltpu.VMEM((count * height, depth), jnp.bfloat16),
        pltpu.VMEM((count * height, shifted.shape[1] // components), jnp.float32),
    ]


def convolve_first(shifted, slips, rows, components, length):
    size = (len(slips), components * rows)
    lanes = round_up(length, LANES) + LANES
    return pl.pallas_call(
        functools.partial(convolve_first_kernel, rows),
        out_shape=(
            jax.ShapeDtypeStruct(size + (length,), jnp.float32),
            jax.ShapeDtypeStruct(size + (lanes,), jnp.int16),
        ),
        scratch_shapes=convolve_scratch(shifted, len(slips), *slips[0].shape, components),
        compiler_params=params(),
        name="convolve_first",
    )(shifted, *slips)


def convolve_last_kernel(rows, shifted_ref, slip_ref, first_ref, early_ref, *refs):
    out_refs, (stack_ref, product_ref, last_ref) = refs[:-3], refs[-3:]
    convolve_blocks(shifted_ref, [slip_ref], stack_ref, product_ref, last_ref, rows)
    count = first_ref.shape[0]
    turn = lax.axis_index("site") ^ (lax.axis_index("patch") // 2)
    last = last_ref[0]
    late = as_sent(last, early_ref.shape[2])
    for step, ref in enumerate(out_refs):
        source = step ^ turn
        before = jnp.minimum(source, count - 1)

        @pl.when(source == count)
        def _():
            ref[...] = late if step else last

        @pl.when(source < count)
        def _():
            ref[...] = early_ref[before] if step else first_ref[before]


def convolve_last(shifted, slip, first, early, rows, components):
    count, height, length = first.shape
    own = jax.ShapeDtypeStruct((height, length), jnp.float32)
    sent = jax.ShapeDtypeStruct(early.shape[1:], jnp.int16)
    return pl.pallas_call(
        functools.partial(convolve_last_kernel, rows),
        out_shape=(own,) + (sent,) * count,
        scratch_shapes=convolve_scratch(shifted, 1, *slip.shape, components)
        + [pltpu.VMEM((1, height, length), jnp.float32)],
        compiler_params=params(),
        name="convolve_last",
    )(shifted, slip, first, early)


def add_kernel(own_ref, *refs):
    sent_refs, out_ref = refs[:-1], refs[-1]
    part, components, length = out_ref.shape
    rows = own_ref.shape[0] // components
    total = own_ref[...]
    for ref in sent_refs:
        unit = unit_of(ref[:, length:].astype(jnp.int32)[:, :1])
        total = total + ref[:, :length].astype(jnp.int32).astype(jnp.float32) * unit
    for comp in range(components):
        out_ref[:, comp, :] = total[comp * rows : comp * rows + part]


def add_up(own, sent, part, components):
    return pl.pallas_call(
        add_kernel,
        out_shape=jax.ShapeDtypeStruct((part, components, own.shape[1]), jnp.float32),
        compiler_params=params(),
        name="add_up",
    )(own, *sent)


def local(slip_rates, green_tiles, patch_slot):
    devices = lax.axis_size("patch")
    sites = lax.axis_size("site")
    chips = devices // 2
    patches, held, samples = slip_rates.shape
    components, lags = green_tiles.shape[2:]
    length = samples + lags
    part = held // 2
    rows = round_up(part, ROWS)
    assert chips == sites and sites & (sites - 1) == 0

    def over_patch(value, offset):
        return lax.ppermute(value, "patch", [(i, i ^ offset) for i in range(devices)])

    slips = slip_rates
    if rows > part:
        slips = slips.reshape(patches, 2, part, samples)
        slips = jnp.pad(slips, ((0, 0), (0, 0), (0, rows - part), (0, 0)))
        slips = slips.reshape(patches, 2 * rows, samples)
    greens = green_tiles[0]
    other_tiles, other = over_patch(greens, 1), over_patch(slips, 1)
    share = 2 * max(1, patches // devices)
    capacity = round_up(4 * share, 16)
    block, send, pick, own_tiles = arrange_own(
        slips, patch_slot.reshape(1, -1), greens, chips, 2 * patches, capacity
    )
    block = arrange_other(other, block)

    pieces = list(route_tiles(send, own_tiles, other_tiles, block, chips))
    arrived = [None] * (len(pieces) - 1)
    for index in reversed(range(len(arrived))):
        hops = [(2 * index + 1, 2 * index + 2), (chips - 1, chips - 1)][index == len(arrived) - 1]
        arrived[index] = lax.ppermute(
            pieces[1 + index], "patch", [(i, i ^ (2 * hops[i % 2])) for i in range(devices)]
        )
    pieces = pieces[:1]
    for piece in arrived[:-1]:
        pieces += [piece, over_patch(piece, 1)]
    pieces.append(arrived[-1])

    blocks = {0: block}
    for step in [2**i for i in range(sites.bit_length())] + list(range(sites)):
        if 0 < step < sites and step not in blocks:
            low = step & -step
            blocks[step] = lax.ppermute(
                blocks[step - low], "site", [(i, i ^ low) for i in range(sites)]
            )
            if step == sites // 2:
                blocks[step] = pass_on(pass_on(pass_on(pass_on(blocks[step], arrived[-1]), arrived[-1]), arrived[-1]), *pieces[1:-1])
    shifted = shift_tiles(pick, pieces, components)

    slips = [blocks[step] for step in range(sites)]
    first, early = convolve_first(shifted, slips[:-1], rows, components, length)
    sums = convolve_last(shifted, slips[-1], first, early, rows, components)
    order = [1, chips - 1] + list(range(2, chips - 1))
    sent = [over_patch(sums[step], 2 * step) for step in order]
    return add_up(sums[0], sent, part, components)[None]


def solution(mesh):
    in_specs = (P("patch", "site", None), P("site", "patch", None, None), P())
    out_specs = P("site", "patch", None, None)
    return jax.shard_map(local, mesh=mesh, in_specs=in_specs, out_specs=out_specs, check_vma=False)
```

```python
import functools

import jax
import jax.numpy as jnp
from jax import lax
from jax.experimental import pallas as pl
from jax.experimental.pallas import tpu as pltpu
from jax.sharding import PartitionSpec as P

BLOCK = 16
LANES = 128
ROWS = 8
VMEM_LIMIT = 32 * 1024 * 1024
LARGEST = 32767.0
STEPS = 16
SMALLEST = 1e-30


def round_up(value, unit):
    return -(-value // unit) * unit


def params(limit=VMEM_LIMIT):
    return pltpu.CompilerParams(vmem_limit_bytes=limit)


def arrange_half(slip_ref, out_ref, core, owner):
    patches, both, samples = slip_ref.shape
    rows = both // 2
    per_reg = LANES // BLOCK
    blocks = samples // BLOCK
    depth = patches * BLOCK
    lane_block = lax.broadcasted_iota(jnp.int32, (rows, LANES), 1) // BLOCK
    for group in range(depth // LANES):
        done = {}
        for place in range(per_reg):
            full = slip_ref[group * per_reg + place].astype(jnp.float32)
            source = jnp.where(core == 0, full[:rows], full[rows:])
            for reg in range(samples // LANES):
                piece = source[:, reg * LANES : (reg + 1) * LANES]
                for inner in range(per_reg):
                    turn = (place - inner) % per_reg * BLOCK
                    moved = pltpu.roll(piece, turn, 1) if turn else piece
                    block = reg * per_reg + inner
                    if block in done:
                        moved = jnp.where(lane_block == place, moved, done[block])
                    done[block] = moved
        lanes = pl.ds(pl.multiple_of(owner * depth + group * LANES, LANES), LANES)
        for block in range(0, blocks, 2):
            pair = jnp.concatenate([done[block], done[block + 1]], axis=0)
            out_ref[block * rows : (block + 2) * rows, lanes] = pair.astype(jnp.bfloat16)


def arrange_own_kernel(
    chips,
    per_chip,
    capacity,
    slip_hbm,
    slots_hbm,
    green_hbm,
    out_ref,
    send_ref,
    pick_ref,
    green_ref,
    slip_ref,
    slots_ref,
    sems,
):
    width = green_ref.shape[0]
    fetch_slips = pltpu.make_async_copy(slip_hbm, slip_ref, sems.at[0])
    fetch_slots = pltpu.make_async_copy(slots_hbm, slots_ref, sems.at[1])
    fetch_greens = pltpu.make_async_copy(green_hbm, green_ref, sems.at[2])
    fetch_slots.start()
    fetch_slips.start()
    fetch_greens.start()
    fetch_slots.wait()
    mark_tiles(chips, per_chip, capacity, width, slots_ref, send_ref, pick_ref)
    fetch_slips.wait()
    core = lax.rem(lax.axis_index("patch"), 2)
    arrange_half(slip_ref, out_ref, core, core)
    fetch_greens.wait()


def arrange_other_kernel(slip_ref, block_ref, out_ref):
    core = lax.rem(lax.axis_index("patch"), 2)
    arrange_half(slip_ref, out_ref, core, 1 - core)


def in_hbm(*values):
    return [pltpu.with_memory_space_constraint(value, pltpu.HBM) for value in values]


def arrange_own(slips, slots, greens, chips, per_chip, capacity):
    patches, both, samples = slips.shape
    width = greens.shape[0]
    block = jax.ShapeDtypeStruct(
        (samples // BLOCK * both // 2, 2 * patches * BLOCK), jnp.bfloat16
    )
    return pl.pallas_call(
        functools.partial(arrange_own_kernel, chips, per_chip, capacity),
        in_specs=[pl.BlockSpec(memory_space=pltpu.HBM)] * 3,
        out_shape=(
            block,
            jax.ShapeDtypeStruct((chips * capacity, 2 * width), jnp.bfloat16),
            jax.ShapeDtypeStruct((chips * capacity, per_chip), jnp.bfloat16),
            jax.ShapeDtypeStruct(greens.shape, greens.dtype),
        ),
        scratch_shapes=[
            pltpu.VMEM(slips.shape, slips.dtype),
            pltpu.VMEM(slots.shape, slots.dtype),
            pltpu.SemaphoreType.DMA((3,)),
        ],
        compiler_params=params(),
        name="arrange_own",
    )(*in_hbm(slips, slots, greens))


def arrange_other(slips, block):
    return pl.pallas_call(
        arrange_other_kernel,
        out_shape=jax.ShapeDtypeStruct(block.shape, block.dtype),
        input_output_aliases={1: 0},
        compiler_params=params(),
        name="arrange_other",
    )(slips, block)


def earlier_in_chip(count, per_chip):
    q = lax.broadcasted_iota(jnp.int32, (count, count), 0)
    p = lax.broadcasted_iota(jnp.int32, (count, count), 1)
    return ((q < p) & (q // per_chip == p // per_chip)).astype(jnp.float32).astype(jnp.bfloat16)


def one_hot(condition):
    return condition.astype(jnp.float32).astype(jnp.bfloat16)


def mark_tiles(chips, per_chip, capacity, width, slots_ref, send_ref, pick_ref):
    half = capacity // 2
    count = slots_ref.shape[1]
    own = lax.axis_index("patch")
    chip, core = own // 2, lax.rem(own, 2)
    slots = slots_ref[...]
    owner = slots // width
    mine = owner // 2 == chip
    place = slots % width + jnp.where(owner % 2 == core, 0, width)
    marks = jnp.broadcast_to(one_hot(mine), (16, count))
    rank = jnp.dot(marks, earlier_in_chip(count, per_chip), preferred_element_type=jnp.float32)
    rank = rank[:1].astype(jnp.int32)
    target = (lax.broadcasted_iota(jnp.int32, (1, count), 1) // per_chip) ^ chip
    code = jnp.where(mine, target * capacity + rank, -1)
    code_pick = one_hot(lax.broadcasted_iota(jnp.int32, (chips * capacity, count), 0) == code)
    slot_pick = one_hot(lax.broadcasted_iota(jnp.int32, (2 * width, count), 0) == place)
    send_ref[...] = lax.dot_general(
        code_pick, slot_pick, (((1,), (1,)), ((), ())), preferred_element_type=jnp.float32
    ).astype(jnp.bfloat16)
    here = pltpu.roll(slots, lax.rem(count - chip * per_chip, count), 1)[:, :per_chip]
    owner = (here // (2 * width)) ^ chip
    marks = lax.broadcasted_iota(jnp.int32, (round_up(chips, 16), per_chip), 0) == owner
    rank = jnp.dot(
        one_hot(marks), earlier_in_chip(per_chip, per_chip), preferred_element_type=jnp.float32
    )
    rank = jnp.sum(jnp.where(marks, rank, 0.0), axis=0, keepdims=True).astype(jnp.int32)
    from_other = jnp.where(owner == chips - 1, rank // half, 1 - owner % 2) != core
    base = (owner - jnp.where(owner == chips - 1, 0, 1 - owner % 2)) * capacity
    code = base + jnp.where(
        owner == chips - 1,
        jnp.where(from_other, half, 0) + rank % half,
        jnp.where(from_other, capacity, 0) + rank,
    )
    code = jnp.where(owner == 0, rank, code)
    pick_ref[...] = one_hot(lax.broadcasted_iota(jnp.int32, pick_ref.shape, 0) == code)


def route_kernel(chips, send_ref, own_ref, other_ref, after_ref, *out_refs):
    capacity = send_ref.shape[0] // chips
    half = capacity // 2
    core = lax.rem(lax.axis_index("patch"), 2)
    tiles = jnp.concatenate([own_ref[...], other_ref[...]], axis=0).astype(jnp.float32)
    by_comp = []
    for comp in range(own_ref.shape[1]):
        both = tiles[:, comp, :].astype(jnp.bfloat16)
        chosen = jnp.dot(send_ref[...], both, preferred_element_type=jnp.float32)
        chosen = [chosen[step * capacity : (step + 1) * capacity] for step in range(chips)]
        last = chosen[-1]
        sent = [chosen[0]]
        for step in range(1, chips - 1, 2):
            sent.append(jnp.where(core == 0, chosen[step], chosen[step + 1]))
        sent.append(jnp.where(core == 0, last[:half], last[half:]))
        by_comp.append(sent)
    for values, out_ref in zip(zip(*by_comp), out_refs):
        out_ref[...] = jnp.concatenate(values, axis=0).astype(jnp.bfloat16)


def route_tiles(send, own, other, after, chips):
    components, lags = other.shape[1:]
    rows = components * send.shape[0] // chips
    shape = jax.ShapeDtypeStruct((rows, lags), jnp.bfloat16)
    part = jax.ShapeDtypeStruct((rows // 2, lags), jnp.bfloat16)
    return pl.pallas_call(
        functools.partial(route_kernel, chips),
        in_specs=[pl.BlockSpec(memory_space=pltpu.VMEM)] * 3
        + [pl.BlockSpec(memory_space=pl.ANY)],
        out_shape=(shape,) * (chips // 2) + (part,),
        compiler_params=params(),
        name="route_tiles",
    )(send, own, other, after)


def pass_on(value, *others):
    def kernel(*refs):
        pass

    return pl.pallas_call(
        kernel,
        in_specs=[pl.BlockSpec(memory_space=pl.ANY)] * (1 + len(others)),
        out_specs=pl.BlockSpec(memory_space=pl.ANY),
        out_shape=jax.ShapeDtypeStruct(value.shape, value.dtype),
        input_output_aliases={0: 0},
        compiler_params=params(),
        name="pass_on",
    )(value, *others)


def shift_kernel(pick_ref, *refs):
    pieces, out_ref = refs[:-1], refs[-1]
    count = pick_ref.shape[1]
    components = sum(piece.shape[0] for piece in pieces) // pick_ref.shape[0]
    lags = pieces[0].shape[1]
    span = out_ref.shape[1] // components
    tail = jnp.zeros((BLOCK, span - lags), jnp.float32)
    for comp in range(components):
        arrived = []
        for piece in pieces:
            size = piece.shape[0] // components
            arrived.append(piece[...].astype(jnp.float32)[comp * size : (comp + 1) * size])
        arrived = jnp.concatenate(arrived, axis=0).astype(jnp.bfloat16)
        tiles = lax.dot_general(
            pick_ref[...], arrived, (((0,), (0,)), ((), ())), preferred_element_type=jnp.float32
        )
        for patch in range(count):
            row = jnp.broadcast_to(tiles[patch : patch + 1], (BLOCK, lags))
            wide = jnp.concatenate([row, tail], axis=1)
            moved = pltpu.roll(wide, 0, 1, stride=1, stride_axis=0)
            out_ref[
                patch * BLOCK : (patch + 1) * BLOCK, comp * span : (comp + 1) * span
            ] = moved.astype(jnp.bfloat16)


def shift_tiles(pick, pieces, components):
    lags = pieces[0].shape[1]
    span = round_up(lags + BLOCK, LANES)
    shape = jax.ShapeDtypeStruct((pick.shape[1] * BLOCK, components * span), jnp.bfloat16)
    return pl.pallas_call(
        shift_kernel, out_shape=shape, compiler_params=params(), name="shift_tiles"
    )(pick, *pieces)


def convolve_blocks(shifted_ref, slip_refs, stack_ref, product_ref, out_ref, rows):
    length = out_ref.shape[2]
    components = out_ref.shape[1] // rows
    height = slip_refs[0].shape[0]
    width = shifted_ref.shape[1] // components
    per_reg = LANES // BLOCK
    blocks = height // rows
    for step, ref in enumerate(slip_refs):
        stack_ref[step * height : (step + 1) * height] = ref[...]
    for comp in range(components):
        product_ref[comp] = jnp.dot(
            stack_ref[...],
            shifted_ref[:, comp * width : (comp + 1) * width],
            preferred_element_type=jnp.float32,
        )
    for comp in range(components):
        for step in range(len(slip_refs)):
            total = None
            for inner in range(per_reg):
                part = None
                for outer in range(inner, blocks, per_reg):
                    lead = outer // per_reg * LANES
                    start = step * height + outer * rows
                    block = product_ref[comp, start : start + rows, :]
                    pieces = [jnp.zeros((rows, lead), jnp.float32)] if lead else []
                    pieces.append(block[:, : min(width, length - lead)])
                    if length > lead + width:
                        pieces.append(jnp.zeros((rows, length - lead - width), jnp.float32))
                    block = jnp.concatenate(pieces, axis=1) if len(pieces) > 1 else pieces[0]
                    part = block if part is None else part + block
                if inner:
                    part = pltpu.roll(part, inner * BLOCK, 1)
                total = part if total is None else total + part
            out_ref[step, comp * rows : (comp + 1) * rows, :] = total


def unit_of(exponent):
    return jnp.exp2(exponent.astype(jnp.float32) * (1.0 / STEPS)) * (1.0 / LARGEST)


def as_sent(total, lanes):
    peak = jnp.maximum(jnp.max(jnp.abs(total), axis=1, keepdims=True), SMALLEST)
    exponent = jnp.ceil(jnp.log2(peak) * STEPS).astype(jnp.int32)
    whole = jnp.clip(jnp.round(total * (1.0 / unit_of(exponent))), -LARGEST, LARGEST)
    rest = jnp.broadcast_to(exponent, (total.shape[0], lanes - total.shape[1]))
    return jnp.concatenate([whole.astype(jnp.int32), rest], axis=1).astype(jnp.int16)


def convolve_first_kernel(rows, shifted_ref, *refs):
    slip_refs, (out_ref, stack_ref, product_ref) = refs[:-3], refs[-3:]
    convolve_blocks(shifted_ref, slip_refs, stack_ref, product_ref, out_ref, rows)


def convolve_scratch(shifted, count, height, depth, components):
    return [
        pltpu.VMEM((count * height, depth), jnp.bfloat16),
        pltpu.VMEM((components, count * height, shifted.shape[1] // components), jnp.float32),
    ]


def convolve_first(shifted, slips, rows, components, length):
    shape = jax.ShapeDtypeStruct((len(slips), components * rows, length), jnp.float32)
    return pl.pallas_call(
        functools.partial(convolve_first_kernel, rows),
        out_shape=shape,
        scratch_shapes=convolve_scratch(shifted, len(slips), *slips[0].shape, components),
        compiler_params=params(),
        name="convolve_first",
    )(shifted, *slips)


def convolve_last_kernel(rows, shifted_ref, slip_ref, first_ref, *refs):
    out_refs, (stack_ref, product_ref, last_ref) = refs[:-3], refs[-3:]
    convolve_blocks(shifted_ref, [slip_ref], stack_ref, product_ref, last_ref, rows)
    count = first_ref.shape[0]
    turn = lax.axis_index("site") ^ (lax.axis_index("patch") // 2)
    last = last_ref[0]
    for step, ref in enumerate(out_refs):
        source = step ^ turn
        total = jnp.where(source == count, last, first_ref[jnp.minimum(source, count - 1)])
        ref[...] = as_sent(total, ref.shape[1]) if step else total


def convolve_last(shifted, slip, first, rows, components):
    count, height, length = first.shape
    own = jax.ShapeDtypeStruct((height, length), jnp.float32)
    sent = jax.ShapeDtypeStruct((height, round_up(length, LANES) + LANES), jnp.int16)
    return pl.pallas_call(
        functools.partial(convolve_last_kernel, rows),
        out_shape=(own,) + (sent,) * count,
        scratch_shapes=convolve_scratch(shifted, 1, *slip.shape, components)
        + [pltpu.VMEM((1, height, length), jnp.float32)],
        compiler_params=params(),
        name="convolve_last",
    )(shifted, slip, first)


def add_kernel(own_ref, *refs):
    sent_refs, out_ref = refs[:-1], refs[-1]
    part, components, length = out_ref.shape
    rows = own_ref.shape[0] // components
    total = own_ref[...]
    for ref in sent_refs:
        unit = unit_of(ref[:, length:].astype(jnp.int32)[:, :1])
        total = total + ref[:, :length].astype(jnp.int32).astype(jnp.float32) * unit
    for comp in range(components):
        out_ref[:, comp, :] = total[comp * rows : comp * rows + part]


def add_up(own, sent, part, components):
    return pl.pallas_call(
        add_kernel,
        out_shape=jax.ShapeDtypeStruct((part, components, own.shape[1]), jnp.float32),
        compiler_params=params(),
        name="add_up",
    )(own, *sent)


def local(slip_rates, green_tiles, patch_slot):
    devices = lax.axis_size("patch")
    sites = lax.axis_size("site")
    chips = devices // 2
    patches, held, samples = slip_rates.shape
    components, lags = green_tiles.shape[2:]
    length = samples + lags
    part = held // 2
    rows = round_up(part, ROWS)
    assert chips == sites and sites & (sites - 1) == 0

    def over_patch(value, offset):
        return lax.ppermute(value, "patch", [(i, i ^ offset) for i in range(devices)])

    slips = slip_rates
    if rows > part:
        slips = slips.reshape(patches, 2, part, samples)
        slips = jnp.pad(slips, ((0, 0), (0, 0), (0, rows - part), (0, 0)))
        slips = slips.reshape(patches, 2 * rows, samples)
    greens = green_tiles[0]
    other_tiles, other = over_patch(greens, 1), over_patch(slips, 1)
    share = 2 * max(1, patches // devices)
    capacity = round_up(4 * share, 16)
    block, send, pick, own_tiles = arrange_own(
        slips, patch_slot.reshape(1, -1), greens, chips, 2 * patches, capacity
    )
    block = arrange_other(other, block)

    pieces = list(route_tiles(send, own_tiles, other_tiles, block, chips))
    arrived = [None] * (len(pieces) - 1)
    for index in reversed(range(len(arrived))):
        hops = [(2 * index + 1, 2 * index + 2), (chips - 1, chips - 1)][index == len(arrived) - 1]
        arrived[index] = lax.ppermute(
            pieces[1 + index], "patch", [(i, i ^ (2 * hops[i % 2])) for i in range(devices)]
        )
    pieces = pieces[:1]
    for piece in arrived:
        pieces += [piece, over_patch(piece, 1)]

    blocks = {0: block}
    for step in [2**i for i in range(sites.bit_length())] + list(range(sites)):
        if 0 < step < sites and step not in blocks:
            low = step & -step
            blocks[step] = lax.ppermute(
                blocks[step - low], "site", [(i, i ^ low) for i in range(sites)]
            )
            if step == sites // 2:
                blocks[step] = pass_on(blocks[step], *arrived)
    shifted = shift_tiles(pick, pieces, components)

    slips = [blocks[step] for step in range(sites)]
    first = convolve_first(shifted, slips[:-1], rows, components, length)
    sums = convolve_last(shifted, slips[-1], first, rows, components)
    order = [chips - 1] + list(range(1, chips - 1))
    sent = [over_patch(sums[step], 2 * step) for step in order]
    return add_up(sums[0], sent, part, components)[None]


def solution(mesh):
    in_specs = (P("patch", "site", None), P("site", "patch", None, None), P())
    out_specs = P("site", "patch", None, None)
    return jax.shard_map(local, mesh=mesh, in_specs=in_specs, out_specs=out_specs, check_vma=False)
```
